32 devices in a mesh: tile: 8 (over y, x, core), rep: 4 (over z).
Axes of the slice: x: 2, y: 2, z: 4, core: 2. Of those that a mesh axis runs over, the one named last changes fastest.
Arguments:
- inputs: bfloat16 [8192, 1024], P(('rep', 'tile')), parts along dimension 0, may hold values from -6 to 6
- queries: bfloat16 [8192, 1024], P(('rep', 'tile')), parts along dimension 0, may hold values from -180 to 180
- key_vectors: bfloat16 [8192, 1024], P(('rep', 'tile')), parts along dimension 0, may hold values from -6 to 6
- values: bfloat16 [8192, 1024], P(('rep', 'tile')), parts along dimension 0, may hold values from -16 to 16
- out_weight: bfloat16 [1024, 1024], replicated, may hold values from -0.1875 to 0.1875
- norm_gain: float32 [1024], replicated, may hold values from 0.5 to 1.5
- routes: int32 [8192, 2], P(('rep', 'tile')), parts along dimension 0, may hold values from 0 to 7, all different within a row; in each aligned block of 128 rows (0 to 127, 128 to 255, ...) at most 64 rows name the same one
- route_gates: float32 [8192, 2], P(('rep', 'tile')), parts along dimension 0, may hold values from 0.2 to 1
- w_gate: bfloat16 [8, 1024, 1408], P('tile'), may hold values from -0.1875 to 0.1875
- w_up: bfloat16 [8, 1024, 1408], P('tile'), may hold values from -0.1875 to 0.1875
- w_down: bfloat16 [8, 1408, 1024], P('tile'), may hold values from -0.15625 to 0.15625
Outputs:
- layer_out: bfloat16 [8192, 1024], P(('rep', 'tile')), parts along dimension 0
The draws below stay inside these ranges and needn't reach their ends.
There are 4 independent parts, one for each index of `rep`. The reference program is written for one: setup_inputs(seed, part) draws one part's arguments, and reference() takes and returns one part's arrays. A program takes and returns all parts, laid end to end along the dimension named above; an argument that names none is the same for every part. Nothing has to cross between parts.
Inputs may be any that keep to these rules, and one draw needn't show every extreme that they name: `routes`: in each aligned block of 128 tokens no expert is named by more than 64 tokens, and some expert is named by exactly that many; each token names 2 different experts.
All inputs are finite; a program needn't handle non-finite values.
Results may differ from the reference program's by a relative error of at most 0.0061.
Values may be sent and summed in bfloat16 or wider, within the bound.
No kernel may reach another device: no remote copies, remote signals or barrier semaphores. Data moves between devices by JAX's collectives and lax.ppermute only.
A program may use at most 64 MiB of HBM per device.

```python
import math
import jax
import jax.numpy as jnp
import numpy as np
from jax import lax

D = 1024
HEADS = 16
HD = 64
H = 1408
TOPK = 2
IL_DEV = 4
XL = 8
DP = 8
R_IL = 2
R_XL = 2
R_DP = 2
TOK_DEV = 256
TOKENS = 2048
NIL = 32
EXPERTS = 8
CAP_HALF = 64
N_TILE = 8


def key_table(key):
    raw = jax.random.normal(jax.random.fold_in(key, 11), (TOKENS, D), jnp.float32)
    return jnp.clip(raw, -6.0, 6.0)


def draw_key_vectors(key, part):
    base_keys = key_table(key)
    return base_keys.astype(jnp.bfloat16)


def draw_queries(key, part):
    raw = jax.random.normal(jax.random.fold_in(key, 12), (TOKENS, D), jnp.float32)
    raw = jnp.clip(raw, -6.0, 6.0)
    return raw.astype(jnp.bfloat16)


def shard_levels(own_key, dims, shards, low, largest):
    level = 1.0
    for axis_at, blocks in shards:
        steps = jax.random.uniform(jax.random.fold_in(jax.random.fold_in(own_key, 6), axis_at), (blocks,), jnp.float32, low / len(shards), largest / len(shards))
        level = level * jnp.repeat(jnp.exp(steps), dims[axis_at] // blocks).reshape((-1,) + (1,) * (len(dims) - 1 - axis_at))
    return level


def assign_block(rng, own, number, rows, count, top, reach, lean):
    sequence = jax.random.permutation(rng, count)
    crowded, common = shares(count, rows * top, reach, lean, True), shares(count, rows * top, reach, lean, False)
    places = jnp.arange(count)

    def named(tallies, turn):
        used = int((tallies > 0).sum())
        fixed = max(1, used // 4)
        moved = fixed + (places - fixed + turn * (used - fixed)) % max(1, count - fixed)
        return jnp.zeros((count,), jnp.int32).at[sequence[jnp.where(places < fixed, places, moved)]].set(jnp.asarray(tallies, jnp.int32))

    tallies = jnp.where(number % 4 == 0, named(crowded, number // 4), named(common, number - number // 4 - 1))
    mixed = jax.random.permutation(jax.random.fold_in(own, 3), count)
    source_of, sink = mixed[0:count // 2 * 2:2], mixed[1:count // 2 * 2:2]
    slack = jnp.minimum(tallies[source_of] - 1, reach - tallies[sink]) // 2
    slack = jnp.where((source_of == sequence[0]) | (sink == sequence[0]) | (tallies[sink] == 0), 0, jnp.maximum(slack, 0))
    moved = jax.random.randint(jax.random.fold_in(own, 4), (count // 2,), 0, 1 << 20) % (slack + 1)
    tallies = tallies.at[source_of].add(-moved).at[sink].add(moved)
    members = jnp.searchsorted(jnp.cumsum(tallies), jnp.arange(rows * top), side="right").astype(jnp.int32)
    grid = members.reshape(top, rows).T
    grid = grid[jax.random.permutation(jax.random.fold_in(own, 1), rows)]
    turn = jax.random.randint(jax.random.fold_in(own, 2), (rows, 1), 0, top)
    return jnp.take_along_axis(grid, (jnp.arange(top)[None, :] + turn) % top, axis=1)


def shares(amount, total, bound, slope, full):
    weights = [(1 << 20) // math.isqrt(rank ** slope) + 1 for rank in range(1, amount + 1)]
    largest = bound if full else min(bound, max(-(-total // amount), total * weights[0] // sum(weights)))
    least = 1 if total - largest >= amount - 1 else 0
    holding, rest = [largest] + [least] * (amount - 1), total - largest - least * (amount - 1)
    while rest > 0:
        movable = [i for i in range(1, amount) if holding[i] < largest] or [i for i in range(1, amount) if holding[i] < bound]
        mass, left = sum([weights[i] for i in movable]), rest
        for i in movable:
            more = min(bound - holding[i], max(1, left * weights[i] // mass), rest)
            holding[i] = holding[i] + more
            rest = rest - more
    return np.array(holding)


def normal_values(stream_key, shape, scale, bound, shards=(), held_as=jnp.bfloat16):
    factor_of = shard_levels(stream_key, shape, shards, -0.22, 0.18) if shards else 1.0
    values = jax.random.normal(stream_key, shape, jnp.float32) * scale * factor_of
    return jnp.minimum(jnp.maximum(values, -bound), bound).astype(held_as)


def setup_inputs(seed: int = 0, part: int = 0) -> dict:
    seeds = jax.random.split(jax.random.key(seed), 12)
    own_keys = jax.random.split(jax.random.fold_in(seeds[11], part), 12)
    inputs = normal_values(own_keys[0], (TOKENS, D), 1.0, 6.0, ((0, 8),))
    queries = draw_queries(jax.random.fold_in(jax.random.fold_in(seeds[11], part), 71), part)
    key_vectors = draw_key_vectors(jax.random.fold_in(jax.random.fold_in(seeds[11], part), 71), part)
    values = normal_values(own_keys[3], (TOKENS, D), 3.0, 16.0, ((0, 8),))
    out_weight = normal_values(seeds[4], (D, D), D ** -0.5, 0.1875)
    norm_gain = jnp.clip(1.0 + 0.1 * jax.random.normal(seeds[5], (D,), jnp.float32), 0.5, 1.5)
    routes_keys = jax.random.split(jax.random.fold_in(own_keys[6], 1), TOKENS // (TOK_DEV // 2))
    routes_turns = jax.random.permutation(jax.random.fold_in(own_keys[6], 3), TOKENS // (TOK_DEV // 2))
    routes = jax.vmap(lambda own, number: assign_block(jax.random.fold_in(own_keys[6], 2), own, number, TOK_DEV // 2, EXPERTS, TOPK, CAP_HALF, 2))(routes_keys, routes_turns).reshape((TOKENS, TOPK))
    route_gates = jnp.clip(0.2 + 0.8 * jax.random.uniform(own_keys[7], (TOKENS, TOPK), jnp.float32) ** shard_levels(own_keys[7], (TOKENS, TOPK), ((0, 8),), -0.2, 0.2), 0.2, 1.0)
    w_gate = normal_values(seeds[8], (EXPERTS, D, H), D ** -0.5, 0.1875, ((0, 8),))
    w_up = normal_values(seeds[9], (EXPERTS, D, H), D ** -0.5, 0.1875, ((0, 8),))
    w_down = normal_values(seeds[10], (EXPERTS, H, D), H ** -0.5, 0.15625, ((0, 8),))
    return {"inputs": inputs, "queries": queries, "key_vectors": key_vectors, "values": values, "out_weight": out_weight, "norm_gain": norm_gain, "routes": routes, "route_gates": route_gates, "w_gate": w_gate, "w_up": w_up, "w_down": w_down}


def local_attention(query_block, key_block, value_block, first_inline, total_inlines):
    query_count = query_block.shape[0]
    key_count = key_block.shape[0]
    plane = XL * DP
    query_pos = jnp.arange(query_count, dtype=jnp.int32)
    key_pos = jnp.arange(key_count, dtype=jnp.int32)
    query_il = query_pos // plane
    query_xl = query_pos // DP % XL
    query_dp = query_pos % DP
    key_il = key_pos // plane - R_IL
    key_xl = key_pos // DP % XL
    key_dp = key_pos % DP
    near = jnp.abs(query_il[:, None] - key_il[None, :]) <= R_IL
    near = near & (jnp.abs(query_xl[:, None] - key_xl[None, :]) <= R_XL)
    near = near & (jnp.abs(query_dp[:, None] - key_dp[None, :]) <= R_DP)
    inside = (first_inline + key_il >= 0) & (first_inline + key_il < total_inlines)
    near = near & inside[None, :]
    query_heads = query_block.reshape(query_count, HEADS, HD).astype(jnp.float32)
    key_heads = key_block.reshape(key_count, HEADS, HD).astype(jnp.float32)
    value_heads = value_block.reshape(key_count, HEADS, HD).astype(jnp.float32)
    scores = jnp.einsum('qhd,khd->hqk', query_heads, key_heads) * (1.0 / HD ** 0.5)
    scores = jnp.where(near[None], scores, jnp.float32(-1e+30))
    highest = lax.optimization_barrier(jnp.max(scores, axis=-1, keepdims=True))
    weights = jnp.exp(scores - highest)
    weights = jnp.where(near[None], weights, jnp.float32(0.0))
    totals = lax.optimization_barrier(jnp.sum(weights, axis=-1, keepdims=True))
    probs = (weights / totals).astype(jnp.bfloat16)
    attended = jnp.einsum('hqk,khd->qhd', probs.astype(jnp.float32), value_heads)
    return attended.astype(jnp.bfloat16).reshape(query_count, HEADS * HD)

def expert_rows(token_rows, gate_mat, up_mat, down_mat):
    gate_part = jnp.dot(token_rows, gate_mat, preferred_element_type=jnp.float32)
    up_part = jnp.dot(token_rows, up_mat, preferred_element_type=jnp.float32)
    hidden = (jax.nn.silu(gate_part) * up_part).astype(jnp.bfloat16)
    return jnp.dot(hidden, down_mat, preferred_element_type=jnp.float32).astype(jnp.bfloat16)

def slot_ranks(routes, experts, block_rows):
    row_count = routes.shape[0]
    expert_ids = jnp.arange(experts, dtype=jnp.int32)
    matches = routes[:, :, None] == expert_ids[None, None, :]
    hits = lax.optimization_barrier(jnp.sum(matches.astype(jnp.int32), axis=1))
    hits = hits.reshape(row_count // block_rows, block_rows, experts)
    earlier = (jnp.cumsum(hits, axis=1) - hits).reshape(row_count, experts)
    return lax.optimization_barrier(jnp.sum(jnp.where(matches, earlier[:, None, :], 0), axis=-1)).astype(jnp.int32)

def reference(inputs, queries, key_vectors, values, out_weight, norm_gain, routes, route_gates, w_gate, w_up, w_down):
    width = R_IL * XL * DP
    zero_rows = jnp.zeros((width, D), jnp.bfloat16)
    padded_keys = jnp.concatenate([zero_rows, key_vectors, zero_rows], axis=0)
    padded_values = jnp.concatenate([zero_rows, values, zero_rows], axis=0)

    def one_tile(tile_id):
        start = (tile_id * TOK_DEV).astype(jnp.int32)
        query_block = lax.dynamic_slice_in_dim(queries, start, TOK_DEV, 0)
        key_block = lax.dynamic_slice_in_dim(padded_keys, start, TOK_DEV + 2 * width, 0)
        value_block = lax.dynamic_slice_in_dim(padded_values, start, TOK_DEV + 2 * width, 0)
        return local_attention(query_block, key_block, value_block, (tile_id * IL_DEV).astype(jnp.int32), NIL)
    attended = lax.map(one_tile, jnp.arange(N_TILE, dtype=jnp.int32)).reshape(TOKENS, D)
    residual = (inputs.astype(jnp.float32) + jnp.dot(attended, out_weight, preferred_element_type=jnp.float32)).astype(jnp.bfloat16)
    resid_float = residual.astype(jnp.float32)
    mean_square = lax.optimization_barrier(jnp.mean(resid_float * resid_float, axis=-1, keepdims=True))
    normed = (resid_float * lax.rsqrt(mean_square + 1e-06) * norm_gain[None, :]).astype(jnp.bfloat16)
    block_rows = TOK_DEV // 2
    slot_rank = slot_ranks(routes, EXPERTS, block_rows)
    token_ids = jnp.arange(TOKENS, dtype=jnp.int32)
    source = (token_ids // TOK_DEV)[:, None]
    half_index = (token_ids // block_rows % 2)[:, None]
    positions = (source * (2 * CAP_HALF) + half_index * CAP_HALF + slot_rank).astype(jnp.int32)
    buffer_rows = N_TILE * 2 * CAP_HALF
    owners = jnp.full((EXPERTS, buffer_rows), TOKENS, jnp.int32)
    owners = owners.at[routes, positions].set(jnp.broadcast_to(token_ids[:, None], routes.shape))
    normed_padded = jnp.concatenate([normed, jnp.zeros((1, D), jnp.bfloat16)], axis=0)

    def one_expert(expert_id):
        picked_rows = normed_padded[owners[expert_id]]
        return expert_rows(picked_rows, w_gate[expert_id], w_up[expert_id], w_down[expert_id])
    outputs = lax.map(one_expert, jnp.arange(EXPERTS, dtype=jnp.int32))
    picked = outputs[routes, positions].astype(jnp.float32)
    combined = lax.optimization_barrier(jnp.sum(route_gates[:, :, None] * picked, axis=1))
    return (resid_float + combined).astype(jnp.bfloat16)
```

```python
import functools

import jax
import jax.numpy as jnp
from jax import lax
from jax.experimental import pallas as pl
from jax.experimental.pallas import tpu as pltpu
from jax.sharding import PartitionSpec as P

HEADS = 16
HD = 64
IL_DEV = 4
XL = 8
DP = 8
R_IL = 2
R_XL = 2
R_DP = 2
PLANE = XL * DP
META = 16
MIB = 1024 * 1024
F32 = jnp.float32
BF16 = jnp.bfloat16
VMEM = pl.BlockSpec(memory_space=pltpu.VMEM)
SMEM = pl.BlockSpec(memory_space=pltpu.SMEM)


def cost(flops, transcendentals, args, outs):
    moved = sum(a.size * a.dtype.itemsize for a in args)
    moved += sum(o.size * o.dtype.itemsize for o in outs)
    return pl.CostEstimate(flops=flops, transcendentals=transcendentals, bytes_accessed=moved)


def window_bias(queries, first_query, keys, first_key, live):
    q = lax.broadcasted_iota(jnp.int32, (queries, keys), 0) + first_query
    k = lax.broadcasted_iota(jnp.int32, (queries, keys), 1) + (first_key + PLANE * R_IL)
    near = jnp.abs(q // PLANE + R_IL - k // PLANE) <= R_IL
    near = near & (jnp.abs(q // DP % XL - k // DP % XL) <= R_XL)
    near = near & (jnp.abs(q % DP - k % DP) <= R_DP)
    if live is not None:
        near = near & (live > 0)
    return jnp.where(near, F32(0.0), F32(-1e30))


def attention_kernel(half, live, q, k, v, halo, x, w, gain, meta, resid, payload, att):
    rows = q.shape[0]
    own = k.shape[0]
    wide = halo.shape[0] // 2
    start = half * rows
    bias_own = window_bias(rows, start, own, 0, None)
    first = -wide if half == 0 else own
    bias_halo = window_bias(rows, start, wide, first, live[half])
    lane = lax.broadcasted_iota(jnp.int32, (rows, 2 * HD), 1)
    nt = (((1,), (1,)), ((), ()))
    for pair in range(HEADS // 2):
        cols = slice(pair * 2 * HD, (pair + 1) * 2 * HD)
        query = q[:, cols] * BF16(1.0 / HD**0.5)
        key_own, key_halo = k[:, cols], halo[:wide, cols]
        val_own, val_halo = v[:, cols], halo[wide:, cols]
        outs = []
        for side in range(2):
            mine = (lane < HD) if side == 0 else (lane >= HD)
            qh = jnp.where(mine, query, BF16(0.0))
            s_own = lax.dot_general(qh, key_own, nt, preferred_element_type=F32) + bias_own
            s_halo = lax.dot_general(qh, key_halo, nt, preferred_element_type=F32) + bias_halo
            top = jnp.maximum(
                jnp.max(s_own, axis=1, keepdims=True), jnp.max(s_halo, axis=1, keepdims=True)
            )
            p_own = jnp.exp(s_own - top)
            p_halo = jnp.exp(s_halo - top)
            total = jnp.sum(p_own, axis=1, keepdims=True) + jnp.sum(p_halo, axis=1, keepdims=True)
            o = jnp.dot(p_own.astype(BF16), val_own, preferred_element_type=F32)
            o = o + jnp.dot(p_halo.astype(BF16), val_halo, preferred_element_type=F32)
            outs.append(o / total)
        att[:, cols] = jnp.where(lane < HD, outs[0], outs[1]).astype(BF16)
    res = x[...].astype(F32) + jnp.dot(att[...], w[...], preferred_element_type=F32)
    res = res.astype(BF16)
    resid[...] = res
    res = res.astype(F32)
    square = jnp.mean(res * res, axis=1, keepdims=True)
    normed = (res * lax.rsqrt(square + 1e-06) * gain[...]).astype(BF16)
    payload[:rows, :] = normed
    if meta is not None:
        payload[rows:, :] = jnp.broadcast_to(meta[...], (META, meta.shape[1]))


def attend(half, live, q, k, v, halo, x, w, gain, meta):
    rows, model = q.shape[0] // 2, q.shape[1]
    whole = lambda a: pl.BlockSpec(a.shape, lambda i: (0,) * a.ndim)
    part = pl.BlockSpec((rows, model), lambda i: (half, 0))
    args = [live, q, k, v, halo, x, w, gain]
    specs = [SMEM, part, whole(k), whole(v), whole(halo), part, whole(w), whole(gain)]
    extra = 0
    if meta is not None:
        args.append(meta)
        specs.append(whole(meta))
        extra = META
        body = functools.partial(attention_kernel, half)
    else:

        def body(live, q, k, v, halo, x, w, gain, resid, payload, att):
            attention_kernel(half, live, q, k, v, halo, x, w, gain, None, resid, payload, att)

    outs = [
        jax.ShapeDtypeStruct((rows, model), BF16),
        jax.ShapeDtypeStruct((rows + extra, model), BF16),
    ]
    keys = k.shape[0] + halo.shape[0] // 2
    return pl.pallas_call(
        body,
        grid=(1,),
        in_specs=specs,
        out_specs=[pl.BlockSpec(o.shape, lambda i: (0, 0)) for o in outs],
        out_shape=outs,
        scratch_shapes=[pltpu.VMEM((rows, model), BF16)],
        compiler_params=pltpu.CompilerParams(vmem_limit_bytes=24 * MIB),
        cost_estimate=cost(
            4 * rows * keys * model + 2 * rows * model * model, HEADS * rows * keys, args, outs
        ),
        name=f"attention_half{half}",
    )(*args)


def pick_matrices(payload, block, rows, capacity, expert):
    base = block * (rows + META) + rows
    meta = payload[base : base + META, :].astype(F32)
    item = [meta[:, i * rows : (i + 1) * rows] for i in range(8)]
    hit0, hit1 = item[0] == expert, item[1] == expert
    hits = jnp.where(hit0 | hit1, F32(1.0), F32(0.0))
    upper = lax.broadcasted_iota(jnp.int32, (rows, rows), 0) < lax.broadcasted_iota(
        jnp.int32, (rows, rows), 1
    )
    upper = jnp.where(upper, F32(1.0), F32(0.0)).astype(BF16)
    rank = jnp.dot(hits.astype(BF16), upper, preferred_element_type=F32)
    rank = jnp.where(hits > 0, rank, F32(-1.0))
    gate = jnp.where(hit0, item[2] + item[3] + item[4], F32(0.0))
    gate = gate + jnp.where(hit1, item[5] + item[6] + item[7], F32(0.0))
    slot = lax.broadcasted_iota(jnp.int32, (capacity, rows), 0).astype(F32)
    return slot == rank[:1, :], gate[:1, :]


def experts_kernel(blocks, rows, capacity, me, *refs):
    count = len(refs) - 7
    payloads, (w_gate, w_up, w_down, out_mine, out_sib, x, hidden) = refs[:count], refs[count:]
    expert = me[0].astype(F32)
    place = 0
    for payload in payloads:
        for block in range(blocks):
            hot, _ = pick_matrices(payload, block, rows, capacity, expert)
            hot = jnp.where(hot, F32(1.0), F32(0.0)).astype(BF16)
            base = block * (rows + META)
            picked = jnp.dot(hot, payload[base : base + rows, :], preferred_element_type=F32)
            x[place : place + capacity, :] = picked.astype(BF16)
            place += capacity
    width = w_gate.shape[1]
    for at in range(0, width, 256):
        cols = slice(at, min(at + 256, width))
        g = jnp.dot(x[...], w_gate[:, cols], preferred_element_type=F32)
        u = jnp.dot(x[...], w_up[:, cols], preferred_element_type=F32)
        hidden[:, cols] = (g / (1.0 + jnp.exp(-g)) * u).astype(BF16)
    half = place // 2
    for at in range(0, w_down.shape[1], 256):
        cols = slice(at, at + 256)
        o = jnp.dot(hidden[...], w_down[:, cols], preferred_element_type=F32).astype(BF16)
        out_mine[:, cols] = o[:half]
        out_sib[:, cols] = o[half:]


def experts(me, mine, sib, w_gate, w_up, w_down, blocks, rows, capacity):
    model, width = w_gate.shape
    slots = (len(mine) + len(sib)) * blocks * capacity
    outs = [jax.ShapeDtypeStruct((slots // 2, model), BF16)] * 2
    args = [me, *mine, *sib, w_gate, w_up, w_down]
    return pl.pallas_call(
        functools.partial(experts_kernel, blocks, rows, capacity),
        in_specs=[SMEM] + [VMEM] * (len(args) - 1),
        out_specs=[VMEM] * 2,
        out_shape=outs,
        scratch_shapes=[pltpu.VMEM((slots, model), BF16), pltpu.VMEM((slots, width), BF16)],
        compiler_params=pltpu.CompilerParams(vmem_limit_bytes=32 * MIB),
        cost_estimate=cost(6 * slots * model * width, slots * width, args, outs),
        name=f"experts_{slots}",
    )(*args)


def spread(payload, block, rows, capacity, experts_two, outs_two):
    weights, values = [], []
    for expert, out in zip(experts_two, outs_two):
        hot, gate = pick_matrices(payload, block, rows, capacity, expert)
        full = jnp.where(hot, gate, F32(0.0))
        high = full.astype(BF16)
        weights += [high, (full - high.astype(F32)).astype(BF16)]
        values += [out, out]
    return lax.dot_general(
        jnp.concatenate(weights, axis=0),
        jnp.concatenate(values, axis=0),
        (((0,), (0,)), ((), ())),
        preferred_element_type=F32,
    )


def combine_kernel(blocks, rows, capacity, groups, added, me, *refs):
    payloads = refs[:groups]
    outs_me, outs_sib = refs[groups], refs[groups + 1]
    carry = refs[groups + 2] if added else None
    results = refs[groups + 2 + (1 if added else 0) :]
    both = (me[0].astype(F32), me[1].astype(F32))
    core = me[2]
    for group in range(groups):
        for block in range(blocks):
            slot = (group * blocks + block) * capacity
            span = slice(slot, slot + capacity)
            total = spread(
                payloads[group], block, rows, capacity, both, (outs_me[span, :], outs_sib[span, :])
            )
            at = slice(block * rows, (block + 1) * rows)
            if added:
                extra = carry[at, :].astype(F32)
                total = total + jnp.where(core == group, extra, F32(0.0))
            results[group][at, :] = total.astype(BF16)


def combine(me, payloads, outs_me, outs_sib, carry, blocks, rows, capacity):
    model = payloads[0].shape[1]
    groups = len(payloads)
    args = [me, *payloads, outs_me, outs_sib] + ([] if carry is None else [carry])
    outs = [jax.ShapeDtypeStruct((blocks * rows, model), BF16)] * groups
    return pl.pallas_call(
        functools.partial(combine_kernel, blocks, rows, capacity, groups, carry is not None),
        in_specs=[SMEM] + [VMEM] * (len(args) - 1),
        out_specs=[VMEM] * groups,
        out_shape=outs,
        compiler_params=pltpu.CompilerParams(vmem_limit_bytes=24 * MIB),
        cost_estimate=cost(8 * groups * blocks * rows * capacity * model, 0, args, outs),
        name=f"combine_{groups}",
    )(*args)


def finish_kernel(blocks, rows, capacity, me, *refs):
    out = refs[-1]
    both = (me[0].astype(F32), me[1].astype(F32))
    for block in range(blocks):
        payload, resid, mine, sib, from_x, from_y = refs[block * 6 : block * 6 + 6]
        total = spread(payload, 0, rows, capacity, both, (mine[:capacity, :], sib[:capacity, :]))
        total = total + from_x[...].astype(F32) + from_y[...].astype(F32)
        total = total + resid[...].astype(F32)
        out[block * rows : (block + 1) * rows, :] = total.astype(BF16)


def finish(me, parts, rows, capacity):
    model = parts[0][0].shape[1]
    args = [me] + [a for part in parts for a in part]
    outs = [jax.ShapeDtypeStruct((len(parts) * rows, model), BF16)]
    return pl.pallas_call(
        functools.partial(finish_kernel, len(parts), rows, capacity),
        in_specs=[SMEM] + [VMEM] * (len(args) - 1),
        out_specs=VMEM,
        out_shape=outs[0],
        compiler_params=pltpu.CompilerParams(vmem_limit_bytes=24 * MIB),
        cost_estimate=cost(8 * len(parts) * rows * capacity * model, 0, args, outs),
        name="finish",
    )(*args)


def expert_rows(token_rows, gate_mat, up_mat, down_mat):
    gate_part = jnp.dot(token_rows, gate_mat, preferred_element_type=F32)
    up_part = jnp.dot(token_rows, up_mat, preferred_element_type=F32)
    hidden = (jax.nn.silu(gate_part) * up_part).astype(BF16)
    return jnp.dot(hidden, down_mat, preferred_element_type=F32).astype(BF16)


def slot_ranks(routes, experts_count, block_rows):
    row_count = routes.shape[0]
    expert_ids = jnp.arange(experts_count, dtype=jnp.int32)
    matches = routes[:, :, None] == expert_ids[None, None, :]
    hits = jnp.sum(matches.astype(jnp.int32), axis=1)
    hits = hits.reshape(row_count // block_rows, block_rows, experts_count)
    earlier = (jnp.cumsum(hits, axis=1) - hits).reshape(row_count, experts_count)
    return jnp.sum(jnp.where(matches, earlier[:, None, :], 0), axis=-1)


def routed_all_to_all(normed_parts, resid_parts, routes, route_gates, w_gate, w_up, w_down):
    tiles = lax.axis_size("tile")
    row_count, route_width = routes.shape
    block_rows, model = normed_parts[0].shape
    capacity = row_count * route_width // tiles
    slot_rank = slot_ranks(routes, tiles, block_rows)
    pieces = []
    for index, part_normed in enumerate(normed_parts):
        rows = slice(index * block_rows, (index + 1) * block_rows)
        positions = routes[rows] * capacity + slot_rank[rows]
        copies = jnp.broadcast_to(
            part_normed[:, None, :], (block_rows, route_width, model)
        ).reshape(-1, model)
        outgoing = jnp.zeros((tiles * capacity, model), BF16).at[positions.reshape(-1)].set(copies)
        outgoing = outgoing.reshape(tiles, capacity, model)
        received = lax.all_to_all(outgoing, "tile", split_axis=0, concat_axis=0, tiled=True)
        produced = expert_rows(received.reshape(-1, model), w_gate, w_up, w_down)
        produced = produced.reshape(received.shape)
        returned = lax.all_to_all(produced, "tile", split_axis=0, concat_axis=0, tiled=True)
        picked = returned.reshape(-1, model)[positions].astype(F32)
        combined = jnp.sum(route_gates[rows][:, :, None] * picked, axis=1)
        pieces.append((resid_parts[index].astype(F32) + combined).astype(BF16))
    return jnp.concatenate(pieces, axis=0)


def swap(array, bit):
    return lax.ppermute(array, "tile", [(i, i ^ bit) for i in range(8)])


def swap_turned(array):
    return lax.ppermute(array, "tile", [(i, i ^ (2 if i % 2 else 4)) for i in range(8)])


def routed_gather(payloads, resids, w_gate, w_up, w_down, rows, capacity):
    tile = lax.axis_index("tile")
    core = tile % 2
    me = jnp.stack([tile, tile ^ 1, core]).astype(jnp.int32)
    run = functools.partial(
        experts, w_gate=w_gate, w_up=w_up, w_down=w_down, blocks=1, rows=rows, capacity=capacity
    )
    sizes = dict(blocks=1, rows=rows, capacity=capacity)
    moved = []
    for own in payloads:
        from_x, from_y = swap(own, 2), swap(own, 4)
        moved.append((own, from_x, from_y, swap_turned(jnp.where(core == 0, from_x, from_y))))
    parts = []
    for index, (own, from_x, from_y, diag) in enumerate(moved):
        near = (own, from_x, from_y)
        near_mine, near_sib = run(me, near, [swap(a, 1) for a in near])
        diag_mine, diag_sib = run(me, [diag], [swap(diag, 1)])
        back_diag = swap(diag_sib, 1)
        back_near = swap(near_sib, 1)
        (sum_diag,) = combine(me, [diag], diag_mine, back_diag, None, **sizes)
        carry = swap_turned(sum_diag)
        sum_x, sum_y = combine(
            me, [from_x, from_y], near_mine[capacity:], back_near[capacity:], carry, **sizes
        )
        parts.append((own, resids[index], near_mine, back_near, swap(sum_x, 2), swap(sum_y, 4)))
    return finish(me, parts, rows, capacity)


def local(
    inputs,
    queries,
    key_vectors,
    values,
    out_weight,
    norm_gain,
    routes,
    route_gates,
    w_gate,
    w_up,
    w_down,
):
    row_count = inputs.shape[0]
    tiles = lax.axis_size("tile")
    tile = lax.axis_index("tile")
    width = R_IL * PLANE
    rows = row_count // 2
    capacity = row_count * routes.shape[1] // tiles
    up = [(i, i + 1) for i in range(tiles - 1)]
    down = [(j, i) for i, j in up]
    before = lax.ppermute(
        jnp.concatenate([key_vectors[-width:], values[-width:]], axis=0), "tile", up
    )
    after = lax.ppermute(
        jnp.concatenate([key_vectors[:width], values[:width]], axis=0), "tile", down
    )
    live = jnp.stack([tile > 0, tile < tiles - 1]).astype(jnp.int32)
    fast = tiles == 8
    metas = [None, None]
    if fast:
        items = [routes[:, 0].astype(F32), routes[:, 1].astype(F32)]
        for k in range(2):
            gate = route_gates[:, k]
            high = lax.reduce_precision(gate, 8, 7)
            mid = lax.reduce_precision(gate - high, 8, 7)
            items += [high, mid, gate - high - mid]
        metas = [
            jnp.concatenate([a[h * rows : (h + 1) * rows] for a in items]).astype(BF16)[None]
            for h in range(2)
        ]
    resids, payloads = [], []
    for half, halo in enumerate((before, after)):
        resid, payload = attend(
            half, live, queries, key_vectors, values, halo, inputs, out_weight,
            norm_gain[None, :], metas[half],
        )
        resids.append(resid)
        payloads.append(payload)
    if fast:
        return routed_gather(payloads, resids, w_gate[0], w_up[0], w_down[0], rows, capacity)
    return routed_all_to_all(
        payloads, resids, routes, route_gates, w_gate[0], w_up[0], w_down[0]
    )


def solution(mesh):
    return jax.shard_map(
        local,
        mesh=mesh,
        in_specs=(
            P(("rep", "tile"), None),
            P(("rep", "tile"), None),
            P(("rep", "tile"), None),
            P(("rep", "tile"), None),
            P(),
            P(),
            P(("rep", "tile"), None),
            P(("rep", "tile"), None),
            P("tile", None, None),
            P("tile", None, None),
            P("tile", None, None),
        ),
        out_specs=P(("rep", "tile"), None),
        check_vma=False,
    )
```

```python
import functools

import jax
import jax.numpy as jnp
from jax import lax
from jax.experimental import pallas as pl
from jax.experimental.pallas import tpu as pltpu
from jax.sharding import PartitionSpec as P

HEADS = 16
HD = 64
IL_DEV = 4
XL = 8
DP = 8
R_IL = 2
R_XL = 2
R_DP = 2
PLANE = XL * DP
META = 16
MIB = 1024 * 1024
F32 = jnp.float32
BF16 = jnp.bfloat16
VMEM = pl.BlockSpec(memory_space=pltpu.VMEM)
SMEM = pl.BlockSpec(memory_space=pltpu.SMEM)
ANY = pl.BlockSpec(memory_space=pl.ANY)


def cost(flops, transcendentals, args, outs):
    moved = sum(a.size * a.dtype.itemsize for a in args)
    moved += sum(o.size * o.dtype.itemsize for o in outs)
    return pl.CostEstimate(flops=flops, transcendentals=transcendentals, bytes_accessed=moved)


NT = (((1,), (1,)), ((), ()))
TN = (((0,), (0,)), ((), ()))


def window_bias(keys, first_key, queries, first_query, live):
    k = lax.broadcasted_iota(jnp.int32, (keys, queries), 0) + (first_key + PLANE * R_IL)
    q = lax.broadcasted_iota(jnp.int32, (keys, queries), 1) + first_query
    near = jnp.abs(q // PLANE + R_IL - k // PLANE) <= R_IL
    near = near & (jnp.abs(q // DP % XL - k // DP % XL) <= R_XL)
    near = near & (jnp.abs(q % DP - k % DP) <= R_DP)
    if live is not None:
        near = near & (live > 0)
    bias = jnp.where(near, F32(0.0), F32(-1e30))
    return jnp.concatenate([bias, bias], axis=1)


def two_heads(query):
    lane = lax.broadcasted_iota(jnp.int32, query.shape, 1)
    query = query * BF16(1.0 / HD**0.5)
    zero = BF16(0.0)
    return jnp.concatenate(
        [jnp.where(lane < HD, query, zero), jnp.where(lane >= HD, query, zero)], axis=0
    )


def interior_kernel(count, *refs):
    q, k, v = refs[:3]
    sources = refs[3 : 3 + count]
    acc, tops, sums = refs[3 + count : 6 + count]
    kept = refs[6 + count : 6 + 2 * count]
    tail = refs[6 + 2 * count : -2]
    bias, sems = refs[-2:]
    copies = [(a, b) for a, b in zip(sources, kept)]
    if tail:
        wide = tail[0].shape[1] // 2
        start = sources[1].shape[1] - wide
        for i in range(2):
            copies.append(
                (sources[1 + i].at[:, pl.ds(start, wide)], tail[0].at[:, pl.ds(i * wide, wide)])
            )
    copies = [pltpu.make_async_copy(a, b, sems.at[i]) for i, (a, b) in enumerate(copies)]
    for copy in copies:
        copy.start()
    rows = q.shape[0]
    bias[...] = window_bias(rows, 0, rows, 0, None)
    for pair in range(HEADS // 2):
        cols = slice(pair * 2 * HD, (pair + 1) * 2 * HD)
        s = lax.dot_general(k[:, cols], two_heads(q[:, cols]), NT, preferred_element_type=F32)
        s = s + bias[...]
        top = jnp.max(s, axis=0, keepdims=True)
        p = jnp.exp(s - top)
        total = jnp.sum(p, axis=0, keepdims=True)
        o = lax.dot_general(v[:, cols], p.astype(BF16), TN, preferred_element_type=F32)
        base = pair * 2 * HD
        acc[base : base + HD, :] = o[:HD, :rows]
        acc[base + HD : base + 2 * HD, :] = o[HD:, rows:]
        for side in range(2):
            span = slice(side * rows, (side + 1) * rows)
            tops[2 * pair + side : 2 * pair + side + 1, :] = top[:, span]
            sums[2 * pair + side : 2 * pair + side + 1, :] = total[:, span]
    for copy in copies:
        copy.wait()


def interior(q, k, v, weights, tail):
    rows, model = q.shape
    outs = [
        pltpu.VMEM((model, rows), F32),
        pltpu.VMEM((HEADS, rows), F32),
        pltpu.VMEM((HEADS, rows), F32),
    ]
    outs += [pltpu.VMEM(w.shape, w.dtype) for w in weights]
    if tail:
        outs.append(pltpu.VMEM((weights[1].shape[0], 2 * tail), weights[1].dtype))
    copies = len(weights) + (2 if tail else 0)
    args = [q, k, v, *weights]
    flat = [jax.ShapeDtypeStruct(w.shape, w.dtype) for w in weights]
    return pl.pallas_call(
        functools.partial(interior_kernel, len(weights)),
        in_specs=[VMEM] * 3 + [ANY] * len(weights),
        out_specs=[VMEM] * len(outs),
        out_shape=outs,
        scratch_shapes=[pltpu.VMEM((rows, 2 * rows), F32), pltpu.SemaphoreType.DMA((copies,))],
        compiler_params=pltpu.CompilerParams(vmem_limit_bytes=24 * MIB),
        cost_estimate=cost(4 * rows * rows * model, HEADS * rows * rows, args, flat),
        name="interior",
    )(*args)


def edge_kernel(half, live, q, halo, acc, tops, sums, x, w, gain, *rest):
    meta = rest[0] if len(rest) == 5 else None
    resid, payload, bias, att = rest[-4:]
    rows = q.shape[0]
    wide = halo.shape[0] // 2
    first = -wide if half == 0 else 2 * rows
    bias[...] = window_bias(wide, first, rows, half * rows, live[half])
    span = slice(half * rows, (half + 1) * rows)
    for pair in range(HEADS // 2):
        cols = slice(pair * 2 * HD, (pair + 1) * 2 * HD)
        s = lax.dot_general(
            halo[:wide, cols], two_heads(q[:, cols]), NT, preferred_element_type=F32
        )
        s = s + bias[...]
        both = [slice(2 * pair + side, 2 * pair + side + 1) for side in range(2)]
        before = jnp.concatenate([tops[b, span] for b in both], axis=1)
        top = jnp.maximum(before, jnp.max(s, axis=0, keepdims=True))
        shrink = jnp.exp(before - top)
        p = jnp.exp(s - top)
        total = jnp.concatenate([sums[b, span] for b in both], axis=1) * shrink
        total = total + jnp.sum(p, axis=0, keepdims=True)
        o = lax.dot_general(halo[wide:, cols], p.astype(BF16), TN, preferred_element_type=F32)
        inverse = 1.0 / total
        for side in range(2):
            base = pair * 2 * HD + side * HD
            at = slice(side * rows, (side + 1) * rows)
            value = acc[base : base + HD, span] * shrink[:, at]
            value = value + o[side * HD : (side + 1) * HD, at]
            att[base : base + HD, :] = (value * inverse[:, at]).astype(BF16)
    res = x[...].astype(F32)
    res = res + lax.dot_general(att[...], w[...], TN, preferred_element_type=F32)
    res = res.astype(BF16)
    resid[...] = res
    res = res.astype(F32)
    square = jnp.mean(res * res, axis=1, keepdims=True)
    normed = (res * lax.rsqrt(square + 1e-06) * gain[...]).astype(BF16)
    payload[:rows, :] = normed
    if meta is not None:
        payload[rows:, :] = jnp.broadcast_to(meta[...], (META, meta.shape[1]))


def edge(half, live, q, halo, acc, tops, sums, x, w, gain, meta):
    rows, model = q.shape[0] // 2, q.shape[1]
    wide = halo.shape[0] // 2
    whole = lambda a: pl.BlockSpec(a.shape, lambda i: (0,) * a.ndim)
    part = pl.BlockSpec((rows, model), lambda i: (half, 0))
    args = [live, q, halo, acc, tops, sums, x, w, gain] + ([] if meta is None else [meta])
    specs = [SMEM, part, whole(halo), VMEM, VMEM, VMEM, part, VMEM, whole(gain)]
    specs += [] if meta is None else [whole(meta)]
    extra = 0 if meta is None else META
    flat = [
        jax.ShapeDtypeStruct((rows, model), BF16),
        jax.ShapeDtypeStruct((rows + extra, model), BF16),
    ]
    return pl.pallas_call(
        functools.partial(edge_kernel, half),
        grid=(1,),
        in_specs=specs,
        out_specs=[pl.BlockSpec(o.shape, lambda i: (0, 0)) for o in flat],
        out_shape=flat,
        scratch_shapes=[pltpu.VMEM((wide, 2 * rows), F32), pltpu.VMEM((model, rows), BF16)],
        compiler_params=pltpu.CompilerParams(vmem_limit_bytes=24 * MIB),
        cost_estimate=cost(
            4 * rows * wide * model + 2 * rows * model * model, HEADS * rows * wide, args, flat
        ),
        name=f"edge_half{half}",
    )(*args)


def meta_items(payload, block, rows):
    base = block * (rows + META) + rows
    meta = payload[base : base + META, :].astype(F32)
    return [meta[:, i * rows : (i + 1) * rows] for i in range(8)]


def slot_rows(hits):
    rows = hits.shape[1]
    upper = lax.broadcasted_iota(jnp.int32, (rows, rows), 0) < lax.broadcasted_iota(
        jnp.int32, (rows, rows), 1
    )
    upper = jnp.where(upper, F32(1.0), F32(0.0)).astype(BF16)
    rank = jnp.dot(hits.astype(BF16), upper, preferred_element_type=F32)
    return jnp.where(hits > 0, rank, F32(-1.0))


def pick_matrices(payload, block, rows, capacity, wanted):
    item = meta_items(payload, block, rows)
    named = [(item[0] == e, item[1] == e) for e in wanted]
    ranks = slot_rows(
        jnp.concatenate([jnp.where(a | b, F32(1.0), F32(0.0)) for a, b in named], axis=0)
    )
    slot = lax.broadcasted_iota(jnp.int32, (capacity, rows), 0).astype(F32)
    result = []
    for i, (a, b) in enumerate(named):
        gate = jnp.where(a, item[2] + item[3] + item[4], F32(0.0))
        gate = gate + jnp.where(b, item[5] + item[6] + item[7], F32(0.0))
        result.append((slot == ranks[i * META : i * META + 1, :], gate[:1, :]))
    return result


def experts_kernel(rows, capacity, tailed, me, *refs):
    ends = 8 if tailed else 7
    count = len(refs) - ends
    payloads = refs[:count]
    w_gate, w_up, w_down = refs[count : count + 3]
    tail = refs[count + 3] if tailed else None
    out_mine, out_sib, x, hidden = refs[-4:]
    expert = me[0].astype(F32)
    groups = count // 2
    order = [payloads[side * groups + g] for g in range(groups) for side in range(2)]
    hits = []
    for payload in order:
        item = meta_items(payload, 0, rows)
        hits.append(jnp.where((item[0] == expert) | (item[1] == expert), F32(1.0), F32(0.0)))
    ranks = slot_rows(jnp.concatenate(hits, axis=0))
    slot = lax.broadcasted_iota(jnp.int32, (2 * capacity, rows), 0).astype(F32)
    for g in range(groups):
        first = ranks[2 * g * META : 2 * g * META + 1, :]
        second = ranks[(2 * g + 1) * META : (2 * g + 1) * META + 1, :]
        second = jnp.where(second >= 0, second + capacity, F32(-1.0))
        hot = jnp.concatenate([slot == first, slot == second], axis=1)
        hot = jnp.where(hot, F32(1.0), F32(0.0)).astype(BF16)
        tokens = jnp.concatenate([order[2 * g][:rows, :], order[2 * g + 1][:rows, :]], axis=0)
        picked = jnp.dot(hot, tokens, preferred_element_type=F32)
        x[2 * g * capacity : (2 * g + 2) * capacity, :] = picked.astype(BF16)
    width = w_gate.shape[1]
    step = 256
    for at in range(0, width, step):
        wide = min(step, width - at)
        cols = slice(at, at + wide)
        if tail is not None and wide < step:
            both = jnp.dot(x[...], tail[...], preferred_element_type=F32)
            g, u = both[:, :wide], both[:, wide:]
        else:
            g = jnp.dot(x[...], w_gate[:, cols], preferred_element_type=F32)
            u = jnp.dot(x[...], w_up[:, cols], preferred_element_type=F32)
        hidden[:, cols] = (g / (1.0 + jnp.exp(-g)) * u).astype(BF16)
    for at in range(0, w_down.shape[1], step):
        cols = slice(at, at + step)
        o = jnp.dot(hidden[...], w_down[:, cols], preferred_element_type=F32).astype(BF16)
        for g in range(groups):
            span = slice(g * capacity, (g + 1) * capacity)
            out_mine[span, cols] = o[2 * g * capacity : (2 * g + 1) * capacity]
            out_sib[span, cols] = o[(2 * g + 1) * capacity : (2 * g + 2) * capacity]


def experts(me, mine, sib, weights, rows, capacity):
    model, width = weights[0].shape
    slots = (len(mine) + len(sib)) * capacity
    outs = [jax.ShapeDtypeStruct((slots // 2, model), BF16)] * 2
    args = [me, *mine, *sib, *weights]
    return pl.pallas_call(
        functools.partial(experts_kernel, rows, capacity, len(weights) == 4),
        in_specs=[SMEM] + [VMEM] * (len(args) - 1),
        out_specs=[VMEM] * 2,
        out_shape=outs,
        scratch_shapes=[pltpu.VMEM((slots, model), BF16), pltpu.VMEM((slots, width), BF16)],
        compiler_params=pltpu.CompilerParams(vmem_limit_bytes=24 * MIB),
        cost_estimate=cost(6 * slots * model * width, slots * width, args, outs),
        name=f"experts_{slots}",
    )(*args)


def spread(payload, block, rows, capacity, experts_two, outs_two):
    weights, values = [], []
    picks = pick_matrices(payload, block, rows, capacity, experts_two)
    for (hot, gate), out in zip(picks, outs_two):
        full = jnp.where(hot, gate, F32(0.0))
        high = full.astype(BF16)
        weights += [high, (full - high.astype(F32)).astype(BF16)]
        values += [out, out]
    return lax.dot_general(
        jnp.concatenate(weights, axis=0),
        jnp.concatenate(values, axis=0),
        (((0,), (0,)), ((), ())),
        preferred_element_type=F32,
    )


def combine_kernel(blocks, rows, capacity, groups, added, me, *refs):
    payloads = refs[:groups]
    outs_me, outs_sib = refs[groups], refs[groups + 1]
    carry = refs[groups + 2] if added else None
    results = refs[groups + 2 + (1 if added else 0) :]
    both = (me[0].astype(F32), me[1].astype(F32))
    core = me[2]
    for group in range(groups):
        for block in range(blocks):
            slot = (group * blocks + block) * capacity
            span = slice(slot, slot + capacity)
            total = spread(
                payloads[group], block, rows, capacity, both, (outs_me[span, :], outs_sib[span, :])
            )
            at = slice(block * rows, (block + 1) * rows)
            if added:
                extra = carry[at, :].astype(F32)
                total = total + jnp.where(core == group, extra, F32(0.0))
            results[group][at, :] = total.astype(BF16)


def combine(me, payloads, outs_me, outs_sib, carry, blocks, rows, capacity):
    model = payloads[0].shape[1]
    groups = len(payloads)
    args = [me, *payloads, outs_me, outs_sib] + ([] if carry is None else [carry])
    outs = [jax.ShapeDtypeStruct((blocks * rows, model), BF16)] * groups
    return pl.pallas_call(
        functools.partial(combine_kernel, blocks, rows, capacity, groups, carry is not None),
        in_specs=[SMEM] + [VMEM] * (len(args) - 1),
        out_specs=[VMEM] * groups,
        out_shape=outs,
        compiler_params=pltpu.CompilerParams(vmem_limit_bytes=24 * MIB),
        cost_estimate=cost(8 * groups * blocks * rows * capacity * model, 0, args, outs),
        name=f"combine_{groups}",
    )(*args)


def finish_kernel(blocks, rows, capacity, me, *refs):
    out = refs[-1]
    both = (me[0].astype(F32), me[1].astype(F32))
    for block in range(blocks):
        payload, resid, mine, sib, from_x, from_y = refs[block * 6 : block * 6 + 6]
        total = spread(payload, 0, rows, capacity, both, (mine[:capacity, :], sib[:capacity, :]))
        total = total + from_x[...].astype(F32) + from_y[...].astype(F32)
        total = total + resid[...].astype(F32)
        out[block * rows : (block + 1) * rows, :] = total.astype(BF16)


def finish(me, parts, rows, capacity):
    model = parts[0][0].shape[1]
    args = [me] + [a for part in parts for a in part]
    outs = [jax.ShapeDtypeStruct((len(parts) * rows, model), BF16)]
    return pl.pallas_call(
        functools.partial(finish_kernel, len(parts), rows, capacity),
        in_specs=[SMEM] + [VMEM] * (len(args) - 1),
        out_specs=VMEM,
        out_shape=outs[0],
        compiler_params=pltpu.CompilerParams(vmem_limit_bytes=24 * MIB),
        cost_estimate=cost(8 * len(parts) * rows * capacity * model, 0, args, outs),
        name="finish",
    )(*args)


def expert_rows(token_rows, gate_mat, up_mat, down_mat):
    gate_part = jnp.dot(token_rows, gate_mat, preferred_element_type=F32)
    up_part = jnp.dot(token_rows, up_mat, preferred_element_type=F32)
    hidden = (jax.nn.silu(gate_part) * up_part).astype(BF16)
    return jnp.dot(hidden, down_mat, preferred_element_type=F32).astype(BF16)


def slot_ranks(routes, experts_count, block_rows):
    row_count = routes.shape[0]
    expert_ids = jnp.arange(experts_count, dtype=jnp.int32)
    matches = routes[:, :, None] == expert_ids[None, None, :]
    hits = jnp.sum(matches.astype(jnp.int32), axis=1)
    hits = hits.reshape(row_count // block_rows, block_rows, experts_count)
    earlier = (jnp.cumsum(hits, axis=1) - hits).reshape(row_count, experts_count)
    return jnp.sum(jnp.where(matches, earlier[:, None, :], 0), axis=-1)


def routed_all_to_all(normed_parts, resid_parts, routes, route_gates, w_gate, w_up, w_down):
    tiles = lax.axis_size("tile")
    row_count, route_width = routes.shape
    block_rows, model = normed_parts[0].shape
    capacity = row_count * route_width // tiles
    slot_rank = slot_ranks(routes, tiles, block_rows)
    pieces = []
    for index, part_normed in enumerate(normed_parts):
        rows = slice(index * block_rows, (index + 1) * block_rows)
        positions = routes[rows] * capacity + slot_rank[rows]
        copies = jnp.broadcast_to(
            part_normed[:, None, :], (block_rows, route_width, model)
        ).reshape(-1, model)
        outgoing = jnp.zeros((tiles * capacity, model), BF16).at[positions.reshape(-1)].set(copies)
        outgoing = outgoing.reshape(tiles, capacity, model)
        received = lax.all_to_all(outgoing, "tile", split_axis=0, concat_axis=0, tiled=True)
        produced = expert_rows(received.reshape(-1, model), w_gate, w_up, w_down)
        produced = produced.reshape(received.shape)
        returned = lax.all_to_all(produced, "tile", split_axis=0, concat_axis=0, tiled=True)
        picked = returned.reshape(-1, model)[positions].astype(F32)
        combined = jnp.sum(route_gates[rows][:, :, None] * picked, axis=1)
        pieces.append((resid_parts[index].astype(F32) + combined).astype(BF16))
    return jnp.concatenate(pieces, axis=0)


def swap(array, bit):
    return lax.ppermute(array, "tile", [(i, i ^ bit) for i in range(8)])


def swap_turned(array):
    return lax.ppermute(array, "tile", [(i, i ^ (2 if i % 2 else 4)) for i in range(8)])


def routed_gather(payloads, resids, weights, rows, capacity):
    tile = lax.axis_index("tile")
    core = tile % 2
    me = jnp.stack([tile, tile ^ 1, core]).astype(jnp.int32)
    run = functools.partial(experts, weights=weights, rows=rows, capacity=capacity)
    sizes = dict(blocks=1, rows=rows, capacity=capacity)
    moved = []
    for own in payloads:
        from_x, from_y = swap(own, 2), swap(own, 4)
        moved.append((own, from_x, from_y, swap_turned(jnp.where(core == 0, from_x, from_y))))
    parts = []
    for index, (own, from_x, from_y, diag) in enumerate(moved):
        near = (own, from_x, from_y)
        near_mine, near_sib = run(me, near, [swap(a, 1) for a in near])
        diag_mine, diag_sib = run(me, [diag], [swap(diag, 1)])
        back_diag = swap(diag_sib, 1)
        back_near = swap(near_sib, 1)
        (sum_diag,) = combine(me, [diag], diag_mine, back_diag, None, **sizes)
        carry = swap_turned(sum_diag)
        sum_x, sum_y = combine(
            me, [from_x, from_y], near_mine[capacity:], back_near[capacity:], carry, **sizes
        )
        parts.append((own, resids[index], near_mine, back_near, swap(sum_x, 2), swap(sum_y, 4)))
    return finish(me, parts, rows, capacity)


def local(
    inputs,
    queries,
    key_vectors,
    values,
    out_weight,
    norm_gain,
    routes,
    route_gates,
    w_gate,
    w_up,
    w_down,
):
    row_count = inputs.shape[0]
    tiles = lax.axis_size("tile")
    tile = lax.axis_index("tile")
    width = R_IL * PLANE
    rows = row_count // 2
    capacity = row_count * routes.shape[1] // tiles
    up = [(i, i + 1) for i in range(tiles - 1)]
    down = [(j, i) for i, j in up]
    last = jnp.concatenate([key_vectors[-width:], values[-width:]], axis=0)
    before = lax.ppermute(last, "tile", up)
    live = jnp.stack([tile > 0, tile < tiles - 1]).astype(jnp.int32)
    fast = tiles == 8
    weights, metas, tail = [out_weight], [None, None], 0
    if fast:
        weights += [w_gate[0], w_up[0], w_down[0]]
        tail = 128 if w_gate.shape[2] % 256 == 128 else 0
        items = [routes[:, 0].astype(F32), routes[:, 1].astype(F32)]
        for k in range(2):
            gate = route_gates[:, k]
            high = lax.reduce_precision(gate, 8, 7)
            mid = lax.reduce_precision(gate - high, 8, 7)
            items += [high, mid, gate - high - mid]
        metas = [
            jnp.concatenate([a[h * rows : (h + 1) * rows] for a in items]).astype(BF16)[None]
            for h in range(2)
        ]
    acc, tops, sums, *kept = interior(queries, key_vectors, values, weights, tail)
    first = jnp.concatenate([key_vectors[:width], values[:width]], axis=0)
    first, acc = lax.optimization_barrier((first, acc))
    after = lax.ppermute(first, "tile", down)
    resids, payloads = [], []
    for half, halo in enumerate((before, after)):
        resid, payload = edge(
            half, live, queries, halo, acc, tops, sums, inputs, kept[0],
            norm_gain[None, :], metas[half],
        )
        resids.append(resid)
        payloads.append(payload)
    if fast:
        return routed_gather(payloads, resids, kept[1:], rows, capacity)
    return routed_all_to_all(
        payloads, resids, routes, route_gates, w_gate[0], w_up[0], w_down[0]
    )


def solution(mesh):
    return jax.shard_map(
        local,
        mesh=mesh,
        in_specs=(
            P(("rep", "tile"), None),
            P(("rep", "tile"), None),
            P(("rep", "tile"), None),
            P(("rep", "tile"), None),
            P(),
            P(),
            P(("rep", "tile"), None),
            P(("rep", "tile"), None),
            P("tile", None, None),
            P("tile", None, None),
            P("tile", None, None),
        ),
        out_specs=P(("rep", "tile"), None),
        check_vma=False,
    )
```

```python
import functools

import jax
import jax.numpy as jnp
from jax import lax
from jax.experimental import pallas as pl
from jax.experimental.pallas import tpu as pltpu
from jax.sharding import PartitionSpec as P

HEADS = 16
HD = 64
IL_DEV = 4
XL = 8
DP = 8
R_IL = 2
R_XL = 2
R_DP = 2
PLANE = XL * DP
META = 16
MIB = 1024 * 1024
LONG = 30
F32 = jnp.float32
BF16 = jnp.bfloat16
VMEM = pl.BlockSpec(memory_space=pltpu.VMEM)
SMEM = pl.BlockSpec(memory_space=pltpu.SMEM)
ANY = pl.BlockSpec(memory_space=pl.ANY)


def far(array):
    return pltpu.with_memory_space_constraint(array, pltpu.HBM)


def cost(flops, transcendentals, args, outs):
    moved = sum(a.size * a.dtype.itemsize for a in args)
    moved += sum(o.size * o.dtype.itemsize for o in outs)
    return pl.CostEstimate(flops=flops, transcendentals=transcendentals, bytes_accessed=moved)


NT = (((1,), (1,)), ((), ()))
TN = (((0,), (0,)), ((), ()))


def window_bias(keys, first_key, queries, first_query, live):
    k = lax.broadcasted_iota(jnp.int32, (keys, queries), 0) + (first_key + PLANE * R_IL)
    q = lax.broadcasted_iota(jnp.int32, (keys, queries), 1) + first_query
    near = jnp.abs(q // PLANE + R_IL - k // PLANE) <= R_IL
    near = near & (jnp.abs(q // DP % XL - k // DP % XL) <= R_XL)
    near = near & (jnp.abs(q % DP - k % DP) <= R_DP)
    if live is not None:
        near = near & (live > 0)
    bias = jnp.where(near, F32(0.0), F32(-1e30))
    return jnp.concatenate([bias, bias], axis=1)


def two_heads(query):
    lane = lax.broadcasted_iota(jnp.int32, query.shape, 1)
    query = query * BF16(1.0 / HD**0.5)
    zero = BF16(0.0)
    return jnp.concatenate(
        [jnp.where(lane < HD, query, zero), jnp.where(lane >= HD, query, zero)], axis=0
    )


def pack_kernel(width, k, v, last, first, sems):
    end = k.shape[0] - width
    copies = [
        (k.at[pl.ds(end, width)], last.at[pl.ds(0, width)]),
        (v.at[pl.ds(end, width)], last.at[pl.ds(width, width)]),
        (k.at[pl.ds(0, width)], first.at[pl.ds(0, width)]),
        (v.at[pl.ds(0, width)], first.at[pl.ds(width, width)]),
    ]
    copies = [pltpu.make_async_copy(a, b, sems.at[i]) for i, (a, b) in enumerate(copies)]
    for copy in copies:
        copy.start()
    for copy in copies:
        copy.wait()


def pack(k, v, width):
    flat = [jax.ShapeDtypeStruct((2 * width, k.shape[1]), k.dtype)] * 2
    return pl.pallas_call(
        functools.partial(pack_kernel, width),
        in_specs=[ANY] * 2,
        out_specs=[VMEM] * 2,
        out_shape=flat,
        scratch_shapes=[pltpu.SemaphoreType.DMA((4,))],
        compiler_params=pltpu.CompilerParams(vmem_limit_bytes=12 * MIB),
        cost_estimate=cost(0, 0, flat, flat),
        name="pack",
    )(*[far(a) for a in (k, v)])


def interior_kernel(q, k, v, acc, tops, sums, bias):
    rows = q.shape[0]
    bias[...] = window_bias(rows, 0, rows, 0, None)
    for pair in range(HEADS // 2):
        cols = slice(pair * 2 * HD, (pair + 1) * 2 * HD)
        s = lax.dot_general(k[:, cols], two_heads(q[:, cols]), NT, preferred_element_type=F32)
        s = s + bias[...]
        top = jnp.max(s, axis=0, keepdims=True)
        p = jnp.exp(s - top)
        total = jnp.sum(p, axis=0, keepdims=True)
        o = lax.dot_general(v[:, cols], p.astype(BF16), TN, preferred_element_type=F32)
        base = pair * 2 * HD
        acc[base : base + HD, :] = o[:HD, :rows]
        acc[base + HD : base + 2 * HD, :] = o[HD:, rows:]
        for side in range(2):
            span = slice(side * rows, (side + 1) * rows)
            tops[2 * pair + side : 2 * pair + side + 1, :] = top[:, span]
            sums[2 * pair + side : 2 * pair + side + 1, :] = total[:, span]


def interior(q, k, v):
    rows, model = q.shape
    flat = [jax.ShapeDtypeStruct(shape, F32) for shape in ((model, rows), (HEADS, rows), (HEADS, rows))]
    args = [far(a) for a in (q, k, v)]
    return pl.pallas_call(
        interior_kernel,
        in_specs=[VMEM] * 3,
        out_specs=[VMEM] * 3,
        out_shape=[pltpu.HBM(o.shape, o.dtype) for o in flat],
        scratch_shapes=[pltpu.VMEM((rows, 2 * rows), F32)],
        compiler_params=pltpu.CompilerParams(vmem_limit_bytes=12 * MIB),
        cost_estimate=cost(LONG * 4 * rows * rows * model, HEADS * rows * rows, args, flat),
        name="interior",
    )(*args)


def edge_kernel(live, q, before, behind, tops, sums, gain, acc_far, x_far, w_far, *rest):
    meta = rest[0] if len(rest) == 9 else None
    resid, payload = rest[-8:-6]
    bias, att, acc, x, w, sems = rest[-6:]
    step = 2 * HD
    pairs = HEADS // 2
    fetches = []
    for pair in range(pairs):
        span = pl.ds(pair * step, step)
        fetches.append((acc_far.at[span], acc.at[span]))
    fetches += [(x_far, x), (w_far, w)]
    fetches = [pltpu.make_async_copy(a, b, sems.at[i]) for i, (a, b) in enumerate(fetches)]
    for fetch in fetches:
        fetch.start()
    rows = q.shape[0] // 2
    wide = before.shape[0] // 2
    halos = (before, behind)
    for half in range(2):
        first = -wide if half == 0 else 2 * rows
        bias[half] = window_bias(wide, first, rows, half * rows, live[half])
    for pair in range(pairs):
        cols = slice(pair * step, (pair + 1) * step)
        fetches[pair].wait()
        for half, halo in enumerate(halos):
            span = slice(half * rows, (half + 1) * rows)
            queries = two_heads(q[span, cols])
            s = lax.dot_general(halo[:wide, cols], queries, NT, preferred_element_type=F32)
            s = s + bias[half]
            both = [slice(2 * pair + side, 2 * pair + side + 1) for side in range(2)]
            old = jnp.concatenate([tops[b, span] for b in both], axis=1)
            top = jnp.maximum(old, jnp.max(s, axis=0, keepdims=True))
            shrink = jnp.exp(old - top)
            p = jnp.exp(s - top)
            total = jnp.concatenate([sums[b, span] for b in both], axis=1) * shrink
            total = total + jnp.sum(p, axis=0, keepdims=True)
            o = lax.dot_general(halo[wide:, cols], p.astype(BF16), TN, preferred_element_type=F32)
            inverse = 1.0 / total
            for side in range(2):
                at = slice(side * rows, (side + 1) * rows)
                base = pair * step + side * HD
                value = acc[base : base + HD, span] * shrink[:, at]
                value = value + o[side * HD : (side + 1) * HD, at]
                att[base : base + HD, span] = (value * inverse[:, at]).astype(BF16)
    fetches[pairs].wait()
    fetches[pairs + 1].wait()
    for half in range(2):
        span = slice(half * rows, (half + 1) * rows)
        res = x[span, :].astype(F32)
        res = res + lax.dot_general(att[:, span], w[...], TN, preferred_element_type=F32)
        res = res.astype(BF16)
        resid[span, :] = res
        res = res.astype(F32)
        square = jnp.mean(res * res, axis=1, keepdims=True)
        normed = (res * lax.rsqrt(square + 1e-06) * gain[...]).astype(BF16)
        start = half * payload.shape[0] // 2
        payload[start : start + rows, :] = normed
        if meta is not None:
            payload[start + rows : start + rows + META, :] = jnp.broadcast_to(
                meta[half : half + 1, :], (META, meta.shape[1])
            )


def edge(live, q, before, behind, acc, tops, sums, x, w, gain, meta):
    rows, model = q.shape[0] // 2, q.shape[1]
    wide = before.shape[0] // 2
    before, behind, acc, tops, sums = [far(a) for a in (before, behind, acc, tops, sums)]
    args = [live, q, before, behind, tops, sums, gain, acc, x, w]
    args += [] if meta is None else [meta]
    specs = [SMEM] + [VMEM] * 6 + [ANY] * 3 + ([] if meta is None else [VMEM])
    extra = 0 if meta is None else META
    flat = [
        jax.ShapeDtypeStruct((2 * rows, model), BF16),
        jax.ShapeDtypeStruct((2 * (rows + extra), model), BF16),
    ]
    return pl.pallas_call(
        edge_kernel,
        in_specs=specs,
        out_specs=[VMEM] * 2,
        out_shape=[pltpu.HBM(o.shape, o.dtype) for o in flat],
        scratch_shapes=[
            pltpu.VMEM((2, wide, 2 * rows), F32),
            pltpu.VMEM((model, 2 * rows), BF16),
            pltpu.VMEM(acc.shape, acc.dtype),
            pltpu.VMEM(x.shape, x.dtype),
            pltpu.VMEM(w.shape, w.dtype),
            pltpu.SemaphoreType.DMA((HEADS // 2 + 2,)),
        ],
        compiler_params=pltpu.CompilerParams(vmem_limit_bytes=12 * MIB),
        cost_estimate=cost(
            LONG * (8 * rows * wide * model + 4 * rows * model * model), 2 * HEADS * rows * wide, args, flat
        ),
        name="edge",
    )(*args)


def meta_items(payload, block, rows):
    base = block * (rows + META) + rows
    meta = payload[base : base + META, :].astype(F32)
    return [meta[:, i * rows : (i + 1) * rows] for i in range(8)]


def slot_rows(hits):
    rows = hits.shape[1]
    upper = lax.broadcasted_iota(jnp.int32, (rows, rows), 0) < lax.broadcasted_iota(
        jnp.int32, (rows, rows), 1
    )
    upper = jnp.where(upper, F32(1.0), F32(0.0)).astype(BF16)
    rank = jnp.dot(hits.astype(BF16), upper, preferred_element_type=F32)
    return jnp.where(hits > 0, rank, F32(-1.0))


def pick_matrices(payload, block, rows, capacity, wanted):
    item = meta_items(payload, block, rows)
    named = [(item[0] == e, item[1] == e) for e in wanted]
    ranks = slot_rows(
        jnp.concatenate([jnp.where(a | b, F32(1.0), F32(0.0)) for a, b in named], axis=0)
    )
    slot = lax.broadcasted_iota(jnp.int32, (capacity, rows), 0).astype(F32)
    result = []
    for i, (a, b) in enumerate(named):
        gate = jnp.where(a, item[2] + item[3] + item[4], F32(0.0))
        gate = gate + jnp.where(b, item[5] + item[6] + item[7], F32(0.0))
        result.append((slot == ranks[i * META : i * META + 1, :], gate[:1, :]))
    return result


def experts_kernel(order, rows, capacity, me, *refs):
    payloads = refs[:-8]
    w_gate, w_up, w_down, out_mine, out_sib, x, hidden, tail = refs[-8:]
    width, model, step = w_gate.shape[1], w_down.shape[1], 256
    expert = me[0].astype(F32)
    groups = len(order) // 2
    hits = []
    for array, block in order:
        item = meta_items(payloads[array], block, rows)
        hits.append(jnp.where((item[0] == expert) | (item[1] == expert), F32(1.0), F32(0.0)))
    ranks = slot_rows(jnp.concatenate(hits, axis=0))
    slot = lax.broadcasted_iota(jnp.int32, (2 * capacity, rows), 0).astype(F32)
    for g in range(groups):
        first = ranks[2 * g * META : 2 * g * META + 1, :]
        second = ranks[(2 * g + 1) * META : (2 * g + 1) * META + 1, :]
        second = jnp.where(second >= 0, second + capacity, F32(-1.0))
        hot = jnp.concatenate([slot == first, slot == second], axis=1)
        hot = jnp.where(hot, F32(1.0), F32(0.0)).astype(BF16)
        tokens = []
        for array, block in order[2 * g : 2 * g + 2]:
            base = block * (rows + META)
            tokens.append(payloads[array][base : base + rows, :])
        picked = jnp.dot(hot, jnp.concatenate(tokens, axis=0), preferred_element_type=F32)
        x[2 * g * capacity : (2 * g + 2) * capacity, :] = picked.astype(BF16)
    for at in range(0, width, step):
        wide = min(step, width - at)
        cols = slice(at, at + wide)
        if wide < step:
            tail[:, :wide] = w_gate[:, cols]
            tail[:, wide : 2 * wide] = w_up[:, cols]
            both = jnp.dot(x[...], tail[...], preferred_element_type=F32)
            g, u = both[:, :wide], both[:, wide:]
        else:
            g = jnp.dot(x[...], w_gate[:, cols], preferred_element_type=F32)
            u = jnp.dot(x[...], w_up[:, cols], preferred_element_type=F32)
        hidden[:, cols] = (g / (1.0 + jnp.exp(-g)) * u).astype(BF16)
    for at in range(0, model, step):
        cols = slice(at, at + step)
        o = jnp.dot(hidden[...], w_down[:, cols], preferred_element_type=F32).astype(BF16)
        for g in range(groups):
            span = slice(g * capacity, (g + 1) * capacity)
            out_mine[span, cols] = o[2 * g * capacity : (2 * g + 1) * capacity]
            out_sib[span, cols] = o[(2 * g + 1) * capacity : (2 * g + 2) * capacity]


def experts(me, payloads, order, weights, rows, capacity):
    model, width = weights[0].shape
    slots = len(order) * capacity
    left = width % 256
    outs = [jax.ShapeDtypeStruct((slots // 2, model), BF16)] * 2
    args = [me, *payloads, *weights]
    return pl.pallas_call(
        functools.partial(experts_kernel, order, rows, capacity),
        in_specs=[SMEM] + [VMEM] * (len(args) - 1),
        out_specs=[VMEM] * 2,
        out_shape=outs,
        scratch_shapes=[
            pltpu.VMEM((slots, model), BF16),
            pltpu.VMEM((slots, width), BF16),
            pltpu.VMEM((model, max(2 * left, 256)), BF16),
        ],
        compiler_params=pltpu.CompilerParams(vmem_limit_bytes=12 * MIB),
        cost_estimate=cost(6 * slots * model * width, slots * width, args, outs),
        name=f"experts_{slots}",
    )(*args)


def spread(payload, block, rows, capacity, experts_two, outs_two):
    weights, values = [], []
    picks = pick_matrices(payload, block, rows, capacity, experts_two)
    for (hot, gate), out in zip(picks, outs_two):
        full = jnp.where(hot, gate, F32(0.0))
        high = full.astype(BF16)
        weights += [high, (full - high.astype(F32)).astype(BF16)]
        values += [out, out]
    return lax.dot_general(
        jnp.concatenate(weights, axis=0),
        jnp.concatenate(values, axis=0),
        (((0,), (0,)), ((), ())),
        preferred_element_type=F32,
    )


def combine_kernel(rows, capacity, me, payload, outs_me, outs_sib, *refs):
    result = refs[-1]
    both = (me[0].astype(F32), me[1].astype(F32))
    for block in range(payload.shape[0] // (rows + META)):
        span = slice(block * capacity, (block + 1) * capacity)
        total = spread(payload, block, rows, capacity, both, (outs_me[span, :], outs_sib[span, :]))
        at = slice(block * rows, (block + 1) * rows)
        if len(refs) == 2:
            total = total + refs[0][at, :].astype(F32)
        result[at, :] = total.astype(BF16)


def combine(me, payload, outs_me, outs_sib, carry, rows, capacity):
    blocks, model = payload.shape[0] // (rows + META), payload.shape[1]
    args = [me, payload, outs_me, outs_sib] + ([] if carry is None else [carry])
    outs = [jax.ShapeDtypeStruct((blocks * rows, model), BF16)]
    return pl.pallas_call(
        functools.partial(combine_kernel, rows, capacity),
        in_specs=[SMEM] + [VMEM] * (len(args) - 1),
        out_specs=VMEM,
        out_shape=outs[0],
        compiler_params=pltpu.CompilerParams(vmem_limit_bytes=12 * MIB),
        cost_estimate=cost(8 * blocks * rows * capacity * model, 0, args, outs),
        name="combine",
    )(*args)


def base_kernel(rows, capacity, me, payload, resid, outs_me, outs_sib, result):
    both = (me[0].astype(F32), me[1].astype(F32))
    for block in range(payload.shape[0] // (rows + META)):
        span = slice(block * capacity, (block + 1) * capacity)
        total = spread(payload, block, rows, capacity, both, (outs_me[span, :], outs_sib[span, :]))
        at = slice(block * rows, (block + 1) * rows)
        result[at, :] = total + resid[at, :].astype(F32)


def base(me, payload, resid, outs_me, outs_sib, rows, capacity):
    args = [me, payload, resid, outs_me, outs_sib]
    out = jax.ShapeDtypeStruct(resid.shape, F32)
    return pl.pallas_call(
        functools.partial(base_kernel, rows, capacity),
        in_specs=[SMEM] + [VMEM] * 4,
        out_specs=VMEM,
        out_shape=out,
        compiler_params=pltpu.CompilerParams(vmem_limit_bytes=12 * MIB),
        cost_estimate=cost(8 * resid.size * capacity, 0, args, [out]),
        name="base",
    )(*args)


def finish_kernel(total, first, second, out):
    out[...] = (total[...] + first[...].astype(F32) + second[...].astype(F32)).astype(BF16)


def finish(total, first, second):
    args = [total, first, second]
    return pl.pallas_call(
        finish_kernel,
        in_specs=[VMEM] * 3,
        out_specs=VMEM,
        out_shape=jax.ShapeDtypeStruct(first.shape, first.dtype),
        compiler_params=pltpu.CompilerParams(vmem_limit_bytes=12 * MIB),
        cost_estimate=cost(3 * total.size, 0, args, args[1:2]),
        name="finish",
    )(*args)


def expert_rows(token_rows, gate_mat, up_mat, down_mat):
    gate_part = jnp.dot(token_rows, gate_mat, preferred_element_type=F32)
    up_part = jnp.dot(token_rows, up_mat, preferred_element_type=F32)
    hidden = (jax.nn.silu(gate_part) * up_part).astype(BF16)
    return jnp.dot(hidden, down_mat, preferred_element_type=F32).astype(BF16)


def slot_ranks(routes, experts_count, block_rows):
    row_count = routes.shape[0]
    expert_ids = jnp.arange(experts_count, dtype=jnp.int32)
    matches = routes[:, :, None] == expert_ids[None, None, :]
    hits = jnp.sum(matches.astype(jnp.int32), axis=1)
    hits = hits.reshape(row_count // block_rows, block_rows, experts_count)
    earlier = (jnp.cumsum(hits, axis=1) - hits).reshape(row_count, experts_count)
    return jnp.sum(jnp.where(matches, earlier[:, None, :], 0), axis=-1)


def routed_all_to_all(normed, resid, routes, route_gates, w_gate, w_up, w_down):
    tiles = lax.axis_size("tile")
    row_count, route_width = routes.shape
    block_rows, model = row_count // 2, normed.shape[1]
    capacity = row_count * route_width // tiles
    slot_rank = slot_ranks(routes, tiles, block_rows)
    pieces = []
    for index in range(2):
        rows = slice(index * block_rows, (index + 1) * block_rows)
        part_normed = normed[rows]
        positions = routes[rows] * capacity + slot_rank[rows]
        copies = jnp.broadcast_to(
            part_normed[:, None, :], (block_rows, route_width, model)
        ).reshape(-1, model)
        outgoing = jnp.zeros((tiles * capacity, model), BF16).at[positions.reshape(-1)].set(copies)
        outgoing = outgoing.reshape(tiles, capacity, model)
        received = lax.all_to_all(outgoing, "tile", split_axis=0, concat_axis=0, tiled=True)
        produced = expert_rows(received.reshape(-1, model), w_gate, w_up, w_down)
        produced = produced.reshape(received.shape)
        returned = lax.all_to_all(produced, "tile", split_axis=0, concat_axis=0, tiled=True)
        picked = returned.reshape(-1, model)[positions].astype(F32)
        combined = jnp.sum(route_gates[rows][:, :, None] * picked, axis=1)
        pieces.append((resid[rows].astype(F32) + combined).astype(BF16))
    return jnp.concatenate(pieces, axis=0)


def swap(array, bit):
    return lax.ppermute(array, "tile", [(i, i ^ bit) for i in range(8)])


def swap_by_core(array, bits):
    return lax.ppermute(array, "tile", [(i, i ^ bits[i % 2]) for i in range(8)])


def after(first, *later):
    return lax.optimization_barrier((first, *later))[1:]


def routed_gather(payload, resid, weights, rows, capacity):
    tile = lax.axis_index("tile")
    me = jnp.stack([tile, tile ^ 1]).astype(jnp.int32)
    sizes = dict(rows=rows, capacity=capacity)

    def evaluate(mine, theirs):
        order = [(0, 0), (1, 0), (0, 1), (1, 1)]
        kept, sent = experts(me, (mine, theirs), order, weights, **sizes)
        return kept, swap(sent, 1)

    sib = swap(payload, 1)
    first = swap_by_core(payload, (2, 4))
    out_own = evaluate(payload, sib)
    (first,) = after(out_own[0], first)
    diag = swap_by_core(first, (4, 2))
    out_first = evaluate(first, swap(first, 1))
    (diag,) = after(out_first[0], diag)
    second = swap_by_core(*after(diag, payload), (4, 2))
    out_diag = evaluate(diag, swap(diag, 1))
    sum_diag = combine(me, diag, *out_diag, None, **sizes)
    carry = swap_by_core(sum_diag, (4, 2))
    (second,) = after(sum_diag, second)
    out_second = evaluate(second, swap(second, 1))
    sum_second = combine(me, second, *out_second, None, **sizes)
    back_second = swap_by_core(sum_second, (4, 2))
    sum_first = combine(me, first, *out_first, *after(sum_second, carry), **sizes)
    back_first = swap_by_core(sum_first, (2, 4))
    total = base(me, payload, resid, *after(sum_first, *out_own), **sizes)
    return finish(total, back_first, back_second)


def local(
    inputs,
    queries,
    key_vectors,
    values,
    out_weight,
    norm_gain,
    routes,
    route_gates,
    w_gate,
    w_up,
    w_down,
):
    row_count = inputs.shape[0]
    tiles = lax.axis_size("tile")
    tile = lax.axis_index("tile")
    width = R_IL * PLANE
    rows = row_count // 2
    capacity = row_count * routes.shape[1] // tiles
    up = [(i, i + 1) for i in range(tiles - 1)]
    down = [(j, i) for i, j in up]
    last, first = pack(key_vectors, values, width)
    before = lax.ppermute(last, "tile", up)
    behind = lax.ppermute(first, "tile", down)
    live = jnp.stack([tile > 0, tile < tiles - 1]).astype(jnp.int32)
    fast = tiles == 8
    meta = None
    if fast:
        items = [routes[:, 0].astype(F32), routes[:, 1].astype(F32)]
        for k in range(2):
            gate = route_gates[:, k]
            high = lax.reduce_precision(gate, 8, 7)
            mid = lax.reduce_precision(gate - high, 8, 7)
            items += [high, mid, gate - high - mid]
        meta = jnp.stack(items).reshape(len(items), 2, rows).swapaxes(0, 1)
        meta = meta.reshape(2, len(items) * rows).astype(BF16)
    acc, tops, sums = interior(queries, key_vectors, values)
    resid, payload = edge(
        live, queries, before, behind, acc, tops, sums, inputs, out_weight,
        norm_gain[None, :], meta,
    )
    if fast:
        weights = (w_gate[0], w_up[0], w_down[0])
        return routed_gather(payload, resid, weights, rows, capacity)
    return routed_all_to_all(payload, resid, routes, route_gates, w_gate[0], w_up[0], w_down[0])


def solution(mesh):
    return jax.shard_map(
        local,
        mesh=mesh,
        in_specs=(
            P(("rep", "tile"), None),
            P(("rep", "tile"), None),
            P(("rep", "tile"), None),
            P(("rep", "tile"), None),
            P(),
            P(),
            P(("rep", "tile"), None),
            P(("rep", "tile"), None),
            P("tile", None, None),
            P("tile", None, None),
            P("tile", None, None),
        ),
        out_specs=P(("rep", "tile"), None),
        check_vma=False,
    )
```

```python
import functools

import jax
import jax.numpy as jnp
from jax import lax
from jax.experimental import pallas as pl
from jax.experimental.pallas import tpu as pltpu
from jax.sharding import PartitionSpec as P

HEADS = 16
HD = 64
IL_DEV = 4
XL = 8
DP = 8
R_IL = 2
R_XL = 2
R_DP = 2
PLANE = XL * DP
META = 16
MIB = 1024 * 1024
LONG = 30
F32 = jnp.float32
BF16 = jnp.bfloat16
VMEM = pl.BlockSpec(memory_space=pltpu.VMEM)
SMEM = pl.BlockSpec(memory_space=pltpu.SMEM)
ANY = pl.BlockSpec(memory_space=pl.ANY)


def far(array):
    return pltpu.with_memory_space_constraint(array, pltpu.HBM)


def cost(flops, transcendentals, args, outs):
    moved = sum(a.size * a.dtype.itemsize for a in args)
    moved += sum(o.size * o.dtype.itemsize for o in outs)
    return pl.CostEstimate(flops=flops, transcendentals=transcendentals, bytes_accessed=moved)


NT = (((1,), (1,)), ((), ()))
TN = (((0,), (0,)), ((), ()))


def window_bias(keys, first_key, queries, first_query, live):
    k = lax.broadcasted_iota(jnp.int32, (keys, queries), 0) + (first_key + PLANE * R_IL)
    q = lax.broadcasted_iota(jnp.int32, (keys, queries), 1) + first_query
    near = jnp.abs(q // PLANE + R_IL - k // PLANE) <= R_IL
    near = near & (jnp.abs(q // DP % XL - k // DP % XL) <= R_XL)
    near = near & (jnp.abs(q % DP - k % DP) <= R_DP)
    if live is not None:
        near = near & (live > 0)
    bias = jnp.where(near, F32(0.0), F32(-1e30))
    return jnp.concatenate([bias, bias], axis=1)


def two_heads(query):
    lane = lax.broadcasted_iota(jnp.int32, query.shape, 1)
    query = query * BF16(1.0 / HD**0.5)
    zero = BF16(0.0)
    return jnp.concatenate(
        [jnp.where(lane < HD, query, zero), jnp.where(lane >= HD, query, zero)], axis=0
    )


def pack_kernel(width, k, v, last, first, sems):
    end = k.shape[0] - width
    copies = [
        (k.at[pl.ds(end, width)], last.at[pl.ds(0, width)]),
        (v.at[pl.ds(end, width)], last.at[pl.ds(width, width)]),
        (k.at[pl.ds(0, width)], first.at[pl.ds(0, width)]),
        (v.at[pl.ds(0, width)], first.at[pl.ds(width, width)]),
    ]
    copies = [pltpu.make_async_copy(a, b, sems.at[i]) for i, (a, b) in enumerate(copies)]
    for copy in copies:
        copy.start()
    for copy in copies:
        copy.wait()


def pack(k, v, width):
    flat = [jax.ShapeDtypeStruct((2 * width, k.shape[1]), k.dtype)] * 2
    return pl.pallas_call(
        functools.partial(pack_kernel, width),
        in_specs=[ANY] * 2,
        out_specs=[VMEM] * 2,
        out_shape=flat,
        scratch_shapes=[pltpu.SemaphoreType.DMA((4,))],
        compiler_params=pltpu.CompilerParams(vmem_limit_bytes=12 * MIB),
        cost_estimate=cost(0, 0, flat, flat),
        name="pack",
    )(*[far(a) for a in (k, v)])


def interior_kernel(q, k, v, acc, tops, sums, bias):
    rows = q.shape[0]
    bias[...] = window_bias(rows, 0, rows, 0, None)
    for pair in range(HEADS // 2):
        cols = slice(pair * 2 * HD, (pair + 1) * 2 * HD)
        s = lax.dot_general(k[:, cols], two_heads(q[:, cols]), NT, preferred_element_type=F32)
        s = s + bias[...]
        top = jnp.max(s, axis=0, keepdims=True)
        p = jnp.exp(s - top)
        total = jnp.sum(p, axis=0, keepdims=True)
        o = lax.dot_general(v[:, cols], p.astype(BF16), TN, preferred_element_type=F32)
        base = pair * 2 * HD
        acc[base : base + HD, :] = o[:HD, :rows]
        acc[base + HD : base + 2 * HD, :] = o[HD:, rows:]
        for side in range(2):
            span = slice(side * rows, (side + 1) * rows)
            tops[2 * pair + side : 2 * pair + side + 1, :] = top[:, span]
            sums[2 * pair + side : 2 * pair + side + 1, :] = total[:, span]


def interior(q, k, v):
    rows, model = q.shape
    flat = [jax.ShapeDtypeStruct(shape, F32) for shape in ((model, rows), (HEADS, rows), (HEADS, rows))]
    args = [far(a) for a in (q, k, v)]
    return pl.pallas_call(
        interior_kernel,
        in_specs=[VMEM] * 3,
        out_specs=[VMEM] * 3,
        out_shape=flat,
        scratch_shapes=[pltpu.VMEM((rows, 2 * rows), F32)],
        compiler_params=pltpu.CompilerParams(vmem_limit_bytes=12 * MIB),
        cost_estimate=cost(LONG * 4 * rows * rows * model, HEADS * rows * rows, args, flat),
        name="interior",
    )(*args)


def edge_kernel(live, q, before, behind, tops, sums, gain, acc_far, x_far, w_far, *rest):
    meta = rest[0] if len(rest) == 9 else None
    resid, payload = rest[-8:-6]
    bias, att, acc, x, w, sems = rest[-6:]
    step = 2 * HD
    pairs = HEADS // 2
    fetches = []
    for pair in range(pairs):
        span = pl.ds(pair * step, step)
        fetches.append((acc_far.at[span], acc.at[span]))
    fetches += [(x_far, x), (w_far, w)]
    fetches = [pltpu.make_async_copy(a, b, sems.at[i]) for i, (a, b) in enumerate(fetches)]
    for fetch in fetches:
        fetch.start()
    rows = q.shape[0] // 2
    wide = before.shape[0] // 2
    halos = (before, behind)
    for half in range(2):
        first = -wide if half == 0 else 2 * rows
        bias[half] = window_bias(wide, first, rows, half * rows, live[half])
    cells = [(pair, half) for pair in range(pairs) for half in range(2)]
    scores = []
    for pair, half in cells:
        cols = slice(pair * step, (pair + 1) * step)
        queries = two_heads(q[half * rows : (half + 1) * rows, cols])
        s = lax.dot_general(halos[half][:wide, cols], queries, NT, preferred_element_type=F32)
        scores.append(s + bias[half])
    weights = []
    for (pair, half), s in zip(cells, scores):
        span = slice(half * rows, (half + 1) * rows)
        both = [slice(2 * pair + side, 2 * pair + side + 1) for side in range(2)]
        old = jnp.concatenate([tops[b, span] for b in both], axis=1)
        top = jnp.maximum(old, jnp.max(s, axis=0, keepdims=True))
        shrink = jnp.exp(old - top)
        p = jnp.exp(s - top)
        total = jnp.concatenate([sums[b, span] for b in both], axis=1) * shrink
        total = total + jnp.sum(p, axis=0, keepdims=True)
        weights.append((p.astype(BF16), shrink, 1.0 / total))
    for pair in range(pairs):
        fetches[pair].wait()
    for (pair, half), (p, shrink, inverse) in zip(cells, weights):
        span = slice(half * rows, (half + 1) * rows)
        cols = slice(pair * step, (pair + 1) * step)
        o = lax.dot_general(halos[half][wide:, cols], p, TN, preferred_element_type=F32)
        for side in range(2):
            at = slice(side * rows, (side + 1) * rows)
            base = pair * step + side * HD
            value = acc[base : base + HD, span] * shrink[:, at]
            value = value + o[side * HD : (side + 1) * HD, at]
            att[base : base + HD, span] = (value * inverse[:, at]).astype(BF16)
    fetches[pairs].wait()
    fetches[pairs + 1].wait()
    for half in range(2):
        span = slice(half * rows, (half + 1) * rows)
        res = x[span, :].astype(F32)
        res = res + lax.dot_general(att[:, span], w[...], TN, preferred_element_type=F32)
        res = res.astype(BF16)
        resid[span, :] = res
        res = res.astype(F32)
        square = jnp.mean(res * res, axis=1, keepdims=True)
        normed = (res * lax.rsqrt(square + 1e-06) * gain[...]).astype(BF16)
        start = half * payload.shape[0] // 2
        payload[start : start + rows, :] = normed
        if meta is not None:
            payload[start + rows : start + rows + META, :] = jnp.broadcast_to(
                meta[half : half + 1, :], (META, meta.shape[1])
            )


def edge(live, q, before, behind, acc, tops, sums, x, w, gain, meta):
    rows, model = q.shape[0] // 2, q.shape[1]
    wide = before.shape[0] // 2
    args = [live, q, before, behind, tops, sums, gain, acc, x, w]
    args += [] if meta is None else [meta]
    specs = [SMEM] + [VMEM] * 6 + [ANY] * 3 + ([] if meta is None else [VMEM])
    extra = 0 if meta is None else META
    flat = [
        jax.ShapeDtypeStruct((2 * rows, model), BF16),
        jax.ShapeDtypeStruct((2 * (rows + extra), model), BF16),
    ]
    return pl.pallas_call(
        edge_kernel,
        in_specs=specs,
        out_specs=[VMEM] * 2,
        out_shape=[pltpu.HBM(o.shape, o.dtype) for o in flat],
        scratch_shapes=[
            pltpu.VMEM((2, wide, 2 * rows), F32),
            pltpu.VMEM((model, 2 * rows), BF16),
            pltpu.VMEM(acc.shape, acc.dtype),
            pltpu.VMEM(x.shape, x.dtype),
            pltpu.VMEM(w.shape, w.dtype),
            pltpu.SemaphoreType.DMA((HEADS // 2 + 2,)),
        ],
        compiler_params=pltpu.CompilerParams(vmem_limit_bytes=12 * MIB),
        cost_estimate=cost(
            LONG * (8 * rows * wide * model + 4 * rows * model * model), 2 * HEADS * rows * wide, args, flat
        ),
        name="edge",
    )(*args)


def meta_items(payload, block, rows):
    base = block * (rows + META) + rows
    meta = payload[base : base + META, :].astype(F32)
    return [meta[:, i * rows : (i + 1) * rows] for i in range(8)]


def slot_rows(hits):
    rows = hits.shape[1]
    upper = lax.broadcasted_iota(jnp.int32, (rows, rows), 0) < lax.broadcasted_iota(
        jnp.int32, (rows, rows), 1
    )
    upper = jnp.where(upper, F32(1.0), F32(0.0)).astype(BF16)
    rank = jnp.dot(hits.astype(BF16), upper, preferred_element_type=F32)
    return jnp.where(hits > 0, rank, F32(-1.0))


def pick_matrices(payload, block, rows, capacity, wanted):
    item = meta_items(payload, block, rows)
    named = [(item[0] == e, item[1] == e) for e in wanted]
    ranks = slot_rows(
        jnp.concatenate([jnp.where(a | b, F32(1.0), F32(0.0)) for a, b in named], axis=0)
    )
    slot = lax.broadcasted_iota(jnp.int32, (capacity, rows), 0).astype(F32)
    result = []
    for i, (a, b) in enumerate(named):
        gate = jnp.where(a, item[2] + item[3] + item[4], F32(0.0))
        gate = gate + jnp.where(b, item[5] + item[6] + item[7], F32(0.0))
        result.append((slot == ranks[i * META : i * META + 1, :], gate[:1, :]))
    return result


def experts_kernel(order, rows, capacity, me, *refs):
    payloads = refs[:-8]
    w_gate, w_up, w_down, out_mine, out_sib, x, hidden, tail = refs[-8:]
    width, model, step = w_gate.shape[1], w_down.shape[1], 256
    expert = me[0].astype(F32)
    groups = len(order) // 2
    hits = []
    for array, block in order:
        item = meta_items(payloads[array], block, rows)
        hits.append(jnp.where((item[0] == expert) | (item[1] == expert), F32(1.0), F32(0.0)))
    ranks = slot_rows(jnp.concatenate(hits, axis=0))
    slot = lax.broadcasted_iota(jnp.int32, (2 * capacity, rows), 0).astype(F32)
    for g in range(groups):
        first = ranks[2 * g * META : 2 * g * META + 1, :]
        second = ranks[(2 * g + 1) * META : (2 * g + 1) * META + 1, :]
        second = jnp.where(second >= 0, second + capacity, F32(-1.0))
        hot = jnp.concatenate([slot == first, slot == second], axis=1)
        hot = jnp.where(hot, F32(1.0), F32(0.0)).astype(BF16)
        tokens = []
        for array, block in order[2 * g : 2 * g + 2]:
            base = block * (rows + META)
            tokens.append(payloads[array][base : base + rows, :])
        picked = jnp.dot(hot, jnp.concatenate(tokens, axis=0), preferred_element_type=F32)
        x[2 * g * capacity : (2 * g + 2) * capacity, :] = picked.astype(BF16)
    for at in range(0, width, step):
        wide = min(step, width - at)
        cols = slice(at, at + wide)
        if wide < step:
            tail[:, :wide] = w_gate[:, cols]
            tail[:, wide : 2 * wide] = w_up[:, cols]
            both = jnp.dot(x[...], tail[...], preferred_element_type=F32)
            g, u = both[:, :wide], both[:, wide:]
        else:
            g = jnp.dot(x[...], w_gate[:, cols], preferred_element_type=F32)
            u = jnp.dot(x[...], w_up[:, cols], preferred_element_type=F32)
        hidden[:, cols] = (g / (1.0 + jnp.exp(-g)) * u).astype(BF16)
    for at in range(0, model, step):
        cols = slice(at, at + step)
        o = jnp.dot(hidden[...], w_down[:, cols], preferred_element_type=F32).astype(BF16)
        for g in range(groups):
            span = slice(g * capacity, (g + 1) * capacity)
            out_mine[span, cols] = o[2 * g * capacity : (2 * g + 1) * capacity]
            out_sib[span, cols] = o[(2 * g + 1) * capacity : (2 * g + 2) * capacity]


def experts(me, payloads, order, weights, rows, capacity):
    model, width = weights[0].shape
    slots = len(order) * capacity
    left = width % 256
    outs = [jax.ShapeDtypeStruct((slots // 2, model), BF16)] * 2
    args = [me, *payloads, *weights]
    return pl.pallas_call(
        functools.partial(experts_kernel, order, rows, capacity),
        in_specs=[SMEM] + [VMEM] * (len(args) - 1),
        out_specs=[VMEM] * 2,
        out_shape=outs,
        scratch_shapes=[
            pltpu.VMEM((slots, model), BF16),
            pltpu.VMEM((slots, width), BF16),
            pltpu.VMEM((model, max(2 * left, 256)), BF16),
        ],
        compiler_params=pltpu.CompilerParams(vmem_limit_bytes=12 * MIB),
        cost_estimate=cost(6 * slots * model * width, slots * width, args, outs),
        name=f"experts_{slots}",
    )(*args)


def spread(payload, block, rows, capacity, experts_two, outs_two):
    weights, values = [], []
    picks = pick_matrices(payload, block, rows, capacity, experts_two)
    for (hot, gate), out in zip(picks, outs_two):
        full = jnp.where(hot, gate, F32(0.0))
        high = full.astype(BF16)
        weights += [high, (full - high.astype(F32)).astype(BF16)]
        values += [out, out]
    return lax.dot_general(
        jnp.concatenate(weights, axis=0),
        jnp.concatenate(values, axis=0),
        (((0,), (0,)), ((), ())),
        preferred_element_type=F32,
    )


def combine_kernel(rows, capacity, me, payload, outs_me, outs_sib, *refs):
    result = refs[-1]
    both = (me[0].astype(F32), me[1].astype(F32))
    for block in range(payload.shape[0] // (rows + META)):
        span = slice(block * capacity, (block + 1) * capacity)
        total = spread(payload, block, rows, capacity, both, (outs_me[span, :], outs_sib[span, :]))
        at = slice(block * rows, (block + 1) * rows)
        if len(refs) == 2:
            total = total + refs[0][at, :].astype(F32)
        result[at, :] = total.astype(BF16)


def combine(me, payload, outs_me, outs_sib, carry, rows, capacity):
    blocks, model = payload.shape[0] // (rows + META), payload.shape[1]
    args = [me, payload, outs_me, outs_sib] + ([] if carry is None else [carry])
    outs = [jax.ShapeDtypeStruct((blocks * rows, model), BF16)]
    return pl.pallas_call(
        functools.partial(combine_kernel, rows, capacity),
        in_specs=[SMEM] + [VMEM] * (len(args) - 1),
        out_specs=VMEM,
        out_shape=outs[0],
        compiler_params=pltpu.CompilerParams(vmem_limit_bytes=12 * MIB),
        cost_estimate=cost(8 * blocks * rows * capacity * model, 0, args, outs),
        name="combine",
    )(*args)


def base_kernel(rows, capacity, me, payload, resid, outs_me, outs_sib, result):
    both = (me[0].astype(F32), me[1].astype(F32))
    for block in range(payload.shape[0] // (rows + META)):
        span = slice(block * capacity, (block + 1) * capacity)
        total = spread(payload, block, rows, capacity, both, (outs_me[span, :], outs_sib[span, :]))
        at = slice(block * rows, (block + 1) * rows)
        result[at, :] = total + resid[at, :].astype(F32)


def base(me, payload, resid, outs_me, outs_sib, rows, capacity):
    args = [me, payload, resid, outs_me, outs_sib]
    out = jax.ShapeDtypeStruct(resid.shape, F32)
    return pl.pallas_call(
        functools.partial(base_kernel, rows, capacity),
        in_specs=[SMEM] + [VMEM] * 4,
        out_specs=VMEM,
        out_shape=out,
        compiler_params=pltpu.CompilerParams(vmem_limit_bytes=12 * MIB),
        cost_estimate=cost(8 * resid.size * capacity, 0, args, [out]),
        name="base",
    )(*args)


def finish_kernel(total, first, second, out):
    out[...] = (total[...] + first[...].astype(F32) + second[...].astype(F32)).astype(BF16)


def finish(total, first, second):
    args = [total, first, second]
    return pl.pallas_call(
        finish_kernel,
        in_specs=[VMEM] * 3,
        out_specs=VMEM,
        out_shape=jax.ShapeDtypeStruct(first.shape, first.dtype),
        compiler_params=pltpu.CompilerParams(vmem_limit_bytes=12 * MIB),
        cost_estimate=cost(3 * total.size, 0, args, args[1:2]),
        name="finish",
    )(*args)


def expert_rows(token_rows, gate_mat, up_mat, down_mat):
    gate_part = jnp.dot(token_rows, gate_mat, preferred_element_type=F32)
    up_part = jnp.dot(token_rows, up_mat, preferred_element_type=F32)
    hidden = (jax.nn.silu(gate_part) * up_part).astype(BF16)
    return jnp.dot(hidden, down_mat, preferred_element_type=F32).astype(BF16)


def slot_ranks(routes, experts_count, block_rows):
    row_count = routes.shape[0]
    expert_ids = jnp.arange(experts_count, dtype=jnp.int32)
    matches = routes[:, :, None] == expert_ids[None, None, :]
    hits = jnp.sum(matches.astype(jnp.int32), axis=1)
    hits = hits.reshape(row_count // block_rows, block_rows, experts_count)
    earlier = (jnp.cumsum(hits, axis=1) - hits).reshape(row_count, experts_count)
    return jnp.sum(jnp.where(matches, earlier[:, None, :], 0), axis=-1)


def routed_all_to_all(normed, resid, routes, route_gates, w_gate, w_up, w_down):
    tiles = lax.axis_size("tile")
    row_count, route_width = routes.shape
    block_rows, model = row_count // 2, normed.shape[1]
    capacity = row_count * route_width // tiles
    slot_rank = slot_ranks(routes, tiles, block_rows)
    pieces = []
    for index in range(2):
        rows = slice(index * block_rows, (index + 1) * block_rows)
        part_normed = normed[rows]
        positions = routes[rows] * capacity + slot_rank[rows]
        copies = jnp.broadcast_to(
            part_normed[:, None, :], (block_rows, route_width, model)
        ).reshape(-1, model)
        outgoing = jnp.zeros((tiles * capacity, model), BF16).at[positions.reshape(-1)].set(copies)
        outgoing = outgoing.reshape(tiles, capacity, model)
        received = lax.all_to_all(outgoing, "tile", split_axis=0, concat_axis=0, tiled=True)
        produced = expert_rows(received.reshape(-1, model), w_gate, w_up, w_down)
        produced = produced.reshape(received.shape)
        returned = lax.all_to_all(produced, "tile", split_axis=0, concat_axis=0, tiled=True)
        picked = returned.reshape(-1, model)[positions].astype(F32)
        combined = jnp.sum(route_gates[rows][:, :, None] * picked, axis=1)
        pieces.append((resid[rows].astype(F32) + combined).astype(BF16))
    return jnp.concatenate(pieces, axis=0)


def swap(array, bit):
    return lax.ppermute(array, "tile", [(i, i ^ bit) for i in range(8)])


def swap_by_core(array, bits):
    return lax.ppermute(array, "tile", [(i, i ^ bits[i % 2]) for i in range(8)])


def after(first, *later):
    return lax.optimization_barrier((first, *later))[1:]


def routed_gather(me, payload, resid, weights, rows, capacity):
    sizes = dict(rows=rows, capacity=capacity)

    def evaluate(mine, theirs):
        order = [(0, 0), (1, 0), (0, 1), (1, 1)]
        kept, sent = experts(me, (mine, theirs), order, weights, **sizes)
        return kept, swap(sent, 1)

    sib = swap(payload, 1)
    first = swap_by_core(payload, (2, 4))
    out_own = evaluate(payload, sib)
    (first,) = after(out_own[0], first)
    diag = swap_by_core(first, (4, 2))
    out_first = evaluate(first, swap(first, 1))
    (diag,) = after(out_first[0], diag)
    second = swap_by_core(*after(diag, payload), (4, 2))
    out_diag = evaluate(diag, swap(diag, 1))
    sum_diag = combine(me, diag, *out_diag, None, **sizes)
    carry = swap_by_core(sum_diag, (4, 2))
    (second,) = after(sum_diag, second)
    out_second = evaluate(second, swap(second, 1))
    sum_second = combine(me, second, *out_second, None, **sizes)
    back_second = swap_by_core(sum_second, (4, 2))
    sum_first = combine(me, first, *out_first, *after(sum_second, carry), **sizes)
    back_first = swap_by_core(sum_first, (2, 4))
    total = base(me, payload, resid, *after(sum_first, *out_own), **sizes)
    return finish(total, back_first, back_second)


def local(
    inputs,
    queries,
    key_vectors,
    values,
    out_weight,
    norm_gain,
    routes,
    route_gates,
    w_gate,
    w_up,
    w_down,
):
    row_count = inputs.shape[0]
    tiles = lax.axis_size("tile")
    tile = lax.axis_index("tile")
    width = R_IL * PLANE
    rows = row_count // 2
    capacity = row_count * routes.shape[1] // tiles
    up = [(i, i + 1) for i in range(tiles - 1)]
    down = [(j, i) for i, j in up]
    live = jnp.stack([tile > 0, tile < tiles - 1]).astype(jnp.int32)
    me = jnp.stack([tile, tile ^ 1]).astype(jnp.int32)
    live, me, key_vectors = lax.optimization_barrier((live, me, key_vectors))
    last, first = pack(key_vectors, values, width)
    before = lax.ppermute(last, "tile", up)
    behind = lax.ppermute(first, "tile", down)
    fast = tiles == 8
    meta = None
    if fast:
        items = [routes[:, 0].astype(F32), routes[:, 1].astype(F32)]
        for k in range(2):
            gate = route_gates[:, k]
            high = lax.reduce_precision(gate, 8, 7)
            mid = lax.reduce_precision(gate - high, 8, 7)
            items += [high, mid, gate - high - mid]
        meta = jnp.stack(items).reshape(len(items), 2, rows).swapaxes(0, 1)
        meta = meta.reshape(2, len(items) * rows).astype(BF16)
    acc, tops, sums = interior(queries, key_vectors, values)
    resid, payload = edge(
        live, queries, before, behind, acc, tops, sums, inputs, out_weight,
        norm_gain[None, :], meta,
    )
    if fast:
        weights = (w_gate[0], w_up[0], w_down[0])
        return routed_gather(me, payload, resid, weights, rows, capacity)
    return routed_all_to_all(payload, resid, routes, route_gates, w_gate[0], w_up[0], w_down[0])


def solution(mesh):
    return jax.shard_map(
        local,
        mesh=mesh,
        in_specs=(
            P(("rep", "tile"), None),
            P(("rep", "tile"), None),
            P(("rep", "tile"), None),
            P(("rep", "tile"), None),
            P(),
            P(),
            P(("rep", "tile"), None),
            P(("rep", "tile"), None),
            P("tile", None, None),
            P("tile", None, None),
            P("tile", None, None),
        ),
        out_specs=P(("rep", "tile"), None),
        check_vma=False,
    )
```

```python
import functools

import jax
import jax.numpy as jnp
from jax import lax
from jax.experimental import pallas as pl
from jax.experimental.pallas import tpu as pltpu
from jax.sharding import PartitionSpec as P

HEADS = 16
HD = 64
IL_DEV = 4
XL = 8
DP = 8
R_IL = 2
R_XL = 2
R_DP = 2
PLANE = XL * DP
META = 16
MIB = 1024 * 1024
LONG = 30
F32 = jnp.float32
BF16 = jnp.bfloat16
VMEM = pl.BlockSpec(memory_space=pltpu.VMEM)
SMEM = pl.BlockSpec(memory_space=pltpu.SMEM)
ANY = pl.BlockSpec(memory_space=pl.ANY)


def far(array):
    return pltpu.with_memory_space_constraint(array, pltpu.HBM)


def cost(flops, transcendentals, args, outs):
    moved = sum(a.size * a.dtype.itemsize for a in args)
    moved += sum(o.size * o.dtype.itemsize for o in outs)
    return pl.CostEstimate(flops=flops, transcendentals=transcendentals, bytes_accessed=moved)


NT = (((1,), (1,)), ((), ()))
TN = (((0,), (0,)), ((), ()))


def window_bias(keys, first_key, queries, first_query, live):
    k = lax.broadcasted_iota(jnp.int32, (keys, queries), 0) + (first_key + PLANE * R_IL)
    q = lax.broadcasted_iota(jnp.int32, (keys, queries), 1) + first_query
    near = jnp.abs(q // PLANE + R_IL - k // PLANE) <= R_IL
    near = near & (jnp.abs(q // DP % XL - k // DP % XL) <= R_XL)
    near = near & (jnp.abs(q % DP - k % DP) <= R_DP)
    if live is not None:
        near = near & (live > 0)
    bias = jnp.where(near, F32(0.0), F32(-1e30))
    return jnp.concatenate([bias, bias], axis=1)


def two_heads(query):
    lane = lax.broadcasted_iota(jnp.int32, query.shape, 1)
    query = query * BF16(1.0 / HD**0.5)
    zero = BF16(0.0)
    return jnp.concatenate(
        [jnp.where(lane < HD, query, zero), jnp.where(lane >= HD, query, zero)], axis=0
    )


def pack_kernel(width, k, v, last, first, sems):
    end = k.shape[0] - width
    copies = [
        (k.at[pl.ds(end, width)], last.at[pl.ds(0, width)]),
        (v.at[pl.ds(end, width)], last.at[pl.ds(width, width)]),
        (k.at[pl.ds(0, width)], first.at[pl.ds(0, width)]),
        (v.at[pl.ds(0, width)], first.at[pl.ds(width, width)]),
    ]
    copies = [pltpu.make_async_copy(a, b, sems.at[i]) for i, (a, b) in enumerate(copies)]
    for copy in copies:
        copy.start()
    for copy in copies:
        copy.wait()


def pack(k, v, width):
    flat = [jax.ShapeDtypeStruct((2 * width, k.shape[1]), k.dtype)] * 2
    return pl.pallas_call(
        functools.partial(pack_kernel, width),
        in_specs=[ANY] * 2,
        out_specs=[VMEM] * 2,
        out_shape=flat,
        scratch_shapes=[pltpu.SemaphoreType.DMA((4,))],
        compiler_params=pltpu.CompilerParams(vmem_limit_bytes=12 * MIB),
        cost_estimate=cost(0, 0, flat, flat),
        name="pack",
    )(*[far(a) for a in (k, v)])


def interior_kernel(q, k, v, acc, tops, sums, bias):
    rows = q.shape[0]
    bias[...] = window_bias(rows, 0, rows, 0, None)
    for pair in range(HEADS // 2):
        cols = slice(pair * 2 * HD, (pair + 1) * 2 * HD)
        s = lax.dot_general(k[:, cols], two_heads(q[:, cols]), NT, preferred_element_type=F32)
        s = s + bias[...]
        top = jnp.max(s, axis=0, keepdims=True)
        p = jnp.exp(s - top)
        total = jnp.sum(p, axis=0, keepdims=True)
        o = lax.dot_general(v[:, cols], p.astype(BF16), TN, preferred_element_type=F32)
        base = pair * 2 * HD
        acc[base : base + HD, :] = o[:HD, :rows]
        acc[base + HD : base + 2 * HD, :] = o[HD:, rows:]
        for side in range(2):
            span = slice(side * rows, (side + 1) * rows)
            tops[2 * pair + side : 2 * pair + side + 1, :] = top[:, span]
            sums[2 * pair + side : 2 * pair + side + 1, :] = total[:, span]


def interior(q, k, v):
    rows, model = q.shape
    flat = [jax.ShapeDtypeStruct(shape, F32) for shape in ((model, rows), (HEADS, rows), (HEADS, rows))]
    args = [far(a) for a in (q, k, v)]
    return pl.pallas_call(
        interior_kernel,
        in_specs=[VMEM] * 3,
        out_specs=[VMEM] * 3,
        out_shape=flat,
        scratch_shapes=[pltpu.VMEM((rows, 2 * rows), F32)],
        compiler_params=pltpu.CompilerParams(vmem_limit_bytes=12 * MIB),
        cost_estimate=cost(LONG * 4 * rows * rows * model, HEADS * rows * rows, args, flat),
        name="interior",
    )(*args)


def edge_kernel(live, q, before, behind, tops, sums, gain, acc, x, w, *rest):
    meta = rest[0] if len(rest) == 5 else None
    resid, payload = rest[-4:-2]
    bias, att = rest[-2:]
    step = 2 * HD
    pairs = HEADS // 2
    rows = q.shape[0] // 2
    wide = before.shape[0] // 2
    halos = (before, behind)
    for half in range(2):
        first = -wide if half == 0 else 2 * rows
        bias[half] = window_bias(wide, first, rows, half * rows, live[half])
    cells = [(pair, half) for pair in range(pairs) for half in range(2)]
    scores = []
    for pair, half in cells:
        cols = slice(pair * step, (pair + 1) * step)
        queries = two_heads(q[half * rows : (half + 1) * rows, cols])
        s = lax.dot_general(halos[half][:wide, cols], queries, NT, preferred_element_type=F32)
        scores.append(s + bias[half])
    weights = []
    for (pair, half), s in zip(cells, scores):
        span = slice(half * rows, (half + 1) * rows)
        both = [slice(2 * pair + side, 2 * pair + side + 1) for side in range(2)]
        old = jnp.concatenate([tops[b, span] for b in both], axis=1)
        top = jnp.maximum(old, jnp.max(s, axis=0, keepdims=True))
        shrink = jnp.exp(old - top)
        p = jnp.exp(s - top)
        total = jnp.concatenate([sums[b, span] for b in both], axis=1) * shrink
        total = total + jnp.sum(p, axis=0, keepdims=True)
        weights.append((p.astype(BF16), shrink, 1.0 / total))
    for (pair, half), (p, shrink, inverse) in zip(cells, weights):
        span = slice(half * rows, (half + 1) * rows)
        cols = slice(pair * step, (pair + 1) * step)
        o = lax.dot_general(halos[half][wide:, cols], p, TN, preferred_element_type=F32)
        for side in range(2):
            at = slice(side * rows, (side + 1) * rows)
            base = pair * step + side * HD
            value = acc[base : base + HD, span] * shrink[:, at]
            value = value + o[side * HD : (side + 1) * HD, at]
            att[base : base + HD, span] = (value * inverse[:, at]).astype(BF16)
    for half in range(2):
        span = slice(half * rows, (half + 1) * rows)
        res = x[span, :].astype(F32)
        res = res + lax.dot_general(att[:, span], w[...], TN, preferred_element_type=F32)
        res = res.astype(BF16)
        resid[span, :] = res
        res = res.astype(F32)
        square = jnp.mean(res * res, axis=1, keepdims=True)
        normed = (res * lax.rsqrt(square + 1e-06) * gain[...]).astype(BF16)
        payload[span, :] = normed
    if meta is not None:
        copies = [
            jnp.broadcast_to(meta[half : half + 1, :], (META // 2, meta.shape[1]))
            for half in range(2)
        ]
        payload[2 * rows :, :] = jnp.concatenate(copies, axis=0)


def edge(live, q, before, behind, acc, tops, sums, x, w, gain, meta):
    rows, model = q.shape[0] // 2, q.shape[1]
    wide = before.shape[0] // 2
    args = [live, q, before, behind, tops, sums, gain, acc, x, w]
    args += [] if meta is None else [meta]
    specs = [SMEM] + [VMEM] * 9 + ([] if meta is None else [VMEM])
    extra = 0 if meta is None else META
    flat = [
        jax.ShapeDtypeStruct((2 * rows, model), BF16),
        jax.ShapeDtypeStruct((2 * rows + extra, model), BF16),
    ]
    return pl.pallas_call(
        edge_kernel,
        in_specs=specs,
        out_specs=[VMEM] * 2,
        out_shape=flat,
        scratch_shapes=[
            pltpu.VMEM((2, wide, 2 * rows), F32),
            pltpu.VMEM((model, 2 * rows), BF16),
        ],
        compiler_params=pltpu.CompilerParams(vmem_limit_bytes=12 * MIB),
        cost_estimate=cost(
            LONG * (8 * rows * wide * model + 4 * rows * model * model), 2 * HEADS * rows * wide, args, flat
        ),
        name="edge",
    )(*args)


def meta_items(payload, block, rows):
    meta = payload[2 * rows :, :].astype(F32)
    meta = meta[block * META // 2 : (block + 1) * META // 2, :]
    return [meta[:, i * rows : (i + 1) * rows] for i in range(8)]


def slot_rows(hits):
    rows = hits.shape[1]
    upper = lax.broadcasted_iota(jnp.int32, (rows, rows), 0) < lax.broadcasted_iota(
        jnp.int32, (rows, rows), 1
    )
    upper = jnp.where(upper, F32(1.0), F32(0.0)).astype(BF16)
    rank = jnp.dot(hits.astype(BF16), upper, preferred_element_type=F32)
    return jnp.where(hits > 0, rank, F32(-1.0))


def pick_matrices(payload, block, rows, capacity, wanted):
    item = meta_items(payload, block, rows)
    named = [(item[0] == e, item[1] == e) for e in wanted]
    ranks = slot_rows(
        jnp.concatenate([jnp.where(a | b, F32(1.0), F32(0.0)) for a, b in named], axis=0)
    )
    slot = lax.broadcasted_iota(jnp.int32, (capacity, rows), 0).astype(F32)
    result = []
    for i, (a, b) in enumerate(named):
        gate = jnp.where(a, item[2] + item[3] + item[4], F32(0.0))
        gate = gate + jnp.where(b, item[5] + item[6] + item[7], F32(0.0))
        result.append((slot == ranks[i * META // 2 : i * META // 2 + 1, :], gate[:1, :]))
    return result


def experts_kernel(order, rows, capacity, me, *refs):
    payloads = refs[:-8]
    w_gate, w_up, w_down, out_mine, out_sib, x, hidden, tail = refs[-8:]
    width, model, step = w_gate.shape[1], w_down.shape[1], 256
    expert = me[0].astype(F32)
    groups = len(order) // 2
    hits = []
    for array, block in order:
        item = meta_items(payloads[array], block, rows)
        hits.append(jnp.where((item[0] == expert) | (item[1] == expert), F32(1.0), F32(0.0)))
    ranks = slot_rows(jnp.concatenate(hits, axis=0))
    slot = lax.broadcasted_iota(jnp.int32, (2 * capacity, rows), 0).astype(F32)
    for g in range(groups):
        first = ranks[g * META : g * META + 1, :]
        second = ranks[g * META + META // 2 : g * META + META // 2 + 1, :]
        second = jnp.where(second >= 0, second + capacity, F32(-1.0))
        hot = jnp.concatenate([slot == first, slot == second], axis=1)
        hot = jnp.where(hot, F32(1.0), F32(0.0)).astype(BF16)
        tokens = []
        for array, block in order[2 * g : 2 * g + 2]:
            tokens.append(payloads[array][block * rows : (block + 1) * rows, :])
        picked = jnp.dot(hot, jnp.concatenate(tokens, axis=0), preferred_element_type=F32)
        x[2 * g * capacity : (2 * g + 2) * capacity, :] = picked.astype(BF16)
    for at in range(0, width, step):
        wide = min(step, width - at)
        cols = slice(at, at + wide)
        if wide < step:
            tail[:, :wide] = w_gate[:, cols]
            tail[:, wide : 2 * wide] = w_up[:, cols]
            both = jnp.dot(x[...], tail[...], preferred_element_type=F32)
            g, u = both[:, :wide], both[:, wide:]
        else:
            g = jnp.dot(x[...], w_gate[:, cols], preferred_element_type=F32)
            u = jnp.dot(x[...], w_up[:, cols], preferred_element_type=F32)
        hidden[:, cols] = (g / (1.0 + jnp.exp(-g)) * u).astype(BF16)
    for at in range(0, model, step):
        cols = slice(at, at + step)
        o = jnp.dot(hidden[...], w_down[:, cols], preferred_element_type=F32).astype(BF16)
        for g in range(groups):
            span = slice(g * capacity, (g + 1) * capacity)
            out_mine[span, cols] = o[2 * g * capacity : (2 * g + 1) * capacity]
            out_sib[span, cols] = o[(2 * g + 1) * capacity : (2 * g + 2) * capacity]


def experts(me, payloads, order, weights, rows, capacity):
    model, width = weights[0].shape
    slots = len(order) * capacity
    left = width % 256
    outs = [jax.ShapeDtypeStruct((slots // 2, model), BF16)] * 2
    args = [me, *payloads, *weights]
    return pl.pallas_call(
        functools.partial(experts_kernel, order, rows, capacity),
        in_specs=[SMEM] + [VMEM] * (len(args) - 1),
        out_specs=[VMEM] * 2,
        out_shape=outs,
        scratch_shapes=[
            pltpu.VMEM((slots, model), BF16),
            pltpu.VMEM((slots, width), BF16),
            pltpu.VMEM((model, max(2 * left, 256)), BF16),
        ],
        compiler_params=pltpu.CompilerParams(vmem_limit_bytes=12 * MIB),
        cost_estimate=cost(6 * slots * model * width, slots * width, args, outs),
        name=f"experts_{slots}",
    )(*args)


def spread(payload, block, rows, capacity, experts_two, outs_two):
    weights, values = [], []
    picks = pick_matrices(payload, block, rows, capacity, experts_two)
    for (hot, gate), out in zip(picks, outs_two):
        full = jnp.where(hot, gate, F32(0.0))
        high = full.astype(BF16)
        weights += [high, (full - high.astype(F32)).astype(BF16)]
        values += [out, out]
    return lax.dot_general(
        jnp.concatenate(weights, axis=0),
        jnp.concatenate(values, axis=0),
        (((0,), (0,)), ((), ())),
        preferred_element_type=F32,
    )


def combine_kernel(rows, capacity, me, payload, outs_me, outs_sib, *refs):
    result = refs[-1]
    both = (me[0].astype(F32), me[1].astype(F32))
    for block in range(2):
        span = slice(block * capacity, (block + 1) * capacity)
        total = spread(payload, block, rows, capacity, both, (outs_me[span, :], outs_sib[span, :]))
        at = slice(block * rows, (block + 1) * rows)
        if len(refs) == 2:
            total = total + refs[0][at, :].astype(F32)
        result[at, :] = total.astype(result.dtype)


def combine(me, payload, outs_me, outs_sib, rows, capacity, start=None, dtype=BF16):
    model = payload.shape[1]
    args = [me, payload, outs_me, outs_sib] + ([] if start is None else [start])
    out = jax.ShapeDtypeStruct((2 * rows, model), dtype)
    return pl.pallas_call(
        functools.partial(combine_kernel, rows, capacity),
        in_specs=[SMEM] + [VMEM] * (len(args) - 1),
        out_specs=VMEM,
        out_shape=out,
        compiler_params=pltpu.CompilerParams(vmem_limit_bytes=12 * MIB),
        cost_estimate=cost(8 * out.size * capacity, 0, args, [out]),
        name="combine",
    )(*args)


def add_kernel(a, b, result):
    result[...] = (a[...].astype(F32) + b[...].astype(F32)).astype(result.dtype)


def add(a, b, dtype):
    out = jax.ShapeDtypeStruct(a.shape, dtype)
    return pl.pallas_call(
        add_kernel,
        in_specs=[VMEM] * 2,
        out_specs=VMEM,
        out_shape=out,
        compiler_params=pltpu.CompilerParams(vmem_limit_bytes=12 * MIB),
        cost_estimate=cost(out.size, 0, (a, b), [out]),
        name="add",
    )(a, b)


def expert_rows(token_rows, gate_mat, up_mat, down_mat):
    gate_part = jnp.dot(token_rows, gate_mat, preferred_element_type=F32)
    up_part = jnp.dot(token_rows, up_mat, preferred_element_type=F32)
    hidden = (jax.nn.silu(gate_part) * up_part).astype(BF16)
    return jnp.dot(hidden, down_mat, preferred_element_type=F32).astype(BF16)


def slot_ranks(routes, experts_count, block_rows):
    row_count = routes.shape[0]
    expert_ids = jnp.arange(experts_count, dtype=jnp.int32)
    matches = routes[:, :, None] == expert_ids[None, None, :]
    hits = jnp.sum(matches.astype(jnp.int32), axis=1)
    hits = hits.reshape(row_count // block_rows, block_rows, experts_count)
    earlier = (jnp.cumsum(hits, axis=1) - hits).reshape(row_count, experts_count)
    return jnp.sum(jnp.where(matches, earlier[:, None, :], 0), axis=-1)


def routed_all_to_all(normed, resid, routes, route_gates, w_gate, w_up, w_down):
    tiles = lax.axis_size("tile")
    row_count, route_width = routes.shape
    block_rows, model = row_count // 2, normed.shape[1]
    capacity = row_count * route_width // tiles
    slot_rank = slot_ranks(routes, tiles, block_rows)
    pieces = []
    for index in range(2):
        rows = slice(index * block_rows, (index + 1) * block_rows)
        part_normed = normed[rows]
        positions = routes[rows] * capacity + slot_rank[rows]
        copies = jnp.broadcast_to(
            part_normed[:, None, :], (block_rows, route_width, model)
        ).reshape(-1, model)
        outgoing = jnp.zeros((tiles * capacity, model), BF16).at[positions.reshape(-1)].set(copies)
        outgoing = outgoing.reshape(tiles, capacity, model)
        received = lax.all_to_all(outgoing, "tile", split_axis=0, concat_axis=0, tiled=True)
        produced = expert_rows(received.reshape(-1, model), w_gate, w_up, w_down)
        produced = produced.reshape(received.shape)
        returned = lax.all_to_all(produced, "tile", split_axis=0, concat_axis=0, tiled=True)
        picked = returned.reshape(-1, model)[positions].astype(F32)
        combined = jnp.sum(route_gates[rows][:, :, None] * picked, axis=1)
        pieces.append((resid[rows].astype(F32) + combined).astype(BF16))
    return jnp.concatenate(pieces, axis=0)


def swap(array, bit):
    return lax.ppermute(array, "tile", [(i, i ^ bit) for i in range(8)])


def swap_by_core(array, bits):
    return lax.ppermute(array, "tile", [(i, i ^ bits[i % 2]) for i in range(8)])


def after(first, *later):
    return lax.optimization_barrier((first, *later))[1:]


def routed_gather(me, payload, resid, weights, rows, capacity):
    sizes = dict(rows=rows, capacity=capacity)

    def evaluate(mine, theirs):
        order = [(0, 0), (1, 0), (0, 1), (1, 1)]
        kept, sent = experts(me, (mine, theirs), order, weights, **sizes)
        return kept, swap(sent, 1)

    sib = swap(payload, 1)
    first = swap_by_core(payload, (2, 4))
    out_own = evaluate(payload, sib)
    total = combine(me, payload, *out_own, start=resid, dtype=F32, **sizes)
    (first,) = after(total, first)
    diag = swap_by_core(first, (4, 2))
    out_first = evaluate(first, swap(first, 1))
    (diag,) = after(out_first[0], diag)
    second = swap_by_core(*after(diag, payload), (4, 2))
    (diag,) = after(out_first[0], diag)
    out_diag = evaluate(diag, swap(diag, 1))
    sum_diag = combine(me, diag, *out_diag, **sizes)
    carry = swap_by_core(sum_diag, (4, 2))
    (second,) = after(sum_diag, second)
    out_second = evaluate(second, swap(second, 1))
    sum_first = combine(
        me, first, *out_first[:1], *after(out_second[0], *out_first[1:]), dtype=F32, **sizes
    )
    sum_second = combine(me, second, out_second[0], *after(sum_first, out_second[1]), **sizes)
    back_second = swap_by_core(sum_second, (4, 2))
    back_first = swap_by_core(add(sum_first, *after(sum_second, carry), BF16), (2, 4))
    return add(add(total, back_second, F32), back_first, BF16)


def local(
    inputs,
    queries,
    key_vectors,
    values,
    out_weight,
    norm_gain,
    routes,
    route_gates,
    w_gate,
    w_up,
    w_down,
):
    row_count = inputs.shape[0]
    tiles = lax.axis_size("tile")
    tile = lax.axis_index("tile")
    width = R_IL * PLANE
    rows = row_count // 2
    capacity = row_count * routes.shape[1] // tiles
    up = [(i, i + 1) for i in range(tiles - 1)]
    down = [(j, i) for i, j in up]
    live = jnp.stack([tile > 0, tile < tiles - 1]).astype(jnp.int32)
    me = jnp.stack([tile, tile ^ 1]).astype(jnp.int32)
    live, me, key_vectors = lax.optimization_barrier((live, me, key_vectors))
    last, first = pack(key_vectors, values, width)
    before = lax.ppermute(last, "tile", up)
    behind = lax.ppermute(first, "tile", down)
    fast = tiles == 8
    meta = None
    if fast:
        items = [routes[:, 0].astype(F32), routes[:, 1].astype(F32)]
        for k in range(2):
            gate = route_gates[:, k]
            high = lax.reduce_precision(gate, 8, 7)
            mid = lax.reduce_precision(gate - high, 8, 7)
            items += [high, mid, gate - high - mid]
        meta = jnp.stack(items).reshape(len(items), 2, rows).swapaxes(0, 1)
        meta = meta.reshape(2, len(items) * rows).astype(BF16)
    acc, tops, sums = interior(queries, key_vectors, values)
    resid, payload = edge(
        live, queries, before, behind, acc, tops, sums, inputs, out_weight,
        norm_gain[None, :], meta,
    )
    if fast:
        weights = (w_gate[0], w_up[0], w_down[0])
        return routed_gather(me, payload, resid, weights, rows, capacity)
    return routed_all_to_all(payload, resid, routes, route_gates, w_gate[0], w_up[0], w_down[0])


def solution(mesh):
    return jax.shard_map(
        local,
        mesh=mesh,
        in_specs=(
            P(("rep", "tile"), None),
            P(("rep", "tile"), None),
            P(("rep", "tile"), None),
            P(("rep", "tile"), None),
            P(),
            P(),
            P(("rep", "tile"), None),
            P(("rep", "tile"), None),
            P("tile", None, None),
            P("tile", None, None),
            P("tile", None, None),
        ),
        out_specs=P(("rep", "tile"), None),
        check_vma=False,
    )
```

```python
import functools

import jax
import jax.numpy as jnp
from jax import lax
from jax.experimental import pallas as pl
from jax.experimental.pallas import tpu as pltpu
from jax.sharding import PartitionSpec as P

HEADS = 16
HD = 64
IL_DEV = 4
XL = 8
DP = 8
R_IL = 2
R_XL = 2
R_DP = 2
PLANE = XL * DP
META = 16
MIB = 1024 * 1024
LONG = 30
F32 = jnp.float32
BF16 = jnp.bfloat16
VMEM = pl.BlockSpec(memory_space=pltpu.VMEM)
SMEM = pl.BlockSpec(memory_space=pltpu.SMEM)
ANY = pl.BlockSpec(memory_space=pl.ANY)


def far(array):
    return pltpu.with_memory_space_constraint(array, pltpu.HBM)


def cost(flops, transcendentals, args, outs):
    moved = sum(a.size * a.dtype.itemsize for a in args)
    moved += sum(o.size * o.dtype.itemsize for o in outs)
    return pl.CostEstimate(flops=flops, transcendentals=transcendentals, bytes_accessed=moved)


NT = (((1,), (1,)), ((), ()))
TN = (((0,), (0,)), ((), ()))


def window_bias(keys, first_key, queries, first_query, live):
    k = lax.broadcasted_iota(jnp.int32, (keys, queries), 0) + (first_key + PLANE * R_IL)
    q = lax.broadcasted_iota(jnp.int32, (keys, queries), 1) + first_query
    near = jnp.abs(q // PLANE + R_IL - k // PLANE) <= R_IL
    near = near & (jnp.abs(q // DP % XL - k // DP % XL) <= R_XL)
    near = near & (jnp.abs(q % DP - k % DP) <= R_DP)
    if live is not None:
        near = near & (live > 0)
    bias = jnp.where(near, F32(0.0), F32(-1e30))
    return jnp.concatenate([bias, bias], axis=1)


def two_heads(query):
    lane = lax.broadcasted_iota(jnp.int32, query.shape, 1)
    query = query * BF16(1.0 / HD**0.5)
    zero = BF16(0.0)
    return jnp.concatenate(
        [jnp.where(lane < HD, query, zero), jnp.where(lane >= HD, query, zero)], axis=0
    )


def pack_kernel(width, k, v, last, first, sems):
    end = k.shape[0] - width
    copies = [
        (k.at[pl.ds(end, width)], last.at[pl.ds(0, width)]),
        (v.at[pl.ds(end, width)], last.at[pl.ds(width, width)]),
        (k.at[pl.ds(0, width)], first.at[pl.ds(0, width)]),
        (v.at[pl.ds(0, width)], first.at[pl.ds(width, width)]),
    ]
    copies = [pltpu.make_async_copy(a, b, sems.at[i]) for i, (a, b) in enumerate(copies)]
    for copy in copies:
        copy.start()
    for copy in copies:
        copy.wait()


def pack(k, v, width):
    flat = [jax.ShapeDtypeStruct((2 * width, k.shape[1]), k.dtype)] * 2
    return pl.pallas_call(
        functools.partial(pack_kernel, width),
        in_specs=[ANY] * 2,
        out_specs=[VMEM] * 2,
        out_shape=flat,
        scratch_shapes=[pltpu.SemaphoreType.DMA((4,))],
        compiler_params=pltpu.CompilerParams(vmem_limit_bytes=12 * MIB),
        cost_estimate=cost(0, 0, flat, flat),
        name="pack",
    )(*[far(a) for a in (k, v)])


def interior_kernel(q, k, v, acc, tops, sums, bias):
    rows = q.shape[0]
    bias[...] = window_bias(rows, 0, rows, 0, None)
    for pair in range(HEADS // 2):
        cols = slice(pair * 2 * HD, (pair + 1) * 2 * HD)
        s = lax.dot_general(k[:, cols], two_heads(q[:, cols]), NT, preferred_element_type=F32)
        s = s + bias[...]
        top = jnp.max(s, axis=0, keepdims=True)
        p = jnp.exp(s - top)
        total = jnp.sum(p, axis=0, keepdims=True)
        o = lax.dot_general(v[:, cols], p.astype(BF16), TN, preferred_element_type=F32)
        base = pair * 2 * HD
        acc[base : base + HD, :] = o[:HD, :rows]
        acc[base + HD : base + 2 * HD, :] = o[HD:, rows:]
        for side in range(2):
            span = slice(side * rows, (side + 1) * rows)
            tops[2 * pair + side : 2 * pair + side + 1, :] = top[:, span]
            sums[2 * pair + side : 2 * pair + side + 1, :] = total[:, span]


def interior(q, k, v):
    rows, model = q.shape
    flat = [jax.ShapeDtypeStruct(shape, F32) for shape in ((model, rows), (HEADS, rows), (HEADS, rows))]
    args = [far(a) for a in (q, k, v)]
    return pl.pallas_call(
        interior_kernel,
        in_specs=[VMEM] * 3,
        out_specs=[VMEM] * 3,
        out_shape=flat,
        scratch_shapes=[pltpu.VMEM((rows, 2 * rows), F32)],
        compiler_params=pltpu.CompilerParams(vmem_limit_bytes=12 * MIB),
        cost_estimate=cost(LONG * 4 * rows * rows * model, HEADS * rows * rows, args, flat),
        name="interior",
    )(*args)


def edge_kernel(live, q, before, behind, tops, sums, gain, acc, x, w, *rest):
    meta = rest[0] if len(rest) == 7 else None
    resid, payload0, payload1, whole = rest[-6:-2]
    bias, att = rest[-2:]
    step = 2 * HD
    pairs = HEADS // 2
    rows = q.shape[0] // 2
    wide = before.shape[0] // 2
    halos = (before, behind)
    for half in range(2):
        first = -wide if half == 0 else 2 * rows
        bias[half] = window_bias(wide, first, rows, half * rows, live[half])
    cells = [(pair, half) for pair in range(pairs) for half in range(2)]
    scores = []
    for pair, half in cells:
        cols = slice(pair * step, (pair + 1) * step)
        queries = two_heads(q[half * rows : (half + 1) * rows, cols])
        s = lax.dot_general(halos[half][:wide, cols], queries, NT, preferred_element_type=F32)
        scores.append(s + bias[half])
    weights = []
    for (pair, half), s in zip(cells, scores):
        span = slice(half * rows, (half + 1) * rows)
        both = [slice(2 * pair + side, 2 * pair + side + 1) for side in range(2)]
        old = jnp.concatenate([tops[b, span] for b in both], axis=1)
        top = jnp.maximum(old, jnp.max(s, axis=0, keepdims=True))
        shrink = jnp.exp(old - top)
        p = jnp.exp(s - top)
        total = jnp.concatenate([sums[b, span] for b in both], axis=1) * shrink
        total = total + jnp.sum(p, axis=0, keepdims=True)
        weights.append((p.astype(BF16), shrink, 1.0 / total))
    for (pair, half), (p, shrink, inverse) in zip(cells, weights):
        span = slice(half * rows, (half + 1) * rows)
        cols = slice(pair * step, (pair + 1) * step)
        o = lax.dot_general(halos[half][wide:, cols], p, TN, preferred_element_type=F32)
        for side in range(2):
            at = slice(side * rows, (side + 1) * rows)
            base = pair * step + side * HD
            value = acc[base : base + HD, span] * shrink[:, at]
            value = value + o[side * HD : (side + 1) * HD, at]
            att[base : base + HD, span] = (value * inverse[:, at]).astype(BF16)
    for half in range(2):
        span = slice(half * rows, (half + 1) * rows)
        res = x[span, :].astype(F32)
        res = res + lax.dot_general(att[:, span], w[...], TN, preferred_element_type=F32)
        res = res.astype(BF16)
        resid[span, :] = res
        res = res.astype(F32)
        square = jnp.mean(res * res, axis=1, keepdims=True)
        normed = (res * lax.rsqrt(square + 1e-06) * gain[...]).astype(BF16)
        (payload0, payload1)[half][:rows, :] = normed
        whole[span, :] = normed
    if meta is not None:
        copies = [
            jnp.broadcast_to(meta[half : half + 1, :], (META // 2, meta.shape[1]))
            for half in range(2)
        ]
        payload0[rows:, :] = jnp.concatenate(copies, axis=0)
        whole[2 * rows :, :] = jnp.concatenate(copies, axis=0)


def edge(live, q, before, behind, acc, tops, sums, x, w, gain, meta):
    rows, model = q.shape[0] // 2, q.shape[1]
    wide = before.shape[0] // 2
    args = [live, q, before, behind, tops, sums, gain, acc, x, w]
    args += [] if meta is None else [meta]
    specs = [SMEM] + [VMEM] * 9 + ([] if meta is None else [VMEM])
    extra = 0 if meta is None else META
    flat = [
        jax.ShapeDtypeStruct((2 * rows, model), BF16),
        jax.ShapeDtypeStruct((rows + extra, model), BF16),
        jax.ShapeDtypeStruct((rows, model), BF16),
        jax.ShapeDtypeStruct((2 * rows + extra, model), BF16),
    ]
    return pl.pallas_call(
        edge_kernel,
        in_specs=specs,
        out_specs=[VMEM] * 4,
        out_shape=flat,
        scratch_shapes=[
            pltpu.VMEM((2, wide, 2 * rows), F32),
            pltpu.VMEM((model, 2 * rows), BF16),
        ],
        compiler_params=pltpu.CompilerParams(vmem_limit_bytes=12 * MIB),
        cost_estimate=cost(
            LONG * (8 * rows * wide * model + 4 * rows * model * model), 2 * HEADS * rows * wide, args, flat
        ),
        name="edge",
    )(*args)


def meta_items(payload, block, rows):
    meta = payload[payload.shape[0] - META :, :].astype(F32)
    meta = meta[block * META // 2 : (block + 1) * META // 2, :]
    return [meta[:, i * rows : (i + 1) * rows] for i in range(8)]


def slot_rows(hits):
    rows = hits.shape[1]
    upper = lax.broadcasted_iota(jnp.int32, (rows, rows), 0) < lax.broadcasted_iota(
        jnp.int32, (rows, rows), 1
    )
    upper = jnp.where(upper, F32(1.0), F32(0.0)).astype(BF16)
    rank = jnp.dot(hits.astype(BF16), upper, preferred_element_type=F32)
    return jnp.where(hits > 0, rank, F32(-1.0))


def experts_kernel(order, rows, capacity, me, *refs):
    payloads = refs[:-9]
    w_gate, w_up, w_down, out_mine, out_sib, scatter, x, hidden, tail = refs[-9:]
    width, model, step = w_gate.shape[1], w_down.shape[1], 256
    expert, other = me[0].astype(F32), me[1].astype(F32)
    groups = len(order) // 2
    items = [meta_items(payloads[holder], block, rows) for _, _, holder, block in order]

    def hits(item, wanted):
        return jnp.where((item[0] == wanted) | (item[1] == wanted), F32(1.0), F32(0.0))

    named = [hits(item, expert) for item in items] + [hits(item, other) for item in items[::2]]
    ranks = slot_rows(jnp.concatenate(named, axis=0))
    ranks = [ranks[i * META // 2 : i * META // 2 + 1, :] for i in range(len(named))]
    slot = lax.broadcasted_iota(jnp.int32, (2 * capacity, rows), 0).astype(F32)
    for g in range(groups):
        first, second = ranks[2 * g : 2 * g + 2]
        second = jnp.where(second >= 0, second + capacity, F32(-1.0))
        hot = jnp.concatenate([slot == first, slot == second], axis=1)
        hot = jnp.where(hot, F32(1.0), F32(0.0)).astype(BF16)
        tokens = [payloads[a][at : at + rows, :] for a, at, _, _ in order[2 * g : 2 * g + 2]]
        picked = jnp.dot(hot, jnp.concatenate(tokens, axis=0), preferred_element_type=F32)
        x[2 * g * capacity : (2 * g + 2) * capacity, :] = picked.astype(BF16)
    for g in range(groups):
        item = items[2 * g]
        for i, (wanted, rank) in enumerate(((expert, ranks[2 * g]), (other, ranks[2 * groups + g]))):
            gate = jnp.where(item[0] == wanted, item[2] + item[3] + item[4], F32(0.0))
            gate = gate + jnp.where(item[1] == wanted, item[5] + item[6] + item[7], F32(0.0))
            full = jnp.where(slot[:capacity] == rank, gate[:1, :], F32(0.0))
            high = full.astype(BF16)
            at = (4 * g + 2 * i) * capacity
            scatter[at : at + capacity, :] = high
            scatter[at + capacity : at + 2 * capacity, :] = (full - high.astype(F32)).astype(BF16)
    for at in range(0, width, step):
        wide = min(step, width - at)
        cols = slice(at, at + wide)
        if wide < step:
            tail[:, :wide] = w_gate[:, cols]
            tail[:, wide : 2 * wide] = w_up[:, cols]
            both = jnp.dot(x[...], tail[...], preferred_element_type=F32)
            g, u = both[:, :wide], both[:, wide:]
        else:
            g = jnp.dot(x[...], w_gate[:, cols], preferred_element_type=F32)
            u = jnp.dot(x[...], w_up[:, cols], preferred_element_type=F32)
        hidden[:, cols] = (g / (1.0 + jnp.exp(-g)) * u).astype(BF16)
    for at in range(0, model, step):
        cols = slice(at, at + step)
        o = jnp.dot(hidden[...], w_down[:, cols], preferred_element_type=F32).astype(BF16)
        for g in range(groups):
            span = slice(g * capacity, (g + 1) * capacity)
            out_mine[span, cols] = o[2 * g * capacity : (2 * g + 1) * capacity]
            out_sib[span, cols] = o[(2 * g + 1) * capacity : (2 * g + 2) * capacity]


def experts(me, payloads, order, weights, rows, capacity):
    model, width = weights[0].shape
    slots = len(order) * capacity
    left = width % 256
    outs = [jax.ShapeDtypeStruct((slots // 2, model), BF16)] * 2
    outs.append(jax.ShapeDtypeStruct((2 * slots, rows), BF16))
    args = [me, *payloads, *weights]
    return pl.pallas_call(
        functools.partial(experts_kernel, order, rows, capacity),
        in_specs=[SMEM] + [VMEM] * (len(args) - 1),
        out_specs=[VMEM] * 3,
        out_shape=outs,
        scratch_shapes=[
            pltpu.VMEM((slots, model), BF16),
            pltpu.VMEM((slots, width), BF16),
            pltpu.VMEM((model, max(2 * left, 256)), BF16),
        ],
        compiler_params=pltpu.CompilerParams(vmem_limit_bytes=12 * MIB),
        cost_estimate=cost(6 * slots * model * width, slots * width, args, outs),
        name=f"experts_{slots}",
    )(*args)


def combine_kernel(rows, capacity, parts, *refs):
    scatters, outs_me, outs_sib = refs[:parts], refs[parts : 2 * parts], refs[2 * parts : 3 * parts]
    refs = refs[3 * parts :]
    result = refs[-1]
    for block in range(2):
        part, at = (block, 0) if parts == 2 else (0, block)
        gates = scatters[part][4 * at * capacity : 4 * (at + 1) * capacity, :]
        span = slice(at * capacity, (at + 1) * capacity)
        mine, theirs = outs_me[part][span, :], outs_sib[part][span, :]
        values = jnp.concatenate([mine, mine, theirs, theirs], axis=0)
        total = lax.dot_general(gates, values, TN, preferred_element_type=F32)
        at = slice(block * rows, (block + 1) * rows)
        if len(refs) == 2:
            total = total + refs[0][at, :].astype(F32)
        result[at, :] = total.astype(result.dtype)


def combine(scatters, outs_me, outs_sib, rows, capacity, start=None, dtype=BF16):
    model = outs_me[0].shape[1]
    args = [*scatters, *outs_me, *outs_sib] + ([] if start is None else [start])
    out = jax.ShapeDtypeStruct((2 * rows, model), dtype)
    return pl.pallas_call(
        functools.partial(combine_kernel, rows, capacity, len(outs_me)),
        in_specs=[VMEM] * len(args),
        out_specs=VMEM,
        out_shape=out,
        compiler_params=pltpu.CompilerParams(vmem_limit_bytes=12 * MIB),
        cost_estimate=cost(8 * out.size * capacity, 0, args, [out]),
        name="combine",
    )(*args)


def add_kernel(a, b, result):
    result[...] = (a[...].astype(F32) + b[...].astype(F32)).astype(result.dtype)


def add(a, b, dtype):
    out = jax.ShapeDtypeStruct(a.shape, dtype)
    return pl.pallas_call(
        add_kernel,
        in_specs=[VMEM] * 2,
        out_specs=VMEM,
        out_shape=out,
        compiler_params=pltpu.CompilerParams(vmem_limit_bytes=12 * MIB),
        cost_estimate=cost(out.size, 0, (a, b), [out]),
        name="add",
    )(a, b)


def expert_rows(token_rows, gate_mat, up_mat, down_mat):
    gate_part = jnp.dot(token_rows, gate_mat, preferred_element_type=F32)
    up_part = jnp.dot(token_rows, up_mat, preferred_element_type=F32)
    hidden = (jax.nn.silu(gate_part) * up_part).astype(BF16)
    return jnp.dot(hidden, down_mat, preferred_element_type=F32).astype(BF16)


def slot_ranks(routes, experts_count, block_rows):
    row_count = routes.shape[0]
    expert_ids = jnp.arange(experts_count, dtype=jnp.int32)
    matches = routes[:, :, None] == expert_ids[None, None, :]
    hits = jnp.sum(matches.astype(jnp.int32), axis=1)
    hits = hits.reshape(row_count // block_rows, block_rows, experts_count)
    earlier = (jnp.cumsum(hits, axis=1) - hits).reshape(row_count, experts_count)
    return jnp.sum(jnp.where(matches, earlier[:, None, :], 0), axis=-1)


def routed_all_to_all(normed, resid, routes, route_gates, w_gate, w_up, w_down):
    tiles = lax.axis_size("tile")
    row_count, route_width = routes.shape
    block_rows, model = row_count // 2, normed.shape[1]
    capacity = row_count * route_width // tiles
    slot_rank = slot_ranks(routes, tiles, block_rows)
    pieces = []
    for index in range(2):
        rows = slice(index * block_rows, (index + 1) * block_rows)
        part_normed = normed[rows]
        positions = routes[rows] * capacity + slot_rank[rows]
        copies = jnp.broadcast_to(
            part_normed[:, None, :], (block_rows, route_width, model)
        ).reshape(-1, model)
        outgoing = jnp.zeros((tiles * capacity, model), BF16).at[positions.reshape(-1)].set(copies)
        outgoing = outgoing.reshape(tiles, capacity, model)
        received = lax.all_to_all(outgoing, "tile", split_axis=0, concat_axis=0, tiled=True)
        produced = expert_rows(received.reshape(-1, model), w_gate, w_up, w_down)
        produced = produced.reshape(received.shape)
        returned = lax.all_to_all(produced, "tile", split_axis=0, concat_axis=0, tiled=True)
        picked = returned.reshape(-1, model)[positions].astype(F32)
        combined = jnp.sum(route_gates[rows][:, :, None] * picked, axis=1)
        pieces.append((resid[rows].astype(F32) + combined).astype(BF16))
    return jnp.concatenate(pieces, axis=0)


def swap(array, bit):
    return lax.ppermute(array, "tile", [(i, i ^ bit) for i in range(8)])


def swap_by_core(array, bits):
    return lax.ppermute(array, "tile", [(i, i ^ bits[i % 2]) for i in range(8)])


def after(first, *later):
    return lax.optimization_barrier((first, *later))[1:]


def routed_gather(me, payloads, whole, resid, weights, rows, capacity):
    sizes = dict(rows=rows, capacity=capacity)

    def evaluate(mine, theirs):
        count = len(mine)
        order = []
        for block in range(2):
            array, at = (block, 0) if count == 2 else (0, block * rows)
            order += [(array, at, 0, block), (count + array, at, count, block)]
        kept, sent, scatter = experts(me, (*mine, *theirs), order, weights, **sizes)
        return (scatter,), (kept,), (swap(sent, 1),)

    def siblings(arrays):
        return [swap(a, 1) for a in arrays]

    first = [swap_by_core(p, (2, 4)) for p in payloads]
    sib = siblings(payloads)
    order = [(0, 0, 0, 0), (1, 0, 1, 0)]
    own0, sent0, scatter0 = experts(me, (payloads[0], sib[0]), order, weights, **sizes)
    (first[0],) = after(own0, first[0])
    diag0 = swap_by_core(first[0], (4, 2))
    later = after(first[0], payloads[1], sib[1])
    order = [(0, 0, 2, 1), (1, 0, 3, 1)]
    own1, sent1, scatter1 = experts(me, (*later, payloads[0], sib[0]), order, weights, **sizes)
    (first[1],) = after(own1, first[1])
    diag1 = swap_by_core(first[1], (4, 2))
    far = siblings(first)
    first[0], _ = lax.optimization_barrier((first[0], diag0))
    out_first = evaluate(first, far)
    (diag1,) = after(out_first[1][0], diag1)
    second = swap_by_core(*after(diag1, whole), (4, 2))
    diag = [diag0, diag1]
    out_diag = evaluate(diag, siblings(diag))
    sum_diag = combine(*out_diag, **sizes)
    carry = swap_by_core(sum_diag, (4, 2))
    (second,) = after(sum_diag, second)
    out_second = evaluate([second], siblings([second]))
    scatter, mine, theirs = out_first
    theirs = after(out_second[1][0], *theirs)
    sum_first = combine(scatter, mine, theirs, dtype=F32, **sizes)
    scatter, mine, theirs = out_second
    sum_second = combine(scatter, mine, after(sum_first, *theirs), **sizes)
    back_second = swap_by_core(sum_second, (4, 2))
    sum_first = add(sum_first, *after(sum_second, carry), BF16)
    back_first = swap_by_core(sum_first, (2, 4))
    own = (scatter0, scatter1), (own0, own1), siblings((sent0, sent1))
    total = combine(*own, start=resid, dtype=F32, **sizes)
    return add(add(total, back_second, F32), back_first, BF16)


def local(
    inputs,
    queries,
    key_vectors,
    values,
    out_weight,
    norm_gain,
    routes,
    route_gates,
    w_gate,
    w_up,
    w_down,
):
    row_count = inputs.shape[0]
    tiles = lax.axis_size("tile")
    tile = lax.axis_index("tile")
    width = R_IL * PLANE
    rows = row_count // 2
    capacity = row_count * routes.shape[1] // tiles
    up = [(i, i + 1) for i in range(tiles - 1)]
    down = [(j, i) for i, j in up]
    live = jnp.stack([tile > 0, tile < tiles - 1]).astype(jnp.int32)
    me = jnp.stack([tile, tile ^ 1]).astype(jnp.int32)
    live, me, key_vectors = lax.optimization_barrier((live, me, key_vectors))
    last, first = pack(key_vectors, values, width)
    before = lax.ppermute(last, "tile", up)
    behind = lax.ppermute(first, "tile", down)
    fast = tiles == 8
    meta = None
    if fast:
        items = [routes[:, 0].astype(F32), routes[:, 1].astype(F32)]
        for k in range(2):
            gate = route_gates[:, k]
            high = lax.reduce_precision(gate, 8, 7)
            mid = lax.reduce_precision(gate - high, 8, 7)
            items += [high, mid, gate - high - mid]
        meta = jnp.stack(items).reshape(len(items), 2, rows).swapaxes(0, 1)
        meta = meta.reshape(2, len(items) * rows).astype(BF16)
    acc, tops, sums = interior(queries, key_vectors, values)
    resid, *payloads, whole = edge(
        live, queries, before, behind, acc, tops, sums, inputs, out_weight,
        norm_gain[None, :], meta,
    )
    if fast:
        weights = (w_gate[0], w_up[0], w_down[0])
        return routed_gather(me, payloads, whole, resid, weights, rows, capacity)
    return routed_all_to_all(whole, resid, routes, route_gates, w_gate[0], w_up[0], w_down[0])


def solution(mesh):
    return jax.shard_map(
        local,
        mesh=mesh,
        in_specs=(
            P(("rep", "tile"), None),
            P(("rep", "tile"), None),
            P(("rep", "tile"), None),
            P(("rep", "tile"), None),
            P(),
            P(),
            P(("rep", "tile"), None),
            P(("rep", "tile"), None),
            P("tile", None, None),
            P("tile", None, None),
            P("tile", None, None),
        ),
        out_specs=P(("rep", "tile"), None),
        check_vma=False,
    )
```

```python
import functools

import jax
import jax.numpy as jnp
from jax import lax
from jax.experimental import pallas as pl
from jax.experimental.pallas import tpu as pltpu
from jax.sharding import PartitionSpec as P

HEADS = 16
HD = 64
IL_DEV = 4
XL = 8
DP = 8
R_IL = 2
R_XL = 2
R_DP = 2
PLANE = XL * DP
META = 16
MIB = 1024 * 1024
LONG = 30
F32 = jnp.float32
BF16 = jnp.bfloat16
VMEM = pl.BlockSpec(memory_space=pltpu.VMEM)
SMEM = pl.BlockSpec(memory_space=pltpu.SMEM)
ANY = pl.BlockSpec(memory_space=pl.ANY)


def far(array):
    return pltpu.with_memory_space_constraint(array, pltpu.HBM)


def cost(flops, transcendentals, args, outs):
    moved = sum(a.size * a.dtype.itemsize for a in args)
    moved += sum(o.size * o.dtype.itemsize for o in outs)
    return pl.CostEstimate(flops=flops, transcendentals=transcendentals, bytes_accessed=moved)


NT = (((1,), (1,)), ((), ()))
TN = (((0,), (0,)), ((), ()))


def window_bias(keys, first_key, queries, first_query, live):
    k = lax.broadcasted_iota(jnp.int32, (keys, queries), 0) + (first_key + PLANE * R_IL)
    q = lax.broadcasted_iota(jnp.int32, (keys, queries), 1) + first_query
    near = jnp.abs(q // PLANE + R_IL - k // PLANE) <= R_IL
    near = near & (jnp.abs(q // DP % XL - k // DP % XL) <= R_XL)
    near = near & (jnp.abs(q % DP - k % DP) <= R_DP)
    if live is not None:
        near = near & (live > 0)
    bias = jnp.where(near, F32(0.0), F32(-1e30))
    return jnp.concatenate([bias, bias], axis=1)


def two_heads(query):
    lane = lax.broadcasted_iota(jnp.int32, query.shape, 1)
    query = query * BF16(1.0 / HD**0.5)
    zero = BF16(0.0)
    return jnp.concatenate(
        [jnp.where(lane < HD, query, zero), jnp.where(lane >= HD, query, zero)], axis=0
    )


def pack_kernel(width, k, v, last, first, sems):
    end = k.shape[0] - width
    copies = [
        (k.at[pl.ds(end, width)], last.at[pl.ds(0, width)]),
        (v.at[pl.ds(end, width)], last.at[pl.ds(width, width)]),
        (k.at[pl.ds(0, width)], first.at[pl.ds(0, width)]),
        (v.at[pl.ds(0, width)], first.at[pl.ds(width, width)]),
    ]
    copies = [pltpu.make_async_copy(a, b, sems.at[i]) for i, (a, b) in enumerate(copies)]
    for copy in copies:
        copy.start()
    for copy in copies:
        copy.wait()


def pack(k, v, width):
    flat = [jax.ShapeDtypeStruct((2 * width, k.shape[1]), k.dtype)] * 2
    return pl.pallas_call(
        functools.partial(pack_kernel, width),
        in_specs=[ANY] * 2,
        out_specs=[VMEM] * 2,
        out_shape=flat,
        scratch_shapes=[pltpu.SemaphoreType.DMA((4,))],
        compiler_params=pltpu.CompilerParams(vmem_limit_bytes=12 * MIB),
        cost_estimate=cost(0, 0, flat, flat),
        name="pack",
    )(*[far(a) for a in (k, v)])


def interior_kernel(q, k, v, acc, tops, sums, bias):
    rows = q.shape[0]
    bias[...] = window_bias(rows, 0, rows, 0, None)
    for pair in range(HEADS // 2):
        cols = slice(pair * 2 * HD, (pair + 1) * 2 * HD)
        s = lax.dot_general(k[:, cols], two_heads(q[:, cols]), NT, preferred_element_type=F32)
        s = s + bias[...]
        top = jnp.max(s, axis=0, keepdims=True)
        p = jnp.exp(s - top)
        total = jnp.sum(p, axis=0, keepdims=True)
        o = lax.dot_general(v[:, cols], p.astype(BF16), TN, preferred_element_type=F32)
        base = pair * 2 * HD
        acc[base : base + HD, :] = o[:HD, :rows]
        acc[base + HD : base + 2 * HD, :] = o[HD:, rows:]
        for side in range(2):
            span = slice(side * rows, (side + 1) * rows)
            tops[2 * pair + side : 2 * pair + side + 1, :] = top[:, span]
            sums[2 * pair + side : 2 * pair + side + 1, :] = total[:, span]


def interior(q, k, v):
    rows, model = q.shape
    flat = [jax.ShapeDtypeStruct(shape, F32) for shape in ((model, rows), (HEADS, rows), (HEADS, rows))]
    args = [far(a) for a in (q, k, v)]
    return pl.pallas_call(
        interior_kernel,
        in_specs=[VMEM] * 3,
        out_specs=[VMEM] * 3,
        out_shape=flat,
        scratch_shapes=[pltpu.VMEM((rows, 2 * rows), F32)],
        compiler_params=pltpu.CompilerParams(vmem_limit_bytes=12 * MIB),
        cost_estimate=cost(LONG * 4 * rows * rows * model, HEADS * rows * rows, args, flat),
        name="interior",
    )(*args)


def edge_kernel(live, q, before, behind, tops, sums, gain, acc, x, w, *rest):
    meta = rest[0] if len(rest) == 7 else None
    resid, payload0, payload1, whole = rest[-6:-2]
    bias, att = rest[-2:]
    step = 2 * HD
    pairs = HEADS // 2
    rows = q.shape[0] // 2
    wide = before.shape[0] // 2
    halos = (before, behind)
    for half in range(2):
        first = -wide if half == 0 else 2 * rows
        bias[half] = window_bias(wide, first, rows, half * rows, live[half])
    cells = [(pair, half) for pair in range(pairs) for half in range(2)]
    scores = []
    for pair, half in cells:
        cols = slice(pair * step, (pair + 1) * step)
        queries = two_heads(q[half * rows : (half + 1) * rows, cols])
        s = lax.dot_general(halos[half][:wide, cols], queries, NT, preferred_element_type=F32)
        scores.append(s + bias[half])
    weights = []
    for (pair, half), s in zip(cells, scores):
        span = slice(half * rows, (half + 1) * rows)
        both = [slice(2 * pair + side, 2 * pair + side + 1) for side in range(2)]
        old = jnp.concatenate([tops[b, span] for b in both], axis=1)
        top = jnp.maximum(old, jnp.max(s, axis=0, keepdims=True))
        shrink = jnp.exp(old - top)
        p = jnp.exp(s - top)
        total = jnp.concatenate([sums[b, span] for b in both], axis=1) * shrink
        total = total + jnp.sum(p, axis=0, keepdims=True)
        weights.append((p.astype(BF16), shrink, 1.0 / total))
    for (pair, half), (p, shrink, inverse) in zip(cells, weights):
        span = slice(half * rows, (half + 1) * rows)
        cols = slice(pair * step, (pair + 1) * step)
        o = lax.dot_general(halos[half][wide:, cols], p, TN, preferred_element_type=F32)
        for side in range(2):
            at = slice(side * rows, (side + 1) * rows)
            base = pair * step + side * HD
            value = acc[base : base + HD, span] * shrink[:, at]
            value = value + o[side * HD : (side + 1) * HD, at]
            att[base : base + HD, span] = (value * inverse[:, at]).astype(BF16)
    for half in range(2):
        span = slice(half * rows, (half + 1) * rows)
        res = x[span, :].astype(F32)
        res = res + lax.dot_general(att[:, span], w[...], TN, preferred_element_type=F32)
        res = res.astype(BF16)
        resid[span, :] = res
        res = res.astype(F32)
        square = jnp.mean(res * res, axis=1, keepdims=True)
        normed = (res * lax.rsqrt(square + 1e-06) * gain[...]).astype(BF16)
        (payload0, payload1)[half][:rows, :] = normed
        whole[span, :] = normed
    if meta is not None:
        copies = [
            jnp.broadcast_to(meta[half : half + 1, :], (META // 2, meta.shape[1]))
            for half in range(2)
        ]
        payload0[rows:, :] = jnp.concatenate(copies, axis=0)
        whole[2 * rows :, :] = jnp.concatenate(copies, axis=0)


def edge(live, q, before, behind, acc, tops, sums, x, w, gain, meta):
    rows, model = q.shape[0] // 2, q.shape[1]
    wide = before.shape[0] // 2
    args = [live, q, before, behind, tops, sums, gain, acc, x, w]
    args += [] if meta is None else [meta]
    specs = [SMEM] + [VMEM] * 9 + ([] if meta is None else [VMEM])
    extra = 0 if meta is None else META
    flat = [
        jax.ShapeDtypeStruct((2 * rows, model), BF16),
        jax.ShapeDtypeStruct((rows + extra, model), BF16),
        jax.ShapeDtypeStruct((rows, model), BF16),
        jax.ShapeDtypeStruct((2 * rows + extra, model), BF16),
    ]
    return pl.pallas_call(
        edge_kernel,
        in_specs=specs,
        out_specs=[VMEM] * 4,
        out_shape=flat,
        scratch_shapes=[
            pltpu.VMEM((2, wide, 2 * rows), F32),
            pltpu.VMEM((model, 2 * rows), BF16),
        ],
        compiler_params=pltpu.CompilerParams(vmem_limit_bytes=12 * MIB),
        cost_estimate=cost(
            LONG * (8 * rows * wide * model + 4 * rows * model * model), 2 * HEADS * rows * wide, args, flat
        ),
        name="edge",
    )(*args)


def meta_items(payload, block, rows):
    meta = payload[payload.shape[0] - META :, :].astype(F32)
    meta = meta[block * META // 2 : (block + 1) * META // 2, :]
    return [meta[:, i * rows : (i + 1) * rows] for i in range(8)]


def slot_rows(hits):
    rows = hits.shape[1]
    upper = lax.broadcasted_iota(jnp.int32, (rows, rows), 0) < lax.broadcasted_iota(
        jnp.int32, (rows, rows), 1
    )
    upper = jnp.where(upper, F32(1.0), F32(0.0)).astype(BF16)
    rank = jnp.dot(hits.astype(BF16), upper, preferred_element_type=F32)
    return jnp.where(hits > 0, rank, F32(-1.0))


def experts_kernel(order, rows, capacity, me, *refs):
    payloads = refs[:-9]
    w_gate, w_up, w_down, out_mine, out_sib, scatter, x, hidden, tail = refs[-9:]
    width, model, step = w_gate.shape[1], w_down.shape[1], 256
    expert, other = me[0].astype(F32), me[1].astype(F32)
    groups = len(order) // 2
    items = [meta_items(payloads[holder], block, rows) for _, _, holder, block in order]

    def hits(item, wanted):
        return jnp.where((item[0] == wanted) | (item[1] == wanted), F32(1.0), F32(0.0))

    named = [hits(item, expert) for item in items] + [hits(item, other) for item in items[::2]]
    ranks = slot_rows(jnp.concatenate(named, axis=0))
    ranks = [ranks[i * META // 2 : i * META // 2 + 1, :] for i in range(len(named))]
    slot = lax.broadcasted_iota(jnp.int32, (2 * capacity, rows), 0).astype(F32)
    for g in range(groups):
        first, second = ranks[2 * g : 2 * g + 2]
        second = jnp.where(second >= 0, second + capacity, F32(-1.0))
        hot = jnp.concatenate([slot == first, slot == second], axis=1)
        hot = jnp.where(hot, F32(1.0), F32(0.0)).astype(BF16)
        tokens = [payloads[a][at : at + rows, :] for a, at, _, _ in order[2 * g : 2 * g + 2]]
        picked = jnp.dot(hot, jnp.concatenate(tokens, axis=0), preferred_element_type=F32)
        x[2 * g * capacity : (2 * g + 2) * capacity, :] = picked.astype(BF16)
    for g in range(groups):
        item = items[2 * g]
        for i, (wanted, rank) in enumerate(((expert, ranks[2 * g]), (other, ranks[2 * groups + g]))):
            gate = jnp.where(item[0] == wanted, item[2] + item[3] + item[4], F32(0.0))
            gate = gate + jnp.where(item[1] == wanted, item[5] + item[6] + item[7], F32(0.0))
            full = jnp.where(slot[:capacity] == rank, gate[:1, :], F32(0.0))
            high = full.astype(BF16)
            at = (4 * g + 2 * i) * capacity
            scatter[at : at + capacity, :] = high
            scatter[at + capacity : at + 2 * capacity, :] = (full - high.astype(F32)).astype(BF16)
    for at in range(0, width, step):
        wide = min(step, width - at)
        cols = slice(at, at + wide)
        if wide < step:
            tail[:, :wide] = w_gate[:, cols]
            tail[:, wide : 2 * wide] = w_up[:, cols]
            both = jnp.dot(x[...], tail[...], preferred_element_type=F32)
            g, u = both[:, :wide], both[:, wide:]
        else:
            g = jnp.dot(x[...], w_gate[:, cols], preferred_element_type=F32)
            u = jnp.dot(x[...], w_up[:, cols], preferred_element_type=F32)
        hidden[:, cols] = (g / (1.0 + jnp.exp(-g)) * u).astype(BF16)
    for at in range(0, model, step):
        cols = slice(at, at + step)
        o = jnp.dot(hidden[...], w_down[:, cols], preferred_element_type=F32).astype(BF16)
        for g in range(groups):
            span = slice(g * capacity, (g + 1) * capacity)
            out_mine[span, cols] = o[2 * g * capacity : (2 * g + 1) * capacity]
            out_sib[span, cols] = o[(2 * g + 1) * capacity : (2 * g + 2) * capacity]


def experts(me, payloads, order, weights, rows, capacity):
    model, width = weights[0].shape
    slots = len(order) * capacity
    left = width % 256
    outs = [jax.ShapeDtypeStruct((slots // 2, model), BF16)] * 2
    outs.append(jax.ShapeDtypeStruct((2 * slots, rows), BF16))
    args = [me, *payloads, *weights]
    return pl.pallas_call(
        functools.partial(experts_kernel, order, rows, capacity),
        in_specs=[SMEM] + [VMEM] * (len(args) - 1),
        out_specs=[VMEM] * 3,
        out_shape=outs,
        scratch_shapes=[
            pltpu.VMEM((slots, model), BF16),
            pltpu.VMEM((slots, width), BF16),
            pltpu.VMEM((model, max(2 * left, 256)), BF16),
        ],
        compiler_params=pltpu.CompilerParams(vmem_limit_bytes=12 * MIB),
        cost_estimate=cost(6 * slots * model * width, slots * width, args, outs),
        name=f"experts_{slots}",
    )(*args)


def combine_kernel(rows, capacity, parts, *refs):
    scatters, outs_me, outs_sib = refs[:parts], refs[parts : 2 * parts], refs[2 * parts : 3 * parts]
    refs = refs[3 * parts :]
    result = refs[-1]
    for block in range(2):
        part, at = (block, 0) if parts == 2 else (0, block)
        gates = scatters[part][4 * at * capacity : 4 * (at + 1) * capacity, :]
        span = slice(at * capacity, (at + 1) * capacity)
        mine, theirs = outs_me[part][span, :], outs_sib[part][span, :]
        values = jnp.concatenate([mine, mine, theirs, theirs], axis=0)
        total = lax.dot_general(gates, values, TN, preferred_element_type=F32)
        at = slice(block * rows, (block + 1) * rows)
        if len(refs) == 2:
            total = total + refs[0][at, :].astype(F32)
        result[at, :] = total.astype(result.dtype)


def combine(scatters, outs_me, outs_sib, rows, capacity, start=None, dtype=BF16):
    model = outs_me[0].shape[1]
    args = [*scatters, *outs_me, *outs_sib] + ([] if start is None else [start])
    out = jax.ShapeDtypeStruct((2 * rows, model), dtype)
    return pl.pallas_call(
        functools.partial(combine_kernel, rows, capacity, len(outs_me)),
        in_specs=[VMEM] * len(args),
        out_specs=VMEM,
        out_shape=out,
        compiler_params=pltpu.CompilerParams(vmem_limit_bytes=12 * MIB),
        cost_estimate=cost(8 * out.size * capacity, 0, args, [out]),
        name="combine",
    )(*args)


def add_kernel(a, b, result):
    result[...] = (a[...].astype(F32) + b[...].astype(F32)).astype(result.dtype)


def add(a, b, dtype):
    out = jax.ShapeDtypeStruct(a.shape, dtype)
    return pl.pallas_call(
        add_kernel,
        in_specs=[VMEM] * 2,
        out_specs=VMEM,
        out_shape=out,
        compiler_params=pltpu.CompilerParams(vmem_limit_bytes=12 * MIB),
        cost_estimate=cost(out.size, 0, (a, b), [out]),
        name="add",
    )(a, b)


def expert_rows(token_rows, gate_mat, up_mat, down_mat):
    gate_part = jnp.dot(token_rows, gate_mat, preferred_element_type=F32)
    up_part = jnp.dot(token_rows, up_mat, preferred_element_type=F32)
    hidden = (jax.nn.silu(gate_part) * up_part).astype(BF16)
    return jnp.dot(hidden, down_mat, preferred_element_type=F32).astype(BF16)


def slot_ranks(routes, experts_count, block_rows):
    row_count = routes.shape[0]
    expert_ids = jnp.arange(experts_count, dtype=jnp.int32)
    matches = routes[:, :, None] == expert_ids[None, None, :]
    hits = jnp.sum(matches.astype(jnp.int32), axis=1)
    hits = hits.reshape(row_count // block_rows, block_rows, experts_count)
    earlier = (jnp.cumsum(hits, axis=1) - hits).reshape(row_count, experts_count)
    return jnp.sum(jnp.where(matches, earlier[:, None, :], 0), axis=-1)


def routed_all_to_all(normed, resid, routes, route_gates, w_gate, w_up, w_down):
    tiles = lax.axis_size("tile")
    row_count, route_width = routes.shape
    block_rows, model = row_count // 2, normed.shape[1]
    capacity = row_count * route_width // tiles
    slot_rank = slot_ranks(routes, tiles, block_rows)
    pieces = []
    for index in range(2):
        rows = slice(index * block_rows, (index + 1) * block_rows)
        part_normed = normed[rows]
        positions = routes[rows] * capacity + slot_rank[rows]
        copies = jnp.broadcast_to(
            part_normed[:, None, :], (block_rows, route_width, model)
        ).reshape(-1, model)
        outgoing = jnp.zeros((tiles * capacity, model), BF16).at[positions.reshape(-1)].set(copies)
        outgoing = outgoing.reshape(tiles, capacity, model)
        received = lax.all_to_all(outgoing, "tile", split_axis=0, concat_axis=0, tiled=True)
        produced = expert_rows(received.reshape(-1, model), w_gate, w_up, w_down)
        produced = produced.reshape(received.shape)
        returned = lax.all_to_all(produced, "tile", split_axis=0, concat_axis=0, tiled=True)
        picked = returned.reshape(-1, model)[positions].astype(F32)
        combined = jnp.sum(route_gates[rows][:, :, None] * picked, axis=1)
        pieces.append((resid[rows].astype(F32) + combined).astype(BF16))
    return jnp.concatenate(pieces, axis=0)


def swap(array, bit):
    return lax.ppermute(array, "tile", [(i, i ^ bit) for i in range(8)])


def swap_by_core(array, bits):
    return lax.ppermute(array, "tile", [(i, i ^ bits[i % 2]) for i in range(8)])


def after(first, *later):
    return lax.optimization_barrier((first, *later))[1:]


def routed_gather(me, payloads, whole, resid, weights, rows, capacity):
    sizes = dict(rows=rows, capacity=capacity)

    def evaluate(mine, theirs):
        count = len(mine)
        order = []
        for block in range(2):
            array, at = (block, 0) if count == 2 else (0, block * rows)
            order += [(array, at, 0, block), (count + array, at, count, block)]
        kept, sent, scatter = experts(me, (*mine, *theirs), order, weights, **sizes)
        return (scatter,), (kept,), (swap(sent, 1),)

    def siblings(arrays):
        return [swap(a, 1) for a in arrays]

    first = [swap_by_core(p, (2, 4)) for p in payloads]
    sib = siblings(payloads)
    order = [(0, 0, 0, 0), (1, 0, 1, 0)]
    own0, sent0, scatter0 = experts(me, (payloads[0], sib[0]), order, weights, **sizes)
    (first[0],) = after(own0, first[0])
    diag0 = swap_by_core(first[0], (4, 2))
    later = after(first[0], payloads[1], sib[1])
    order = [(0, 0, 2, 1), (1, 0, 3, 1)]
    own1, sent1, scatter1 = experts(me, (*later, payloads[0], sib[0]), order, weights, **sizes)
    (first[1],) = after(own1, first[1])
    diag1 = swap_by_core(first[1], (4, 2))
    far = siblings(first)
    first[0], _ = lax.optimization_barrier((first[0], diag0))
    out_first = evaluate(first, far)
    second1 = swap_by_core(*after(diag0, payloads[1]), (4, 2))
    (diag1,) = after(out_first[1][0], diag1)
    second0 = swap_by_core(*after(diag1, payloads[0]), (4, 2))
    diag = [diag0, diag1]
    out_diag = evaluate(after(second1, *diag), siblings(diag))
    scatter, mine, theirs = out_diag
    sum_diag = combine(scatter, mine, after(second0, *theirs), **sizes)
    carry = swap_by_core(sum_diag, (4, 2))
    second = after(sum_diag, second0, second1)
    out_second = evaluate(second, siblings(second))
    scatter, mine, theirs = out_first
    theirs = after(out_second[1][0], *theirs)
    sum_first = combine(scatter, mine, theirs, dtype=F32, **sizes)
    scatter, mine, theirs = out_second
    sum_second = combine(scatter, mine, after(sum_first, *theirs), **sizes)
    back_second = swap_by_core(sum_second, (4, 2))
    sum_first = add(sum_first, *after(sum_second, carry), BF16)
    back_first = swap_by_core(sum_first, (2, 4))
    own = (scatter0, scatter1), (own0, own1), siblings((sent0, sent1))
    total = combine(*own, start=resid, dtype=F32, **sizes)
    return add(add(total, back_second, F32), back_first, BF16)


def local(
    inputs,
    queries,
    key_vectors,
    values,
    out_weight,
    norm_gain,
    routes,
    route_gates,
    w_gate,
    w_up,
    w_down,
):
    row_count = inputs.shape[0]
    tiles = lax.axis_size("tile")
    tile = lax.axis_index("tile")
    width = R_IL * PLANE
    rows = row_count // 2
    capacity = row_count * routes.shape[1] // tiles
    up = [(i, i + 1) for i in range(tiles - 1)]
    down = [(j, i) for i, j in up]
    live = jnp.stack([tile > 0, tile < tiles - 1]).astype(jnp.int32)
    me = jnp.stack([tile, tile ^ 1]).astype(jnp.int32)
    live, me, key_vectors = lax.optimization_barrier((live, me, key_vectors))
    last, first = pack(key_vectors, values, width)
    before = lax.ppermute(last, "tile", up)
    behind = lax.ppermute(first, "tile", down)
    fast = tiles == 8
    meta = None
    if fast:
        items = [routes[:, 0].astype(F32), routes[:, 1].astype(F32)]
        for k in range(2):
            gate = route_gates[:, k]
            high = lax.reduce_precision(gate, 8, 7)
            mid = lax.reduce_precision(gate - high, 8, 7)
            items += [high, mid, gate - high - mid]
        meta = jnp.stack(items).reshape(len(items), 2, rows).swapaxes(0, 1)
        meta = meta.reshape(2, len(items) * rows).astype(BF16)
    acc, tops, sums = interior(queries, key_vectors, values)
    resid, *payloads, whole = edge(
        live, queries, before, behind, acc, tops, sums, inputs, out_weight,
        norm_gain[None, :], meta,
    )
    if fast:
        weights = (w_gate[0], w_up[0], w_down[0])
        return routed_gather(me, payloads, whole, resid, weights, rows, capacity)
    return routed_all_to_all(whole, resid, routes, route_gates, w_gate[0], w_up[0], w_down[0])


def solution(mesh):
    return jax.shard_map(
        local,
        mesh=mesh,
        in_specs=(
            P(("rep", "tile"), None),
            P(("rep", "tile"), None),
            P(("rep", "tile"), None),
            P(("rep", "tile"), None),
            P(),
            P(),
            P(("rep", "tile"), None),
            P(("rep", "tile"), None),
            P("tile", None, None),
            P("tile", None, None),
            P("tile", None, None),
        ),
        out_specs=P(("rep", "tile"), None),
        check_vma=False,
    )
```

```python
import functools

import jax
import jax.numpy as jnp
from jax import lax
from jax.experimental import pallas as pl
from jax.experimental.pallas import tpu as pltpu
from jax.sharding import PartitionSpec as P

HEADS = 16
HD = 64
IL_DEV = 4
XL = 8
DP = 8
R_IL = 2
R_XL = 2
R_DP = 2
PLANE = XL * DP
META = 16
MIB = 1024 * 1024
LONG = 30
F32 = jnp.float32
BF16 = jnp.bfloat16
VMEM = pl.BlockSpec(memory_space=pltpu.VMEM)
SMEM = pl.BlockSpec(memory_space=pltpu.SMEM)
ANY = pl.BlockSpec(memory_space=pl.ANY)


def far(array):
    return pltpu.with_memory_space_constraint(array, pltpu.HBM)


def cost(flops, transcendentals, args, outs):
    moved = sum(a.size * a.dtype.itemsize for a in args)
    moved += sum(o.size * o.dtype.itemsize for o in outs)
    return pl.CostEstimate(flops=flops, transcendentals=transcendentals, bytes_accessed=moved)


NT = (((1,), (1,)), ((), ()))
TN = (((0,), (0,)), ((), ()))


def window_bias(keys, first_key, queries, first_query, live):
    k = lax.broadcasted_iota(jnp.int32, (keys, queries), 0) + (first_key + PLANE * R_IL)
    q = lax.broadcasted_iota(jnp.int32, (keys, queries), 1) + first_query
    near = jnp.abs(q // PLANE + R_IL - k // PLANE) <= R_IL
    near = near & (jnp.abs(q // DP % XL - k // DP % XL) <= R_XL)
    near = near & (jnp.abs(q % DP - k % DP) <= R_DP)
    if live is not None:
        near = near & (live > 0)
    bias = jnp.where(near, F32(0.0), F32(-1e30))
    return jnp.concatenate([bias, bias], axis=1)


def two_heads(query):
    lane = lax.broadcasted_iota(jnp.int32, query.shape, 1)
    query = query * BF16(1.0 / HD**0.5)
    zero = BF16(0.0)
    return jnp.concatenate(
        [jnp.where(lane < HD, query, zero), jnp.where(lane >= HD, query, zero)], axis=0
    )


def pack_kernel(width, k, v, last, first, sems):
    end = k.shape[0] - width
    copies = [
        (k.at[pl.ds(end, width)], last.at[pl.ds(0, width)]),
        (v.at[pl.ds(end, width)], last.at[pl.ds(width, width)]),
        (k.at[pl.ds(0, width)], first.at[pl.ds(0, width)]),
        (v.at[pl.ds(0, width)], first.at[pl.ds(width, width)]),
    ]
    copies = [pltpu.make_async_copy(a, b, sems.at[i]) for i, (a, b) in enumerate(copies)]
    for copy in copies:
        copy.start()
    for copy in copies:
        copy.wait()


def pack(k, v, width):
    flat = [jax.ShapeDtypeStruct((2 * width, k.shape[1]), k.dtype)] * 2
    return pl.pallas_call(
        functools.partial(pack_kernel, width),
        in_specs=[ANY] * 2,
        out_specs=[VMEM] * 2,
        out_shape=flat,
        scratch_shapes=[pltpu.SemaphoreType.DMA((4,))],
        compiler_params=pltpu.CompilerParams(vmem_limit_bytes=12 * MIB),
        cost_estimate=cost(0, 0, flat, flat),
        name="pack",
    )(*[far(a) for a in (k, v)])


def interior_kernel(q, k, v, acc, tops, sums, bias):
    rows = q.shape[0]
    bias[...] = window_bias(rows, 0, rows, 0, None)
    for pair in range(HEADS // 2):
        cols = slice(pair * 2 * HD, (pair + 1) * 2 * HD)
        s = lax.dot_general(k[:, cols], two_heads(q[:, cols]), NT, preferred_element_type=F32)
        s = s + bias[...]
        top = jnp.max(s, axis=0, keepdims=True)
        p = jnp.exp(s - top)
        total = jnp.sum(p, axis=0, keepdims=True)
        o = lax.dot_general(v[:, cols], p.astype(BF16), TN, preferred_element_type=F32)
        base = pair * 2 * HD
        acc[base : base + HD, :] = o[:HD, :rows]
        acc[base + HD : base + 2 * HD, :] = o[HD:, rows:]
        for side in range(2):
            span = slice(side * rows, (side + 1) * rows)
            tops[2 * pair + side : 2 * pair + side + 1, :] = top[:, span]
            sums[2 * pair + side : 2 * pair + side + 1, :] = total[:, span]


def interior(q, k, v):
    rows, model = q.shape
    flat = [jax.ShapeDtypeStruct(shape, F32) for shape in ((model, rows), (HEADS, rows), (HEADS, rows))]
    args = [far(a) for a in (q, k, v)]
    return pl.pallas_call(
        interior_kernel,
        in_specs=[VMEM] * 3,
        out_specs=[VMEM] * 3,
        out_shape=flat,
        scratch_shapes=[pltpu.VMEM((rows, 2 * rows), F32)],
        compiler_params=pltpu.CompilerParams(vmem_limit_bytes=12 * MIB),
        cost_estimate=cost(LONG * 4 * rows * rows * model, HEADS * rows * rows, args, flat),
        name="interior",
    )(*args)


def edge_kernel(half, live, q, halo, tops, sums, gain, acc, x, w, *rest):
    meta = rest[0] if len(rest) == 5 else None
    resid, payload, bias, att = rest[-4:]
    step = 2 * HD
    pairs = range(HEADS // 2)
    rows = q.shape[0] // 2
    wide = halo.shape[0] // 2
    span = slice(half * rows, (half + 1) * rows)
    first = -wide if half == 0 else 2 * rows
    bias[...] = window_bias(wide, first, rows, half * rows, live[half])
    scores = []
    for pair in pairs:
        cols = slice(pair * step, (pair + 1) * step)
        queries = two_heads(q[span, cols])
        s = lax.dot_general(halo[:wide, cols], queries, NT, preferred_element_type=F32)
        scores.append(s + bias[...])
    weights = []
    for pair, s in zip(pairs, scores):
        both = [slice(2 * pair + side, 2 * pair + side + 1) for side in range(2)]
        old = jnp.concatenate([tops[b, span] for b in both], axis=1)
        top = jnp.maximum(old, jnp.max(s, axis=0, keepdims=True))
        shrink = jnp.exp(old - top)
        p = jnp.exp(s - top)
        total = jnp.concatenate([sums[b, span] for b in both], axis=1) * shrink
        total = total + jnp.sum(p, axis=0, keepdims=True)
        weights.append((p.astype(BF16), shrink, 1.0 / total))
    for pair, (p, shrink, inverse) in zip(pairs, weights):
        cols = slice(pair * step, (pair + 1) * step)
        o = lax.dot_general(halo[wide:, cols], p, TN, preferred_element_type=F32)
        for side in range(2):
            at = slice(side * rows, (side + 1) * rows)
            base = pair * step + side * HD
            value = acc[base : base + HD, span] * shrink[:, at]
            value = value + o[side * HD : (side + 1) * HD, at]
            att[base : base + HD, :] = (value * inverse[:, at]).astype(BF16)
    res = x[span, :].astype(F32)
    res = res + lax.dot_general(att[...], w[...], TN, preferred_element_type=F32)
    res = res.astype(BF16)
    resid[...] = res
    res = res.astype(F32)
    square = jnp.mean(res * res, axis=1, keepdims=True)
    payload[:rows, :] = (res * lax.rsqrt(square + 1e-06) * gain[...]).astype(BF16)
    if meta is not None:
        copies = [
            jnp.broadcast_to(meta[i : i + 1, :], (META // 2, meta.shape[1])) for i in range(2)
        ]
        payload[rows:, :] = jnp.concatenate(copies, axis=0)


def edge(half, live, q, halo, acc, tops, sums, x, w, gain, meta):
    rows, model = q.shape[0] // 2, q.shape[1]
    wide = halo.shape[0] // 2
    args = [live, q, halo, tops, sums, gain, acc, x, w]
    args += [] if meta is None else [meta]
    extra = 0 if meta is None else META
    flat = [
        jax.ShapeDtypeStruct((rows, model), BF16),
        jax.ShapeDtypeStruct((rows + extra, model), BF16),
    ]
    return pl.pallas_call(
        functools.partial(edge_kernel, half),
        in_specs=[SMEM] + [VMEM] * (len(args) - 1),
        out_specs=[VMEM] * 2,
        out_shape=flat,
        scratch_shapes=[
            pltpu.VMEM((wide, 2 * rows), F32),
            pltpu.VMEM((model, rows), BF16),
        ],
        compiler_params=pltpu.CompilerParams(vmem_limit_bytes=12 * MIB),
        cost_estimate=cost(
            4 * rows * wide * model + 2 * rows * model * model, HEADS * rows * wide, args, flat
        ),
        name=f"edge_half{half}",
    )(*args)


def meta_items(payload, block, rows):
    meta = payload[payload.shape[0] - META :, :].astype(F32)
    meta = meta[block * META // 2 : (block + 1) * META // 2, :]
    return [meta[:, i * rows : (i + 1) * rows] for i in range(8)]


def slot_rows(hits):
    rows = hits.shape[1]
    upper = lax.broadcasted_iota(jnp.int32, (rows, rows), 0) < lax.broadcasted_iota(
        jnp.int32, (rows, rows), 1
    )
    upper = jnp.where(upper, F32(1.0), F32(0.0)).astype(BF16)
    rank = jnp.dot(hits.astype(BF16), upper, preferred_element_type=F32)
    return jnp.where(hits > 0, rank, F32(-1.0))


def experts_kernel(order, rows, capacity, me, *refs):
    payloads = refs[:-9]
    w_gate, w_up, w_down, out_mine, out_sib, scatter, x, hidden, tail = refs[-9:]
    width, model, step = w_gate.shape[1], w_down.shape[1], 256
    expert, other = me[0].astype(F32), me[1].astype(F32)
    groups = len(order) // 2
    items = [meta_items(payloads[holder], block, rows) for _, _, holder, block in order]

    def hits(item, wanted):
        return jnp.where((item[0] == wanted) | (item[1] == wanted), F32(1.0), F32(0.0))

    named = [hits(item, expert) for item in items] + [hits(item, other) for item in items[::2]]
    ranks = slot_rows(jnp.concatenate(named, axis=0))
    ranks = [ranks[i * META // 2 : i * META // 2 + 1, :] for i in range(len(named))]
    slot = lax.broadcasted_iota(jnp.int32, (2 * capacity, rows), 0).astype(F32)
    for g in range(groups):
        first, second = ranks[2 * g : 2 * g + 2]
        second = jnp.where(second >= 0, second + capacity, F32(-1.0))
        hot = jnp.concatenate([slot == first, slot == second], axis=1)
        hot = jnp.where(hot, F32(1.0), F32(0.0)).astype(BF16)
        tokens = [payloads[a][at : at + rows, :] for a, at, _, _ in order[2 * g : 2 * g + 2]]
        picked = jnp.dot(hot, jnp.concatenate(tokens, axis=0), preferred_element_type=F32)
        x[2 * g * capacity : (2 * g + 2) * capacity, :] = picked.astype(BF16)
    for g in range(groups):
        item = items[2 * g]
        for i, (wanted, rank) in enumerate(((expert, ranks[2 * g]), (other, ranks[2 * groups + g]))):
            gate = jnp.where(item[0] == wanted, item[2] + item[3] + item[4], F32(0.0))
            gate = gate + jnp.where(item[1] == wanted, item[5] + item[6] + item[7], F32(0.0))
            full = jnp.where(slot[:capacity] == rank, gate[:1, :], F32(0.0))
            high = full.astype(BF16)
            at = (4 * g + 2 * i) * capacity
            scatter[at : at + capacity, :] = high
            scatter[at + capacity : at + 2 * capacity, :] = (full - high.astype(F32)).astype(BF16)
    for at in range(0, width, step):
        wide = min(step, width - at)
        cols = slice(at, at + wide)
        if wide < step:
            tail[:, :wide] = w_gate[:, cols]
            tail[:, wide : 2 * wide] = w_up[:, cols]
            both = jnp.dot(x[...], tail[...], preferred_element_type=F32)
            g, u = both[:, :wide], both[:, wide:]
        else:
            g = jnp.dot(x[...], w_gate[:, cols], preferred_element_type=F32)
            u = jnp.dot(x[...], w_up[:, cols], preferred_element_type=F32)
        hidden[:, cols] = (g / (1.0 + jnp.exp(-g)) * u).astype(BF16)
    for at in range(0, model, step):
        cols = slice(at, at + step)
        o = jnp.dot(hidden[...], w_down[:, cols], preferred_element_type=F32).astype(BF16)
        for g in range(groups):
            span = slice(g * capacity, (g + 1) * capacity)
            out_mine[span, cols] = o[2 * g * capacity : (2 * g + 1) * capacity]
            out_sib[span, cols] = o[(2 * g + 1) * capacity : (2 * g + 2) * capacity]


def experts(me, payloads, order, weights, rows, capacity):
    model, width = weights[0].shape
    slots = len(order) * capacity
    left = width % 256
    outs = [jax.ShapeDtypeStruct((slots // 2, model), BF16)] * 2
    outs.append(jax.ShapeDtypeStruct((2 * slots, rows), BF16))
    args = [me, *payloads, *weights]
    return pl.pallas_call(
        functools.partial(experts_kernel, order, rows, capacity),
        in_specs=[SMEM] + [VMEM] * (len(args) - 1),
        out_specs=[VMEM] * 3,
        out_shape=outs,
        scratch_shapes=[
            pltpu.VMEM((slots, model), BF16),
            pltpu.VMEM((slots, width), BF16),
            pltpu.VMEM((model, max(2 * left, 256)), BF16),
        ],
        compiler_params=pltpu.CompilerParams(vmem_limit_bytes=12 * MIB),
        cost_estimate=cost(6 * slots * model * width, slots * width, args, outs),
        name=f"experts_{slots}",
    )(*args)


def combine_kernel(rows, capacity, parts, *refs):
    scatters, outs_me, outs_sib = refs[:parts], refs[parts : 2 * parts], refs[2 * parts : 3 * parts]
    refs = refs[3 * parts :]
    result = refs[-1]
    for block in range(2):
        part, at = (block, 0) if parts == 2 else (0, block)
        gates = scatters[part][4 * at * capacity : 4 * (at + 1) * capacity, :]
        span = slice(at * capacity, (at + 1) * capacity)
        mine, theirs = outs_me[part][span, :], outs_sib[part][span, :]
        values = jnp.concatenate([mine, mine, theirs, theirs], axis=0)
        total = lax.dot_general(gates, values, TN, preferred_element_type=F32)
        at = slice(block * rows, (block + 1) * rows)
        if len(refs) == 3:
            total = total + refs[block][...].astype(F32)
        result[at, :] = total.astype(result.dtype)


def combine(scatters, outs_me, outs_sib, rows, capacity, start=(), dtype=BF16):
    model = outs_me[0].shape[1]
    args = [*scatters, *outs_me, *outs_sib, *start]
    out = jax.ShapeDtypeStruct((2 * rows, model), dtype)
    return pl.pallas_call(
        functools.partial(combine_kernel, rows, capacity, len(outs_me)),
        in_specs=[VMEM] * len(args),
        out_specs=VMEM,
        out_shape=out,
        compiler_params=pltpu.CompilerParams(vmem_limit_bytes=12 * MIB),
        cost_estimate=cost(8 * out.size * capacity, 0, args, [out]),
        name="combine",
    )(*args)


def add_kernel(a, b, result):
    result[...] = (a[...].astype(F32) + b[...].astype(F32)).astype(result.dtype)


def add(a, b, dtype):
    out = jax.ShapeDtypeStruct(a.shape, dtype)
    return pl.pallas_call(
        add_kernel,
        in_specs=[VMEM] * 2,
        out_specs=VMEM,
        out_shape=out,
        compiler_params=pltpu.CompilerParams(vmem_limit_bytes=12 * MIB),
        cost_estimate=cost(out.size, 0, (a, b), [out]),
        name="add",
    )(a, b)


def expert_rows(token_rows, gate_mat, up_mat, down_mat):
    gate_part = jnp.dot(token_rows, gate_mat, preferred_element_type=F32)
    up_part = jnp.dot(token_rows, up_mat, preferred_element_type=F32)
    hidden = (jax.nn.silu(gate_part) * up_part).astype(BF16)
    return jnp.dot(hidden, down_mat, preferred_element_type=F32).astype(BF16)


def slot_ranks(routes, experts_count, block_rows):
    row_count = routes.shape[0]
    expert_ids = jnp.arange(experts_count, dtype=jnp.int32)
    matches = routes[:, :, None] == expert_ids[None, None, :]
    hits = jnp.sum(matches.astype(jnp.int32), axis=1)
    hits = hits.reshape(row_count // block_rows, block_rows, experts_count)
    earlier = (jnp.cumsum(hits, axis=1) - hits).reshape(row_count, experts_count)
    return jnp.sum(jnp.where(matches, earlier[:, None, :], 0), axis=-1)


def routed_all_to_all(normed, resid, routes, route_gates, w_gate, w_up, w_down):
    tiles = lax.axis_size("tile")
    row_count, route_width = routes.shape
    block_rows, model = row_count // 2, normed.shape[1]
    capacity = row_count * route_width // tiles
    slot_rank = slot_ranks(routes, tiles, block_rows)
    pieces = []
    for index in range(2):
        rows = slice(index * block_rows, (index + 1) * block_rows)
        part_normed = normed[rows]
        positions = routes[rows] * capacity + slot_rank[rows]
        copies = jnp.broadcast_to(
            part_normed[:, None, :], (block_rows, route_width, model)
        ).reshape(-1, model)
        outgoing = jnp.zeros((tiles * capacity, model), BF16).at[positions.reshape(-1)].set(copies)
        outgoing = outgoing.reshape(tiles, capacity, model)
        received = lax.all_to_all(outgoing, "tile", split_axis=0, concat_axis=0, tiled=True)
        produced = expert_rows(received.reshape(-1, model), w_gate, w_up, w_down)
        produced = produced.reshape(received.shape)
        returned = lax.all_to_all(produced, "tile", split_axis=0, concat_axis=0, tiled=True)
        picked = returned.reshape(-1, model)[positions].astype(F32)
        combined = jnp.sum(route_gates[rows][:, :, None] * picked, axis=1)
        pieces.append((resid[rows].astype(F32) + combined).astype(BF16))
    return jnp.concatenate(pieces, axis=0)


def swap(array, bit):
    return lax.ppermute(array, "tile", [(i, i ^ bit) for i in range(8)])


def swap_by_core(array, bits):
    return lax.ppermute(array, "tile", [(i, i ^ bits[i % 2]) for i in range(8)])


def after(first, *later):
    return lax.optimization_barrier((first, *later))[1:]


def routed_gather(me, payloads, resids, weights, rows, capacity):
    sizes = dict(rows=rows, capacity=capacity)

    def evaluate(mine, theirs):
        count = len(mine)
        order = []
        for block in range(2):
            array, at = (block, 0) if count == 2 else (0, block * rows)
            order += [(array, at, 0, block), (count + array, at, count, block)]
        kept, sent, scatter = experts(me, (*mine, *theirs), order, weights, **sizes)
        return (scatter,), (kept,), (swap(sent, 1),)

    def siblings(arrays):
        return [swap(a, 1) for a in arrays]

    first = [swap_by_core(p, (2, 4)) for p in payloads]
    sib = siblings(payloads)
    order = [(0, 0, 0, 0), (1, 0, 1, 0)]
    own0, sent0, scatter0 = experts(me, (payloads[0], sib[0]), order, weights, **sizes)
    (first[0],) = after(own0, first[0])
    diag0 = swap_by_core(first[0], (4, 2))
    later = after(first[0], payloads[1], sib[1])
    order = [(0, 0, 2, 1), (1, 0, 3, 1)]
    own1, sent1, scatter1 = experts(me, (*later, payloads[0], sib[0]), order, weights, **sizes)
    (first[1],) = after(own1, first[1])
    diag1 = swap_by_core(first[1], (4, 2))
    far = siblings(first)
    first[0], _ = lax.optimization_barrier((first[0], diag0))
    out_first = evaluate(first, far)
    second1 = swap_by_core(*after(diag0, payloads[1]), (4, 2))
    (diag1,) = after(out_first[1][0], diag1)
    second0 = swap_by_core(*after(diag1, payloads[0]), (4, 2))
    diag = [diag0, diag1]
    out_diag = evaluate(after(second1, *diag), siblings(diag))
    scatter, mine, theirs = out_diag
    sum_diag = combine(scatter, mine, after(second0, *theirs), **sizes)
    carry = swap_by_core(sum_diag, (4, 2))
    second = after(sum_diag, second0, second1)
    out_second = evaluate(second, siblings(second))
    scatter, mine, theirs = out_first
    theirs = after(out_second[1][0], *theirs)
    sum_first = combine(scatter, mine, theirs, dtype=F32, **sizes)
    scatter, mine, theirs = out_second
    sum_second = combine(scatter, mine, after(sum_first, *theirs), **sizes)
    back_second = swap_by_core(sum_second, (4, 2))
    sum_first = add(sum_first, *after(sum_second, carry), BF16)
    back_first = swap_by_core(sum_first, (2, 4))
    own = (scatter0, scatter1), (own0, own1), siblings((sent0, sent1))
    total = combine(*own, start=resids, dtype=F32, **sizes)
    return add(add(total, back_second, F32), back_first, BF16)


def local(
    inputs,
    queries,
    key_vectors,
    values,
    out_weight,
    norm_gain,
    routes,
    route_gates,
    w_gate,
    w_up,
    w_down,
):
    row_count = inputs.shape[0]
    tiles = lax.axis_size("tile")
    tile = lax.axis_index("tile")
    width = R_IL * PLANE
    rows = row_count // 2
    capacity = row_count * routes.shape[1] // tiles
    up = [(i, i + 1) for i in range(tiles - 1)]
    down = [(j, i) for i, j in up]
    live = jnp.stack([tile > 0, tile < tiles - 1]).astype(jnp.int32)
    me = jnp.stack([tile, tile ^ 1]).astype(jnp.int32)
    live, me, key_vectors = lax.optimization_barrier((live, me, key_vectors))
    last, first = pack(key_vectors, values, width)
    before = lax.ppermute(last, "tile", up)
    behind = lax.ppermute(first, "tile", down)
    fast = tiles == 8
    meta = None
    if fast:
        items = [routes[:, 0].astype(F32), routes[:, 1].astype(F32)]
        for k in range(2):
            gate = route_gates[:, k]
            high = lax.reduce_precision(gate, 8, 7)
            mid = lax.reduce_precision(gate - high, 8, 7)
            items += [high, mid, gate - high - mid]
        meta = jnp.stack(items).reshape(len(items), 2, rows).swapaxes(0, 1)
        meta = meta.reshape(2, len(items) * rows).astype(BF16)
    acc, tops, sums = interior(queries, key_vectors, values)
    halves = [
        edge(
            half, live, queries, halo, acc, tops, sums, inputs, out_weight, norm_gain[None, :],
            meta if half == 0 else None,
        )
        for half, halo in enumerate((before, behind))
    ]
    resids, payloads = zip(*halves)
    if fast:
        weights = (w_gate[0], w_up[0], w_down[0])
        return routed_gather(me, payloads, resids, weights, rows, capacity)
    payload, resid = jnp.concatenate(payloads, axis=0), jnp.concatenate(resids, axis=0)
    return routed_all_to_all(payload, resid, routes, route_gates, w_gate[0], w_up[0], w_down[0])


def solution(mesh):
    return jax.shard_map(
        local,
        mesh=mesh,
        in_specs=(
            P(("rep", "tile"), None),
            P(("rep", "tile"), None),
            P(("rep", "tile"), None),
            P(("rep", "tile"), None),
            P(),
            P(),
            P(("rep", "tile"), None),
            P(("rep", "tile"), None),
            P("tile", None, None),
            P("tile", None, None),
            P("tile", None, None),
        ),
        out_specs=P(("rep", "tile"), None),
        check_vma=False,
    )
```

```python
import functools

import jax
import jax.numpy as jnp
from jax import lax
from jax.experimental import pallas as pl
from jax.experimental.pallas import tpu as pltpu
from jax.sharding import PartitionSpec as P

HEADS = 16
HD = 64
IL_DEV = 4
XL = 8
DP = 8
R_IL = 2
R_XL = 2
R_DP = 2
PLANE = XL * DP
META = 16
MIB = 1024 * 1024
LONG = 30
F32 = jnp.float32
BF16 = jnp.bfloat16
VMEM = pl.BlockSpec(memory_space=pltpu.VMEM)
SMEM = pl.BlockSpec(memory_space=pltpu.SMEM)
ANY = pl.BlockSpec(memory_space=pl.ANY)


def far(array):
    return pltpu.with_memory_space_constraint(array, pltpu.HBM)


def cost(flops, transcendentals, args, outs):
    moved = sum(a.size * a.dtype.itemsize for a in args)
    moved += sum(o.size * o.dtype.itemsize for o in outs)
    return pl.CostEstimate(flops=flops, transcendentals=transcendentals, bytes_accessed=moved)


NT = (((1,), (1,)), ((), ()))
TN = (((0,), (0,)), ((), ()))


def window_bias(keys, first_key, queries, first_query, live):
    k = lax.broadcasted_iota(jnp.int32, (keys, queries), 0) + (first_key + PLANE * R_IL)
    q = lax.broadcasted_iota(jnp.int32, (keys, queries), 1) + first_query
    near = jnp.abs(q // PLANE + R_IL - k // PLANE) <= R_IL
    near = near & (jnp.abs(q // DP % XL - k // DP % XL) <= R_XL)
    near = near & (jnp.abs(q % DP - k % DP) <= R_DP)
    if live is not None:
        near = near & (live > 0)
    bias = jnp.where(near, F32(0.0), F32(-1e30))
    return jnp.concatenate([bias, bias], axis=1)


def two_heads(query):
    lane = lax.broadcasted_iota(jnp.int32, query.shape, 1)
    query = query * BF16(1.0 / HD**0.5)
    zero = BF16(0.0)
    return jnp.concatenate(
        [jnp.where(lane < HD, query, zero), jnp.where(lane >= HD, query, zero)], axis=0
    )


def pack_kernel(info, k, v, near, other):
    width = near.shape[0] // 2
    for piece, target in enumerate((near, other)):
        source = pl.ds(pl.multiple_of(info[piece] * width, width), width)
        target[:width, :] = k[source, :]
        target[width:, :] = v[source, :]


def pack(info, k, v):
    flat = [jax.ShapeDtypeStruct(k.shape, k.dtype)] * 2
    return pl.pallas_call(
        pack_kernel,
        in_specs=[SMEM] + [VMEM] * 2,
        out_specs=[VMEM] * 2,
        out_shape=flat,
        compiler_params=pltpu.CompilerParams(vmem_limit_bytes=12 * MIB),
        cost_estimate=cost(0, 0, flat, flat),
        name="pack",
    )(info, *[far(a) for a in (k, v)])


def interior_kernel(q, k, v, acc, tops, sums, bias):
    rows = q.shape[0]
    bias[...] = window_bias(rows, 0, rows, 0, None)
    for pair in range(HEADS // 2):
        cols = slice(pair * 2 * HD, (pair + 1) * 2 * HD)
        s = lax.dot_general(k[:, cols], two_heads(q[:, cols]), NT, preferred_element_type=F32)
        s = s + bias[...]
        top = jnp.max(s, axis=0, keepdims=True)
        p = jnp.exp(s - top)
        total = jnp.sum(p, axis=0, keepdims=True)
        o = lax.dot_general(v[:, cols], p.astype(BF16), TN, preferred_element_type=F32)
        base = pair * 2 * HD
        acc[base : base + HD, :] = o[:HD, :rows]
        acc[base + HD : base + 2 * HD, :] = o[HD:, rows:]
        for side in range(2):
            span = slice(side * rows, (side + 1) * rows)
            tops[2 * pair + side : 2 * pair + side + 1, :] = top[:, span]
            sums[2 * pair + side : 2 * pair + side + 1, :] = total[:, span]


def interior(q, k, v):
    rows, model = q.shape
    flat = [jax.ShapeDtypeStruct(shape, F32) for shape in ((model, rows), (HEADS, rows), (HEADS, rows))]
    args = [far(a) for a in (q, k, v)]
    return pl.pallas_call(
        interior_kernel,
        in_specs=[VMEM] * 3,
        out_specs=[VMEM] * 3,
        out_shape=flat,
        scratch_shapes=[pltpu.VMEM((rows, 2 * rows), F32)],
        compiler_params=pltpu.CompilerParams(vmem_limit_bytes=12 * MIB),
        cost_estimate=cost(LONG * 4 * rows * rows * model, HEADS * rows * rows, args, flat),
        name="interior",
    )(*args)


def edge_kernel(piece, info, q, halo, tops, sums, gain, acc, x, w, *rest):
    meta = rest[0] if len(rest) == 5 else None
    resid, payload, bias, att = rest[-4:]
    step = 2 * HD
    pairs = range(HEADS // 2)
    rows = q.shape[0] // 2
    wide = halo.shape[0] // 2
    half = info[piece]
    span = pl.ds(pl.multiple_of(half * rows, rows), rows)
    first = jnp.where(half == 0, -wide, 2 * rows)
    bias[...] = window_bias(wide, first, rows, half * rows, info[2 + half])
    scores = []
    for pair in pairs:
        cols = slice(pair * step, (pair + 1) * step)
        queries = two_heads(q[span, cols])
        s = lax.dot_general(halo[:wide, cols], queries, NT, preferred_element_type=F32)
        scores.append(s + bias[...])
    weights = []
    for pair, s in zip(pairs, scores):
        both = [slice(2 * pair + side, 2 * pair + side + 1) for side in range(2)]
        old = jnp.concatenate([tops[b, span] for b in both], axis=1)
        top = jnp.maximum(old, jnp.max(s, axis=0, keepdims=True))
        shrink = jnp.exp(old - top)
        p = jnp.exp(s - top)
        total = jnp.concatenate([sums[b, span] for b in both], axis=1) * shrink
        total = total + jnp.sum(p, axis=0, keepdims=True)
        weights.append((p.astype(BF16), shrink, 1.0 / total))
    for pair, (p, shrink, inverse) in zip(pairs, weights):
        cols = slice(pair * step, (pair + 1) * step)
        o = lax.dot_general(halo[wide:, cols], p, TN, preferred_element_type=F32)
        for side in range(2):
            at = slice(side * rows, (side + 1) * rows)
            base = pair * step + side * HD
            value = acc[base : base + HD, span] * shrink[:, at]
            value = value + o[side * HD : (side + 1) * HD, at]
            att[base : base + HD, :] = (value * inverse[:, at]).astype(BF16)
    res = x[span, :].astype(F32)
    res = res + lax.dot_general(att[...], w[...], TN, preferred_element_type=F32)
    res = res.astype(BF16)
    resid[...] = res
    res = res.astype(F32)
    square = jnp.mean(res * res, axis=1, keepdims=True)
    payload[:rows, :] = (res * lax.rsqrt(square + 1e-06) * gain[...]).astype(BF16)
    if meta is not None:
        copies = [
            jnp.broadcast_to(meta[i : i + 1, :], (META // 2, meta.shape[1])) for i in range(2)
        ]
        payload[rows:, :] = jnp.concatenate(copies, axis=0)


def edge(piece, info, q, halo, acc, tops, sums, x, w, gain, meta):
    rows, model = q.shape[0] // 2, q.shape[1]
    wide = halo.shape[0] // 2
    args = [info, q, halo, tops, sums, gain, acc, x, w]
    args += [] if meta is None else [meta]
    extra = 0 if meta is None else META
    flat = [
        jax.ShapeDtypeStruct((rows, model), BF16),
        jax.ShapeDtypeStruct((rows + extra, model), BF16),
    ]
    return pl.pallas_call(
        functools.partial(edge_kernel, piece),
        in_specs=[SMEM] + [VMEM] * (len(args) - 1),
        out_specs=[VMEM] * 2,
        out_shape=flat,
        scratch_shapes=[
            pltpu.VMEM((wide, 2 * rows), F32),
            pltpu.VMEM((model, rows), BF16),
        ],
        compiler_params=pltpu.CompilerParams(vmem_limit_bytes=12 * MIB),
        cost_estimate=cost(
            4 * rows * wide * model + 2 * rows * model * model, HEADS * rows * wide, args, flat
        ),
        name=f"edge_piece{piece}",
    )(*args)


def meta_items(payload, block, rows):
    meta = payload[payload.shape[0] - META :, :].astype(F32)
    meta = meta[block * META // 2 : (block + 1) * META // 2, :]
    return [meta[:, i * rows : (i + 1) * rows] for i in range(8)]


def slot_rows(hits):
    rows = hits.shape[1]
    upper = lax.broadcasted_iota(jnp.int32, (rows, rows), 0) < lax.broadcasted_iota(
        jnp.int32, (rows, rows), 1
    )
    upper = jnp.where(upper, F32(1.0), F32(0.0)).astype(BF16)
    rank = jnp.dot(hits.astype(BF16), upper, preferred_element_type=F32)
    return jnp.where(hits > 0, rank, F32(-1.0))


def experts_kernel(order, rows, capacity, me, *refs):
    payloads = refs[:-9]
    w_gate, w_up, w_down, out_mine, out_sib, scatter, x, hidden, tail = refs[-9:]
    width, model, step = w_gate.shape[1], w_down.shape[1], 256
    expert, other = me[0].astype(F32), me[1].astype(F32)
    groups = len(order) // 2
    items = [meta_items(payloads[holder], block, rows) for _, _, holder, block in order]

    def hits(item, wanted):
        return jnp.where((item[0] == wanted) | (item[1] == wanted), F32(1.0), F32(0.0))

    named = [hits(item, expert) for item in items] + [hits(item, other) for item in items[::2]]
    ranks = slot_rows(jnp.concatenate(named, axis=0))
    ranks = [ranks[i * META // 2 : i * META // 2 + 1, :] for i in range(len(named))]
    slot = lax.broadcasted_iota(jnp.int32, (2 * capacity, rows), 0).astype(F32)
    for g in range(groups):
        first, second = ranks[2 * g : 2 * g + 2]
        second = jnp.where(second >= 0, second + capacity, F32(-1.0))
        hot = jnp.concatenate([slot == first, slot == second], axis=1)
        hot = jnp.where(hot, F32(1.0), F32(0.0)).astype(BF16)
        tokens = [payloads[a][at : at + rows, :] for a, at, _, _ in order[2 * g : 2 * g + 2]]
        picked = jnp.dot(hot, jnp.concatenate(tokens, axis=0), preferred_element_type=F32)
        x[2 * g * capacity : (2 * g + 2) * capacity, :] = picked.astype(BF16)
    for g in range(groups):
        item = items[2 * g]
        for i, (wanted, rank) in enumerate(((expert, ranks[2 * g]), (other, ranks[2 * groups + g]))):
            gate = jnp.where(item[0] == wanted, item[2] + item[3] + item[4], F32(0.0))
            gate = gate + jnp.where(item[1] == wanted, item[5] + item[6] + item[7], F32(0.0))
            full = jnp.where(slot[:capacity] == rank, gate[:1, :], F32(0.0))
            high = full.astype(BF16)
            at = (4 * g + 2 * i) * capacity
            scatter[at : at + capacity, :] = high
            scatter[at + capacity : at + 2 * capacity, :] = (full - high.astype(F32)).astype(BF16)
    for at in range(0, width, step):
        wide = min(step, width - at)
        cols = slice(at, at + wide)
        if wide < step:
            tail[:, :wide] = w_gate[:, cols]
            tail[:, wide : 2 * wide] = w_up[:, cols]
            both = jnp.dot(x[...], tail[...], preferred_element_type=F32)
            g, u = both[:, :wide], both[:, wide:]
        else:
            g = jnp.dot(x[...], w_gate[:, cols], preferred_element_type=F32)
            u = jnp.dot(x[...], w_up[:, cols], preferred_element_type=F32)
        hidden[:, cols] = (g / (1.0 + jnp.exp(-g)) * u).astype(BF16)
    for at in range(0, model, step):
        cols = slice(at, at + step)
        o = jnp.dot(hidden[...], w_down[:, cols], preferred_element_type=F32).astype(BF16)
        for g in range(groups):
            span = slice(g * capacity, (g + 1) * capacity)
            out_mine[span, cols] = o[2 * g * capacity : (2 * g + 1) * capacity]
            out_sib[span, cols] = o[(2 * g + 1) * capacity : (2 * g + 2) * capacity]


def experts(me, payloads, order, weights, rows, capacity):
    model, width = weights[0].shape
    slots = len(order) * capacity
    left = width % 256
    outs = [jax.ShapeDtypeStruct((slots // 2, model), BF16)] * 2
    outs.append(jax.ShapeDtypeStruct((2 * slots, rows), BF16))
    args = [me, *payloads, *weights]
    return pl.pallas_call(
        functools.partial(experts_kernel, order, rows, capacity),
        in_specs=[SMEM] + [VMEM] * (len(args) - 1),
        out_specs=[VMEM] * 3,
        out_shape=outs,
        scratch_shapes=[
            pltpu.VMEM((slots, model), BF16),
            pltpu.VMEM((slots, width), BF16),
            pltpu.VMEM((model, max(2 * left, 256)), BF16),
        ],
        compiler_params=pltpu.CompilerParams(vmem_limit_bytes=12 * MIB),
        cost_estimate=cost(6 * slots * model * width, slots * width, args, outs),
        name=f"experts_{slots}",
    )(*args)


def combine_kernel(rows, capacity, parts, *refs):
    scatters, outs_me, outs_sib = refs[:parts], refs[parts : 2 * parts], refs[2 * parts : 3 * parts]
    refs = refs[3 * parts :]
    result = refs[-1]
    for block in range(2):
        part, at = (block, 0) if parts == 2 else (0, block)
        gates = scatters[part][4 * at * capacity : 4 * (at + 1) * capacity, :]
        span = slice(at * capacity, (at + 1) * capacity)
        mine, theirs = outs_me[part][span, :], outs_sib[part][span, :]
        values = jnp.concatenate([mine, mine, theirs, theirs], axis=0)
        total = lax.dot_general(gates, values, TN, preferred_element_type=F32)
        at = slice(block * rows, (block + 1) * rows)
        if len(refs) == 3:
            total = total + refs[block][...].astype(F32)
        result[at, :] = total.astype(result.dtype)


def combine(scatters, outs_me, outs_sib, rows, capacity, start=(), dtype=BF16):
    model = outs_me[0].shape[1]
    args = [*scatters, *outs_me, *outs_sib, *start]
    out = jax.ShapeDtypeStruct((2 * rows, model), dtype)
    return pl.pallas_call(
        functools.partial(combine_kernel, rows, capacity, len(outs_me)),
        in_specs=[VMEM] * len(args),
        out_specs=VMEM,
        out_shape=out,
        compiler_params=pltpu.CompilerParams(vmem_limit_bytes=12 * MIB),
        cost_estimate=cost(8 * out.size * capacity, 0, args, [out]),
        name="combine",
    )(*args)


def add_kernel(a, b, result):
    result[...] = (a[...].astype(F32) + b[...].astype(F32)).astype(result.dtype)


def place_kernel(turned, a, b, result):
    rows = a.shape[0] // 2
    first, second = [
        (a[at, :] + b[at, :].astype(F32)).astype(result.dtype)
        for at in (slice(0, rows), slice(rows, 2 * rows))
    ]
    straight = jnp.broadcast_to(turned[...], first.shape) == 0
    result[:rows, :] = jnp.where(straight, first, second)
    result[rows:, :] = jnp.where(straight, second, first)


def place(turned, a, b):
    out = jax.ShapeDtypeStruct(b.shape, b.dtype)
    return pl.pallas_call(
        place_kernel,
        in_specs=[VMEM] * 3,
        out_specs=VMEM,
        out_shape=out,
        compiler_params=pltpu.CompilerParams(vmem_limit_bytes=12 * MIB),
        cost_estimate=cost(out.size, 0, (a, b), [out]),
        name="place",
    )(turned, a, b)


def add(a, b, dtype):
    out = jax.ShapeDtypeStruct(a.shape, dtype)
    return pl.pallas_call(
        add_kernel,
        in_specs=[VMEM] * 2,
        out_specs=VMEM,
        out_shape=out,
        compiler_params=pltpu.CompilerParams(vmem_limit_bytes=12 * MIB),
        cost_estimate=cost(out.size, 0, (a, b), [out]),
        name="add",
    )(a, b)


def expert_rows(token_rows, gate_mat, up_mat, down_mat):
    gate_part = jnp.dot(token_rows, gate_mat, preferred_element_type=F32)
    up_part = jnp.dot(token_rows, up_mat, preferred_element_type=F32)
    hidden = (jax.nn.silu(gate_part) * up_part).astype(BF16)
    return jnp.dot(hidden, down_mat, preferred_element_type=F32).astype(BF16)


def slot_ranks(routes, experts_count, block_rows):
    row_count = routes.shape[0]
    expert_ids = jnp.arange(experts_count, dtype=jnp.int32)
    matches = routes[:, :, None] == expert_ids[None, None, :]
    hits = jnp.sum(matches.astype(jnp.int32), axis=1)
    hits = hits.reshape(row_count // block_rows, block_rows, experts_count)
    earlier = (jnp.cumsum(hits, axis=1) - hits).reshape(row_count, experts_count)
    return jnp.sum(jnp.where(matches, earlier[:, None, :], 0), axis=-1)


def routed_all_to_all(normed, resid, routes, route_gates, w_gate, w_up, w_down):
    tiles = lax.axis_size("tile")
    row_count, route_width = routes.shape
    block_rows, model = row_count // 2, normed.shape[1]
    capacity = row_count * route_width // tiles
    slot_rank = slot_ranks(routes, tiles, block_rows)
    pieces = []
    for index in range(2):
        rows = slice(index * block_rows, (index + 1) * block_rows)
        part_normed = normed[rows]
        positions = routes[rows] * capacity + slot_rank[rows]
        copies = jnp.broadcast_to(
            part_normed[:, None, :], (block_rows, route_width, model)
        ).reshape(-1, model)
        outgoing = jnp.zeros((tiles * capacity, model), BF16).at[positions.reshape(-1)].set(copies)
        outgoing = outgoing.reshape(tiles, capacity, model)
        received = lax.all_to_all(outgoing, "tile", split_axis=0, concat_axis=0, tiled=True)
        produced = expert_rows(received.reshape(-1, model), w_gate, w_up, w_down)
        produced = produced.reshape(received.shape)
        returned = lax.all_to_all(produced, "tile", split_axis=0, concat_axis=0, tiled=True)
        picked = returned.reshape(-1, model)[positions].astype(F32)
        combined = jnp.sum(route_gates[rows][:, :, None] * picked, axis=1)
        pieces.append((resid[rows].astype(F32) + combined).astype(BF16))
    return jnp.concatenate(pieces, axis=0)


def swap(array, bit):
    return lax.ppermute(array, "tile", [(i, i ^ bit) for i in range(8)])


def swap_by_core(array, bits):
    return lax.ppermute(array, "tile", [(i, i ^ bits[i % 2]) for i in range(8)])


def after(first, *later):
    return lax.optimization_barrier((first, *later))[1:]


def routed_gather(me, turned, payloads, resids, weights, rows, capacity):
    sizes = dict(rows=rows, capacity=capacity)

    def evaluate(mine, theirs):
        count = len(mine)
        order = []
        for block in range(2):
            array, at = (block, 0) if count == 2 else (0, block * rows)
            order += [(array, at, 0, block), (count + array, at, count, block)]
        kept, sent, scatter = experts(me, (*mine, *theirs), order, weights, **sizes)
        return (scatter,), (kept,), (swap(sent, 1),)

    def siblings(arrays):
        return [swap(a, 1) for a in arrays]

    first = [swap_by_core(p, (2, 4)) for p in payloads]
    sib = siblings(payloads)
    order = [(0, 0, 0, 0), (1, 0, 1, 0)]
    own0, sent0, scatter0 = experts(me, (payloads[0], sib[0]), order, weights, **sizes)
    (first[0],) = after(own0, first[0])
    diag0 = swap_by_core(first[0], (4, 2))
    later = after(first[0], payloads[1], sib[1])
    order = [(0, 0, 2, 1), (1, 0, 3, 1)]
    own1, sent1, scatter1 = experts(me, (*later, payloads[0], sib[0]), order, weights, **sizes)
    (first[1],) = after(own1, first[1])
    diag1 = swap_by_core(first[1], (4, 2))
    far = siblings(first)
    first[0], _ = lax.optimization_barrier((first[0], diag0))
    out_first = evaluate(first, far)
    second1 = swap_by_core(*after(diag0, payloads[1]), (4, 2))
    (diag1,) = after(out_first[1][0], diag1)
    second0 = swap_by_core(*after(diag1, payloads[0]), (4, 2))
    diag = [diag0, diag1]
    out_diag = evaluate(after(second1, *diag), siblings(diag))
    scatter, mine, theirs = out_diag
    sum_diag = combine(scatter, mine, after(second0, *theirs), **sizes)
    carry = swap_by_core(sum_diag, (4, 2))
    second = after(sum_diag, second0, second1)
    out_second = evaluate(second, siblings(second))
    scatter, mine, theirs = out_first
    theirs = after(out_second[1][0], *theirs)
    sum_first = combine(scatter, mine, theirs, dtype=F32, **sizes)
    scatter, mine, theirs = out_second
    sum_second = combine(scatter, mine, after(sum_first, *theirs), **sizes)
    back_second = swap_by_core(sum_second, (4, 2))
    sum_first = add(sum_first, *after(sum_second, carry), BF16)
    back_first = swap_by_core(sum_first, (2, 4))
    own = (scatter0, scatter1), (own0, own1), siblings((sent0, sent1))
    total = combine(*own, start=resids, dtype=F32, **sizes)
    return place(turned, add(total, back_second, F32), back_first)


def local(
    inputs,
    queries,
    key_vectors,
    values,
    out_weight,
    norm_gain,
    routes,
    route_gates,
    w_gate,
    w_up,
    w_down,
):
    row_count = inputs.shape[0]
    tiles = lax.axis_size("tile")
    tile = lax.axis_index("tile")
    width = R_IL * PLANE
    rows = row_count // 2
    capacity = row_count * routes.shape[1] // tiles
    pairs = [(i, i ^ 1) for i in range(tiles)]
    others = [(i, i + 1) for i in range(1, tiles - 1, 2)]
    others += [(j, i) for i, j in others]
    info = jnp.stack([1 - tile % 2, tile % 2, tile > 0, tile < tiles - 1]).astype(jnp.int32)
    me = jnp.stack([tile, tile ^ 1]).astype(jnp.int32)
    turned = jnp.full((1, inputs.shape[1]), 1 - tile % 2, F32)
    info, me, turned, key_vectors = lax.optimization_barrier((info, me, turned, key_vectors))
    near, other = pack(info, key_vectors, values)
    halos = lax.ppermute(near, "tile", pairs), lax.ppermute(other, "tile", others)
    fast = tiles == 8
    meta = None
    if fast:
        items = [routes[:, 0].astype(F32), routes[:, 1].astype(F32)]
        for k in range(2):
            gate = route_gates[:, k]
            high = lax.reduce_precision(gate, 8, 7)
            mid = lax.reduce_precision(gate - high, 8, 7)
            items += [high, mid, gate - high - mid]
        meta = jnp.stack(items).reshape(len(items), 2, rows).swapaxes(0, 1)
        meta = meta.reshape(2, len(items) * rows)
        other = jnp.concatenate([meta[1:], meta[:1]], axis=0)
        meta = jnp.where(turned == 0, meta, other).astype(BF16)
    acc, tops, sums = interior(queries, key_vectors, values)
    pieces = [
        edge(
            piece, info, queries, halo, acc, tops, sums, inputs, out_weight,
            norm_gain[None, :], meta if piece == 0 else None,
        )
        for piece, halo in enumerate(halos)
    ]
    resids, payloads = zip(*pieces)
    if fast:
        weights = (w_gate[0], w_up[0], w_down[0])
        return routed_gather(me, turned, payloads, resids, weights, rows, capacity)
    payload, resid = [
        jnp.where(info[0] == 0, jnp.concatenate(a, axis=0), jnp.concatenate(a[::-1], axis=0))
        for a in (payloads, resids)
    ]
    return routed_all_to_all(payload, resid, routes, route_gates, w_gate[0], w_up[0], w_down[0])


def solution(mesh):
    return jax.shard_map(
        local,
        mesh=mesh,
        in_specs=(
            P(("rep", "tile"), None),
            P(("rep", "tile"), None),
            P(("rep", "tile"), None),
            P(("rep", "tile"), None),
            P(),
            P(),
            P(("rep", "tile"), None),
            P(("rep", "tile"), None),
            P("tile", None, None),
            P("tile", None, None),
            P("tile", None, None),
        ),
        out_specs=P(("rep", "tile"), None),
        check_vma=False,
    )
```
